32 devices in a mesh: sec: 2 (over core), tile: 16 (over z, y, x).
Axes of the slice: x: 2, y: 2, z: 4, core: 2. Of those that a mesh axis runs over, the one named last changes fastest.
Arguments:
- velocity: float32 [3, 64, 128, 128], P(None, 'tile', 'sec'), may hold values from -6 to 6
- stresses: float32 [6, 64, 128, 128], P(None, 'tile', 'sec'), may hold values from -6 to 6
- buoyancy: float32 [64, 128, 128], P('tile', 'sec'), may hold values from 0.5 to 1.5
- lame_first: float32 [64, 128, 128], P('tile', 'sec'), may hold values from 0.5 to 1.5
- shear_mod: float32 [64, 128, 128], P('tile', 'sec'), may hold values from 0.3 to 1
- ocean_state: float32 [3, 1024, 512], P(None, 'tile', 'sec'), may hold values from -6 to 6
- depth_map: float32 [1024, 512], P('tile', 'sec'), may hold values from 0.5 to 2
- wet_mask: int32 [1024, 512], P('tile', 'sec'), may hold values 0 or 1
- intersection_src: int32 [1024], P('tile'), may hold values from 0 to 15, as said below
- intersection_share: float32 [1024], P('tile'), may hold values from 0.3 to 1
Outputs:
- velocity_out: float32 [3, 64, 128, 128], P(None, 'tile', 'sec')
- stress_out: float32 [6, 64, 128, 128], P(None, 'tile', 'sec')
- ocean_out: float32 [3, 1024, 512], P(None, 'tile', 'sec')
The draws below stay inside these ranges and needn't reach their ends.
Inputs may be any that keep to these rules, and one draw needn't show every extreme that they name: intersection_src[r] differs from r // 64 by at most 2.
All inputs are finite; a program needn't handle non-finite values. No bound on the sum of `wet_mask` on one device may be relied on, other than what follows from the above.
Results may differ from the reference program's by a relative error of at most 0.000096.
Values sent between devices are 32-bit elements; how exact they have to be, the bound alone decides.
No kernel may reach another device: no remote copies, remote signals or barrier semaphores. Data moves between devices by JAX's collectives and lax.ppermute only.
A program may use at most 64 MiB of HBM per device.

```python
import math
import jax
import jax.numpy as jnp

CX = 4
CY = 64
NZ = 128
OCX = 64
STEPS = 2
OSTEPS = 2
REACH = 2
NX = 64
NY = 128
OX = 1024
OY = 512
N_SEC = 2
N_TILE = 16


def draw_intersection_src(key, part):
    tiles = jnp.arange(OX, dtype=jnp.int32) // OCX
    offsets = jax.random.randint(key, (OX,), -REACH, REACH + 1, dtype=jnp.int32)
    return jnp.clip(tiles + offsets, 0, OX // OCX - 1).astype(jnp.int32)


def touch_ends(entries, key, smallest, largest):
    place = [jax.random.randint(jax.random.fold_in(key, axis), (), 0, length) for axis, length in enumerate(entries.shape)]
    widest = entries.shape.index(max(entries.shape))
    beside = place[:widest] + [(place[widest] + 1) % entries.shape[widest]] + place[widest + 1:]
    return entries.at[tuple(place)].set(smallest).at[tuple(beside)].set(largest)


def level_of(stream_key, dims, cuts, low, top_value):
    def one(dim, blocks):
        steps = jax.random.uniform(jax.random.fold_in(jax.random.fold_in(stream_key, 6), dim), (blocks,), jnp.float32, low / len(cuts), top_value / len(cuts))
        return jnp.repeat(jnp.exp(steps), dims[dim] // blocks).reshape((-1,) + (1,) * (len(dims) - dim - 1))

    gain = one(*cuts[0])
    for cut in cuts[1:]:
        gain = gain * one(*cut)
    return gain


def noise(own_key, shape, width, bound, pieces=(), kind=jnp.bfloat16):
    loudness = level_of(own_key, shape, pieces, -0.22, 0.18) if pieces else 1.0
    values = jax.random.normal(own_key, shape, jnp.float32) * width * loudness
    return jnp.minimum(jnp.maximum(values, -bound), bound).astype(kind)


def setup_inputs(seed: int = 0) -> dict:
    key_list = jax.random.split(jax.random.key(seed), 11)
    return {
        "velocity": noise(key_list[0], (3, NX, NY, NZ), 1.0, 6.0, ((1, 16), (2, 2)), jnp.float32),
        "stresses": noise(key_list[1], (6, NX, NY, NZ), 1.0, 6.0, ((1, 16), (2, 2)), jnp.float32),
        "buoyancy": jnp.clip(0.5 + 1.0 * jax.random.uniform(key_list[2], (NX, NY, NZ), jnp.float32) ** level_of(key_list[2], (NX, NY, NZ), ((0, 16), (1, 2)), -0.2, 0.2), 0.5, 1.5),
        "lame_first": jnp.clip(0.5 + 1.0 * jax.random.uniform(key_list[3], (NX, NY, NZ), jnp.float32) ** level_of(key_list[3], (NX, NY, NZ), ((0, 16), (1, 2)), -0.2, 0.2), 0.5, 1.5),
        "shear_mod": jnp.clip(0.3 + 0.7 * jax.random.uniform(key_list[4], (NX, NY, NZ), jnp.float32) ** level_of(key_list[4], (NX, NY, NZ), ((0, 16), (1, 2)), -0.2, 0.2), 0.3, 1.0),
        "ocean_state": noise(key_list[5], (3, OX, OY), 1.0, 6.0, ((1, 16), (2, 2)), jnp.float32),
        "depth_map": jnp.clip(jnp.exp(math.log(2.0) - 1.3862944 * jax.random.uniform(key_list[6], (OX, OY), jnp.float32) ** level_of(key_list[6], (OX, OY), ((0, 16), (1, 2)), -0.2, 0.2)), 0.5, 2.0),
        "wet_mask": touch_ends((jax.random.randint(key_list[7], (OX, OY), 0, 8) < 7).astype(jnp.int32), jax.random.fold_in(key_list[7], 1), 0, 1),
        "intersection_src": draw_intersection_src(jax.random.fold_in(key_list[10], 71), 0),
        "intersection_share": jnp.clip(0.3 + 0.7 * jax.random.uniform(key_list[9], (OX,), jnp.float32) ** level_of(key_list[9], (OX,), ((0, 16),), -0.2, 0.2), 0.3, 1.0),
    }


NEAR_COEF = 9.0 / 8.0
FAR_COEF = -1.0 / 24.0
TIME_STEP = 0.15
OCEAN_STEP = 0.3


def offset_slice(field, shift, dimension):
    window = []
    for current in range(3):
        displaced = shift if current == dimension else 0
        window.append(slice(2 + displaced, field.shape[current] - 2 + displaced))
    return field[tuple(window)]


def forward_diff(field, dimension):
    return NEAR_COEF * (offset_slice(field, 1, dimension) - offset_slice(field, 0, dimension)) + FAR_COEF * (offset_slice(field, 2, dimension) - offset_slice(field, -1, dimension))


def backward_diff(field, dimension):
    return NEAR_COEF * (offset_slice(field, 0, dimension) - offset_slice(field, -1, dimension)) + FAR_COEF * (offset_slice(field, 1, dimension) - offset_slice(field, -2, dimension))


def update_velocity(velocity, stress_pad, buoyancy):
    accel_x = forward_diff(stress_pad[0], 0) + backward_diff(stress_pad[3], 1) + backward_diff(stress_pad[4], 2)
    accel_y = backward_diff(stress_pad[3], 0) + forward_diff(stress_pad[1], 1) + backward_diff(stress_pad[5], 2)
    accel_z = backward_diff(stress_pad[4], 0) + backward_diff(stress_pad[5], 1) + forward_diff(stress_pad[2], 2)
    return velocity + TIME_STEP * buoyancy * jnp.stack([accel_x, accel_y, accel_z])


def update_stress(stresses, velocity_pad, lame_first, shear_mod):
    strain_x = backward_diff(velocity_pad[0], 0)
    strain_y = backward_diff(velocity_pad[1], 1)
    strain_z = backward_diff(velocity_pad[2], 2)
    volume = strain_x + strain_y + strain_z
    normal_x = stresses[0] + TIME_STEP * (lame_first * volume + 2.0 * shear_mod * strain_x)
    normal_y = stresses[1] + TIME_STEP * (lame_first * volume + 2.0 * shear_mod * strain_y)
    normal_z = stresses[2] + TIME_STEP * (lame_first * volume + 2.0 * shear_mod * strain_z)
    shear_xy = stresses[3] + TIME_STEP * shear_mod * (forward_diff(velocity_pad[0], 1) + forward_diff(velocity_pad[1], 0))
    shear_xz = stresses[4] + TIME_STEP * shear_mod * (forward_diff(velocity_pad[0], 2) + forward_diff(velocity_pad[2], 0))
    shear_yz = stresses[5] + TIME_STEP * shear_mod * (forward_diff(velocity_pad[1], 2) + forward_diff(velocity_pad[2], 1))
    return jnp.stack([normal_x, normal_y, normal_z, shear_xy, shear_xz, shear_yz])


def pad_all(stacked):
    return jnp.pad(stacked, ((0, 0), (2, 2), (2, 2), (2, 2)))


def ocean_step(ocean_state, depth_map, wet_float, source):
    surface = ocean_state[0]
    padded = jnp.pad(surface, 1)
    grad_x = (padded[2:, 1:-1] - padded[:-2, 1:-1]) * 0.5
    grad_y = (padded[1:-1, 2:] - padded[1:-1, :-2]) * 0.5
    flow_x = wet_float * (ocean_state[1] - OCEAN_STEP * grad_x)
    flow_y = wet_float * (ocean_state[2] - OCEAN_STEP * grad_y)
    flux_pad = jnp.pad(jnp.stack([depth_map * flow_x, depth_map * flow_y]), ((0, 0), (1, 1), (1, 1)))
    spread = (flux_pad[0, 2:, 1:-1] - flux_pad[0, :-2, 1:-1]) * 0.5 + (flux_pad[1, 1:-1, 2:] - flux_pad[1, 1:-1, :-2]) * 0.5
    surface = surface - OCEAN_STEP * spread + OCEAN_STEP * source
    return jnp.stack([surface, flow_x, flow_y])


def reference(velocity, stresses, buoyancy, lame_first, shear_mod, ocean_state, depth_map, wet_mask, intersection_src, intersection_share):
    velocity_out = velocity
    stress_out = stresses
    for step_index in range(STEPS):
        velocity_out = update_velocity(velocity_out, pad_all(stress_out), buoyancy)
        stress_out = update_stress(stress_out, pad_all(velocity_out), lame_first, shear_mod)
    seafloor = velocity_out[2, :, :, 0].reshape(N_TILE, CX, N_SEC, CY).transpose(0, 2, 1, 3).reshape(N_TILE, N_SEC, CX * CY)
    uplift = seafloor[intersection_src.astype(jnp.int32)].reshape(OX, OY)
    wet_float = wet_mask.astype(jnp.float32)
    source = intersection_share[:, None] * wet_float * uplift
    ocean_out = ocean_state
    for step_index in range(OSTEPS):
        ocean_out = ocean_step(ocean_out, depth_map, wet_float, source)
    return (velocity_out, stress_out, ocean_out)
```

```python
import functools

import jax
import jax.numpy as jnp
from jax import lax
from jax.experimental import pallas as pl
from jax.experimental.pallas import tpu as pltpu
from jax.sharding import PartitionSpec as P

STEPS = 2
REACH = 2
NEAR = 9.0 / 8.0
FAR = 1.0 / 24.0
DT = 0.15
ODT = 0.3
F32 = jnp.float32
EDGE = 5
SIDE = 8
WINDOW = 8


def depth_weights(width):
    lane = lax.broadcasted_iota(jnp.int32, (1, width), 1)

    def weight(value, first, last):
        return jnp.where((lane >= first) & (lane < last), value, 0.0).astype(F32)

    forward = (weight(NEAR, 0, width - 1), weight(-FAR, 0, width - 2), weight(FAR, 1, width))
    backward = (weight(-NEAR, 1, width), weight(-FAR, 0, width - 1), weight(FAR, 2, width))
    return forward, backward


def forward_z(f, weights):
    near, far, behind = weights
    n = f.shape[-1]
    return (
        pltpu.roll(f, n - 1, 1) * near
        - NEAR * f
        + pltpu.roll(f, n - 2, 1) * far
        + pltpu.roll(f, 1, 1) * behind
    )


def backward_z(f, weights):
    near, far, behind = weights
    n = f.shape[-1]
    return (
        NEAR * f
        + pltpu.roll(f, 1, 1) * near
        + pltpu.roll(f, n - 1, 1) * far
        + pltpu.roll(f, 2, 1) * behind
    )


def forward(at, i):
    return NEAR * (at(i + 1) - at(i)) - FAR * (at(i + 2) - at(i - 1))


def backward(at, i):
    return NEAR * (at(i) - at(i - 1)) - FAR * (at(i + 1) - at(i - 2))


def sides(odd, from_b, from_a, rows):
    def low(k):
        part = slice(k * rows, (k + 1) * rows)
        return jnp.where(odd, from_a[part, :], from_b[part, :])

    def high(k):
        part = slice(k * rows, (k + 1) * rows)
        return jnp.where(odd, from_b[part, :], from_a[part, :])

    return low, high


def along(own, count, low, low_from, high, high_from):
    def at(x):
        if x < 0:
            return low(low_from[x])
        if x >= count:
            return high(high_from[x])
        return own(x)

    return at


def fill_rows(rows_ref, comps, own, side_ref, sec, cx, cy):
    low_on = (sec == 1).astype(F32)
    high_on = (sec == 0).astype(F32)
    for k, comp in enumerate(comps):
        for x in range(cx):
            rows_ref[k, x, SIDE : SIDE + cy, :] = own(comp, x)
            got = side_ref[(k * cx + x) * SIDE : (k * cx + x + 1) * SIDE, :]
            rows_ref[k, x, 0:SIDE, :] = got * low_on
            rows_ref[k, x, SIDE + cy : SIDE + cy + SIDE, :] = got * high_on


def rows_at(rows_ref, k, x, cy):
    return lambda shift: rows_ref[k, x, SIDE + shift : SIDE + shift + cy, :]


def send_sides(odd, up, down, pay_b, pay_a, rows, get):
    for k, (u, d) in enumerate(zip(up, down)):
        part = slice(k * rows, (k + 1) * rows)
        upper, lower = get(*u), get(*d)
        pay_b[part, :] = jnp.where(odd, upper, lower)
        pay_a[part, :] = jnp.where(odd, lower, upper)


def send_rows(sec, comps, pay_s, get_rows, cx, cy):
    for k, comp in enumerate(comps):
        for x in range(cx):
            part = slice((k * cx + x) * SIDE, (k * cx + x + 1) * SIDE)
            pay_s[part, :] = jnp.where(
                sec == 0, get_rows(comp, x, cy - SIDE), get_rows(comp, x, 0)
            )


STRESS_ROWS = (1, 3, 5)
VELOCITY_ROWS = (0, 1, 2)


def stress_up(cx):
    return [(0, cx - 1), (3, cx - 2), (3, cx - 1), (4, cx - 2), (4, cx - 1)]


def stress_down(cx):
    return [(0, 0), (0, 1), (3, 0), (4, 0), (4, 0)]


def velocity_up(cx):
    return [(0, cx - 2), (0, cx - 1), (1, cx - 1), (2, cx - 1), (2, cx - 1)]


def velocity_down(cx):
    return [(0, 0), (1, 0), (1, 1), (2, 0), (2, 1)]


def step_velocity(info, s, v, b, from_b, from_a, from_s, v_out, pay_b, pay_a, pay_s, rows_ref):
    odd, sec = info[0] == 1, info[1]
    _, cx, cy, nz = s.shape
    fw, bw = depth_weights(nz)
    low, high = sides(odd, from_b, from_a, cy)
    fill_rows(rows_ref, STRESS_ROWS, lambda c, x: s[c, x], from_s, sec, cx, cy)
    xx = along(lambda x: s[0, x], cx, low, {-1: 0}, high, {cx: 0, cx + 1: 1})
    xy = along(lambda x: s[3, x], cx, low, {-2: 1, -1: 2}, high, {cx: 2})
    xz = along(lambda x: s[4, x], cx, low, {-2: 3, -1: 4}, high, {cx: 3})
    for x in range(cx):
        scale = DT * b[x]
        yy = rows_at(rows_ref, 0, x, cy)
        xy_rows = rows_at(rows_ref, 1, x, cy)
        yz = rows_at(rows_ref, 2, x, cy)
        v_out[0, x] = v[0, x] + scale * (
            forward(xx, x) + backward(xy_rows, 0) + backward_z(s[4, x], bw)
        )
        v_out[1, x] = v[1, x] + scale * (
            backward(xy, x) + forward(yy, 0) + backward_z(s[5, x], bw)
        )
        v_out[2, x] = v[2, x] + scale * (
            backward(xz, x) + backward(yz, 0) + forward_z(s[2, x], fw)
        )
    send_sides(odd, velocity_up(cx), velocity_down(cx), pay_b, pay_a, cy, lambda c, x: v_out[c, x])
    send_rows(sec, VELOCITY_ROWS, pay_s, lambda c, x, y: v_out[c, x, y : y + SIDE, :], cx, cy)


def last_velocity(
    info, s, v, b, from_b, from_a, from_s, ocean, marks, v_out, pay_b, pay_a, pay_s, patch, rows_ref
):
    step_velocity(info, s, v, b, from_b, from_a, from_s, v_out, pay_b, pay_a, pay_s, rows_ref)
    odd = info[0] == 1
    _, cx, cy, nz = s.shape
    first = (lax.broadcasted_iota(jnp.int32, (8, nz), 1) == 0).astype(F32)
    floor = jnp.concatenate([v_out[2, x] for x in range(cx)], axis=0)
    line = lax.dot_general(
        first,
        floor,
        (((1,), (1,)), ((), ())),
        precision=lax.Precision.HIGHEST,
        preferred_element_type=F32,
    )
    patch[...] = line[0:1, :]
    fields, rows, columns = ocean.shape
    base = EDGE * cy
    tiles = columns // 128
    for f in range(fields + 1):
        for k in range(tiles if f < fields else 1):
            part = slice(base, base + SIDE)
            if f < fields:
                upper = ocean[f, rows - SIDE : rows, k * 128 : (k + 1) * 128]
                lower = ocean[f, 0:SIDE, k * 128 : (k + 1) * 128]
            else:
                upper, lower = marks[rows - SIDE : rows, :], marks[0:SIDE, :]
            pay_b[part, :] = jnp.where(odd, upper, lower)
            pay_a[part, :] = jnp.where(odd, lower, upper)
            base += SIDE


def update_stress(info, v, s, lam, mu, from_b, from_a, from_s, s_out, rows_ref):
    odd, sec = info[0] == 1, info[1]
    _, cx, cy, nz = s.shape
    fw, bw = depth_weights(nz)
    low, high = sides(odd, from_b, from_a, cy)
    fill_rows(rows_ref, VELOCITY_ROWS, lambda c, x: v[c, x], from_s, sec, cx, cy)
    vx = along(lambda x: v[0, x], cx, low, {-2: 0, -1: 1}, high, {cx: 0})
    vy = along(lambda x: v[1, x], cx, low, {-1: 2}, high, {cx: 1, cx + 1: 2})
    vz = along(lambda x: v[2, x], cx, low, {-1: 3}, high, {cx: 3, cx + 1: 4})
    for x in range(cx):
        shear = DT * mu[x]
        double = 2.0 * shear
        vx_rows, vy_rows, vz_rows = (rows_at(rows_ref, k, x, cy) for k in range(3))
        exx = backward(vx, x)
        eyy = backward(vy_rows, 0)
        ezz = backward_z(v[2, x], bw)
        volume = (DT * lam[x]) * (exx + eyy + ezz)
        s_out[0, x] = s[0, x] + (volume + double * exx)
        s_out[1, x] = s[1, x] + (volume + double * eyy)
        s_out[2, x] = s[2, x] + (volume + double * ezz)
        s_out[3, x] = s[3, x] + shear * (forward(vx_rows, 0) + forward(vy, x))
        s_out[4, x] = s[4, x] + shear * (forward_z(v[0, x], fw) + forward(vz, x))
        s_out[5, x] = s[5, x] + shear * (forward_z(v[1, x], fw) + forward(vz_rows, 0))


def step_stress(
    info, v, s, lam, mu, from_b, from_a, from_s, s_out, pay_b, pay_a, pay_s, rows_ref
):
    odd, sec = info[0] == 1, info[1]
    _, cx, cy, nz = s.shape
    update_stress(info, v, s, lam, mu, from_b, from_a, from_s, s_out, rows_ref)
    send_sides(odd, stress_up(cx), stress_down(cx), pay_b, pay_a, cy, lambda c, x: s_out[c, x])
    send_rows(sec, STRESS_ROWS, pay_s, lambda c, x, y: s_out[c, x, y : y + SIDE, :], cx, cy)


def last_stress(
    info,
    v,
    s,
    lam,
    mu,
    from_b,
    from_a,
    from_s,
    ocean,
    marks,
    patches,
    s_out,
    ocean_out,
    rows_ref,
    ocean_ref,
    marks_ref,
):
    odd, sec, tile, count, base = info[0] == 1, info[1], info[2], info[3], info[4]
    _, cx, cy, nz = s.shape
    update_stress(info, v, s, lam, mu, from_b, from_a, from_s, s_out, rows_ref)

    fields, rows, columns = ocean.shape
    own = ocean_out.shape[2]
    at = EDGE * cy
    top, bottom = slice(0, SIDE), slice(SIDE + rows, SIDE + rows + SIDE)
    for f in range(fields):
        ocean_ref[f, SIDE : SIDE + rows, :] = ocean[f]
        for k in range(columns // 128):
            lanes = slice(k * 128, (k + 1) * 128)
            b, a = from_b[at : at + SIDE, :], from_a[at : at + SIDE, :]
            ocean_ref[f, top, lanes] = jnp.where(odd, a, b)
            ocean_ref[f, bottom, lanes] = jnp.where(odd, b, a)
            at += SIDE
    b, a = from_b[at : at + SIDE, :], from_a[at : at + SIDE, :]
    marks_ref[SIDE : SIDE + rows, :] = marks[...]
    marks_ref[top, :] = jnp.where(odd, a, b)
    marks_ref[bottom, :] = jnp.where(odd, b, a)

    total = rows + 2 * SIDE
    lane = lax.broadcasted_iota(jnp.int32, (1, columns), 1)
    ahead = jnp.where((lane == own - 1) & (sec == 1), 0.0, 0.5).astype(F32)
    behind = jnp.where((lane == 0) & (sec == 0), 0.0, 0.5).astype(F32)
    line = lax.broadcasted_iota(jnp.int32, (total, 1), 0)
    inside = ((line >= SIDE) | (tile > 0)) & ((line < SIDE + rows) | (tile < count - 1))
    inside = inside.astype(F32)

    def across(f):
        return pltpu.roll(f, columns - 1, 1) * ahead - pltpu.roll(f, 1, 1) * behind

    def down(f):
        return 0.5 * (pltpu.roll(f, total - 1, 0) - pltpu.roll(f, 1, 0))

    eta, u, v_sea = ocean_ref[0], ocean_ref[1], ocean_ref[2]
    depth, wet = ocean_ref[3], ocean_ref[4]
    owner = marks_ref[:, 0:1] - base.astype(F32)
    share = marks_ref[:, 1:2]
    uplift = jnp.zeros((total, columns), F32)
    for k in range(patches.shape[0]):
        uplift = jnp.where(owner == float(k), patches[k : k + 1, :], uplift)
    lift = ODT * (share * wet * uplift)
    for _ in range(2):
        u = wet * (u - ODT * down(eta))
        v_sea = wet * (v_sea - ODT * across(eta))
        eta = inside * (eta - ODT * (down(depth * u) + across(depth * v_sea)) + lift)
    part = slice(SIDE, SIDE + rows)
    ocean_out[0] = eta[part, :own]
    ocean_out[1] = u[part, :own]
    ocean_out[2] = v_sea[part, :own]


def call(body, name, outs, scratch, operands, flops):
    shapes = [jax.ShapeDtypeStruct(o, F32) for o in outs]
    smem = pl.BlockSpec(memory_space=pltpu.SMEM)
    vmem = pl.BlockSpec(memory_space=pltpu.VMEM)
    moved = sum(o.size for o in operands) * 4 + sum(o.size for o in shapes) * 4
    return pl.pallas_call(
        body,
        name=name,
        out_shape=shapes,
        in_specs=[smem] + [vmem] * (len(operands) - 1),
        out_specs=[vmem] * len(outs),
        scratch_shapes=[pltpu.VMEM(shape, F32) for shape in scratch],
        compiler_params=pltpu.CompilerParams(vmem_limit_bytes=32 * 1024 * 1024),
        cost_estimate=pl.CostEstimate(flops=flops, bytes_accessed=moved, transcendentals=0),
    )(*operands)


def exchange(pay_b, pay_a, count):
    def swap(pay, first):
        pairs = []
        for i in range(first, count - 1, 2):
            pairs += [(i, i + 1), (i + 1, i)]
        return lax.ppermute(pay, "tile", pairs)

    return swap(pay_b, 1), swap(pay_a, 0)


def across(pay):
    return lax.ppermute(pay, "sec", [(0, 1), (1, 0)])


def shards(
    velocity,
    stresses,
    buoyancy,
    lame_first,
    shear_mod,
    ocean_state,
    depth_map,
    wet_mask,
    intersection_src,
    intersection_share,
):
    count = lax.axis_size("tile")
    tile, sec = lax.axis_index("tile"), lax.axis_index("sec")
    odd = lax.rem(tile, 2)
    _, cx, cy, nz = stresses.shape
    _, rows, columns = ocean_state.shape
    base = jnp.clip(tile - REACH - 1, 0, max(count - WINDOW, 0))
    info = jnp.stack([odd, sec, tile, jnp.int32(count), base]).astype(jnp.int32)

    up = jnp.concatenate([stresses[c, x] for c, x in stress_up(cx)])
    down = jnp.concatenate([stresses[c, x] for c, x in stress_down(cx)])
    pay_b, pay_a = jnp.where(odd == 1, up, down), jnp.where(odd == 1, down, up)
    from_b, from_a = exchange(pay_b, pay_a, count)

    edge = jnp.stack([stresses[c] for c in STRESS_ROWS])
    edge = jnp.where(sec == 0, edge[:, :, cy - SIDE :, :], edge[:, :, :SIDE, :])
    fields = jnp.concatenate([ocean_state, depth_map[None], wet_mask.astype(F32)[None]])
    near = jnp.where(sec == 0, fields[:, :, columns - 128 :], fields[:, :, :128])
    got = across(jnp.concatenate([edge.reshape(-1, nz), near.reshape(-1, 128)]))
    from_s = got[: 3 * cx * SIDE]
    ocean = jnp.concatenate([fields, got[3 * cx * SIDE :].reshape(-1, rows, 128)], axis=2)
    lane = lax.broadcasted_iota(jnp.int32, (rows, 128), 1)
    marks = jnp.where(
        lane == 0,
        intersection_src.astype(F32)[:, None],
        jnp.where(lane == 1, intersection_share[:, None], 0.0),
    )

    cells = cx * cy * nz
    side = (EDGE * cy, nz)
    strip = (3 * cx * SIDE, nz)
    halo_rows = (3, cx, cy + 2 * SIDE, nz)
    tiles = (ocean.shape[0] * ocean.shape[2] // 128 + 1) * SIDE
    long_side = (EDGE * cy + tiles, nz)
    velocity, pay_b, pay_a, pay_s = call(
        step_velocity,
        "velocity_step",
        [velocity.shape, side, side, strip],
        [halo_rows],
        [info, stresses, velocity, buoyancy, from_b, from_a, from_s],
        60 * cells,
    )
    from_b, from_a = exchange(pay_b, pay_a, count)
    from_s = across(pay_s)
    stresses, pay_b, pay_a, pay_s = call(
        step_stress,
        "stress_step",
        [stresses.shape, side, side, strip],
        [halo_rows],
        [info, velocity, stresses, lame_first, shear_mod, from_b, from_a, from_s],
        70 * cells,
    )
    from_b, from_a = exchange(pay_b, pay_a, count)
    from_s = across(pay_s)
    velocity, pay_b, pay_a, pay_s, patch = call(
        last_velocity,
        "velocity_last",
        [velocity.shape, long_side, long_side, strip, (1, cx * cy)],
        [halo_rows],
        [info, stresses, velocity, buoyancy, from_b, from_a, from_s, ocean, marks],
        60 * cells,
    )
    from_b, from_a = exchange(pay_b, pay_a, count)
    from_s = across(pay_s)
    spread = jnp.broadcast_to(patch.reshape(1, -1, 128), (2 * count, cx * cy // 128, 128))
    patches = lax.all_to_all(spread, ("sec", "tile"), 0, 0).reshape(2, count, cx * cy)
    window = min(WINDOW, count)
    mine = lax.dynamic_slice(patches, (sec, base, 0), (1, window, cx * cy))[0]
    theirs = lax.dynamic_slice(
        patches, (1 - sec, base, sec * (cx * cy - 128)), (1, window, 128)
    )[0]
    patches = jnp.concatenate([mine, theirs], axis=1)
    stresses, ocean_state = call(
        last_stress,
        "stress_last",
        [stresses.shape, ocean_state.shape],
        [
            halo_rows,
            (ocean.shape[0], rows + 2 * SIDE, ocean.shape[2]),
            (rows + 2 * SIDE, 128),
        ],
        [info, velocity, stresses, lame_first, shear_mod, from_b, from_a, from_s, ocean, marks]
        + [patches],
        80 * cells,
    )
    return velocity, stresses, ocean_state


def solution(mesh):
    cube = P("tile", "sec", None)
    return jax.shard_map(
        shards,
        mesh=mesh,
        in_specs=(
            P(None, "tile", "sec", None),
            P(None, "tile", "sec", None),
            cube,
            cube,
            cube,
            P(None, "tile", "sec"),
            P("tile", "sec"),
            P("tile", "sec"),
            P("tile"),
            P("tile"),
        ),
        out_specs=(
            P(None, "tile", "sec", None),
            P(None, "tile", "sec", None),
            P(None, "tile", "sec"),
        ),
        check_vma=False,
    )
```

```python
import functools

import jax
import jax.numpy as jnp
from jax import lax
from jax.experimental import pallas as pl
from jax.experimental.pallas import tpu as pltpu
from jax.sharding import PartitionSpec as P

STEPS = 2
REACH = 2
NEAR = 9.0 / 8.0
FAR = 1.0 / 24.0
DT = 0.15
ODT = 0.3
F32 = jnp.float32
EDGE = 5
SIDE = 8
WINDOW = 8
DEEP = (4, 3, 3, 3, 3)
PACK = sum(DEEP)


def depth_weights(width):
    lane = lax.broadcasted_iota(jnp.int32, (1, width), 1)

    def weight(value, first, last):
        return jnp.where((lane >= first) & (lane < last), value, 0.0).astype(F32)

    forward = (weight(NEAR, 0, width - 1), weight(-FAR, 0, width - 2), weight(FAR, 1, width))
    backward = (weight(-NEAR, 1, width), weight(-FAR, 0, width - 1), weight(FAR, 2, width))
    return forward, backward


def forward_z(f, weights):
    near, far, behind = weights
    n = f.shape[-1]
    return (
        pltpu.roll(f, n - 1, 1) * near
        - NEAR * f
        + pltpu.roll(f, n - 2, 1) * far
        + pltpu.roll(f, 1, 1) * behind
    )


def backward_z(f, weights):
    near, far, behind = weights
    n = f.shape[-1]
    return (
        NEAR * f
        + pltpu.roll(f, 1, 1) * near
        + pltpu.roll(f, n - 1, 1) * far
        + pltpu.roll(f, 2, 1) * behind
    )


def forward(at, i):
    return NEAR * (at(i + 1) - at(i)) - FAR * (at(i + 2) - at(i - 1))


def backward(at, i):
    return NEAR * (at(i) - at(i - 1)) - FAR * (at(i + 1) - at(i - 2))


def place():
    tile, sec = lax.axis_index("tile"), lax.axis_index("sec")
    return lax.rem(tile, 2) == 1, sec, tile


def sides(odd, from_b, from_a, rows):
    def low(k):
        part = slice(k * rows, (k + 1) * rows)
        return jnp.where(odd, from_a[part, :], from_b[part, :])

    def high(k):
        part = slice(k * rows, (k + 1) * rows)
        return jnp.where(odd, from_b[part, :], from_a[part, :])

    return low, high


def along(own, count, low, low_from, high, high_from):
    def at(x):
        if x < 0:
            return low(low_from[x])
        if x >= count:
            return high(high_from[x])
        return own(x)

    return at


def fill_rows(rows_ref, comps, own, side_ref, sec, cx, cy):
    low_on = (sec == 1).astype(F32)
    high_on = (sec == 0).astype(F32)
    for k, comp in enumerate(comps):
        for x in range(cx):
            rows_ref[k, x, SIDE : SIDE + cy, :] = own(comp, x)
            got = side_ref[(k * cx + x) * SIDE : (k * cx + x + 1) * SIDE, :]
            rows_ref[k, x, 0:SIDE, :] = got * low_on
            rows_ref[k, x, SIDE + cy : SIDE + cy + SIDE, :] = got * high_on


def rows_at(rows_ref, k, x, cy):
    return lambda shift: rows_ref[k, x, SIDE + shift : SIDE + shift + cy, :]


def send_sides(odd, up, down, pay_b, pay_a, rows, get):
    for k, (u, d) in enumerate(zip(up, down)):
        part = slice(k * rows, (k + 1) * rows)
        upper, lower = get(*u), get(*d)
        pay_b[part, :] = jnp.where(odd, upper, lower)
        pay_a[part, :] = jnp.where(odd, lower, upper)


def send_rows(sec, comps, pay_s, get_rows, cx, cy):
    for k, comp in enumerate(comps):
        for x in range(cx):
            part = slice((k * cx + x) * SIDE, (k * cx + x + 1) * SIDE)
            pay_s[part, :] = jnp.where(
                sec == 0, get_rows(comp, x, cy - SIDE), get_rows(comp, x, 0)
            )


STRESS_ROWS = (1, 3, 5)
VELOCITY_ROWS = (0, 1, 2)


def stress_up(cx):
    return [(0, cx - 1), (3, cx - 2), (3, cx - 1), (4, cx - 2), (4, cx - 1)]


def stress_down(cx):
    return [(0, 0), (0, 1), (3, 0), (4, 0), (4, 0)]


def velocity_up(cx):
    return [(0, cx - 2), (0, cx - 1), (1, cx - 1), (2, cx - 1), (2, cx - 1)]


def velocity_down(cx):
    return [(0, 0), (1, 0), (1, 1), (2, 0), (2, 1)]


def first_sides(s, pay_b, pay_a, pay_s, sems):
    odd, sec, _ = place()
    _, cx, cy, _ = s.shape
    copies = []
    for k, (u, d) in enumerate(zip(stress_up(cx), stress_down(cx))):
        part = pl.ds(k * cy, cy)
        for pay, (p, q) in ((pay_b, (u, d)), (pay_a, (d, u))):
            source = s.at[jnp.where(odd, p[0], q[0]), jnp.where(odd, p[1], q[1])]
            copies.append(pltpu.make_async_copy(source, pay.at[part], sems.at[len(copies)]))
    begin = pl.multiple_of(jnp.where(sec == 0, cy - SIDE, 0), SIDE)
    for k, comp in enumerate(STRESS_ROWS):
        source = s.at[comp, :, pl.ds(begin, SIDE), :]
        copies.append(pltpu.make_async_copy(source, pay_s.at[k], sems.at[len(copies)]))
    for copy in copies:
        copy.start()
    for copy in copies:
        copy.wait()


def step_velocity(s, v, b, from_b, from_a, from_s, v_out, pay_b, pay_a, pay_s, rows_ref):
    odd, sec, _ = place()
    _, cx, cy, nz = s.shape
    fw, bw = depth_weights(nz)
    low, high = sides(odd, from_b, from_a, cy)
    fill_rows(rows_ref, STRESS_ROWS, lambda c, x: s[c, x], from_s, sec, cx, cy)
    xx = along(lambda x: s[0, x], cx, low, {-1: 0}, high, {cx: 0, cx + 1: 1})
    xy = along(lambda x: s[3, x], cx, low, {-2: 1, -1: 2}, high, {cx: 2})
    xz = along(lambda x: s[4, x], cx, low, {-2: 3, -1: 4}, high, {cx: 3})
    for x in range(cx):
        scale = DT * b[x]
        yy = rows_at(rows_ref, 0, x, cy)
        xy_rows = rows_at(rows_ref, 1, x, cy)
        yz = rows_at(rows_ref, 2, x, cy)
        v_out[0, x] = v[0, x] + scale * (
            forward(xx, x) + backward(xy_rows, 0) + backward_z(s[4, x], bw)
        )
        v_out[1, x] = v[1, x] + scale * (
            backward(xy, x) + forward(yy, 0) + backward_z(s[5, x], bw)
        )
        v_out[2, x] = v[2, x] + scale * (
            backward(xz, x) + backward(yz, 0) + forward_z(s[2, x], fw)
        )
    send_sides(odd, velocity_up(cx), velocity_down(cx), pay_b, pay_a, cy, lambda c, x: v_out[c, x])
    send_rows(sec, VELOCITY_ROWS, pay_s, lambda c, x, y: v_out[c, x, y : y + SIDE, :], cx, cy)


def last_velocity(
    s, v, b, from_b, from_a, from_s, ocean, marks, v_out, pay_b, pay_a, pay_s, patch, rows_ref
):
    step_velocity(s, v, b, from_b, from_a, from_s, v_out, pay_b, pay_a, pay_s, rows_ref)
    odd, _, _ = place()
    _, cx, cy, nz = s.shape
    first = (lax.broadcasted_iota(jnp.int32, (8, nz), 1) == 0).astype(F32)
    floor = jnp.concatenate([v_out[2, x] for x in range(cx)], axis=0)
    line = lax.dot_general(
        first,
        floor,
        (((1,), (1,)), ((), ())),
        precision=lax.Precision.HIGHEST,
        preferred_element_type=F32,
    )
    pieces = cx * cy // 128
    turn = lax.rem(lax.broadcasted_iota(jnp.int32, (8, 128), 0), pieces)
    tiled = line[:, 0:128]
    for k in range(1, pieces):
        tiled = jnp.where(turn == k, line[:, k * 128 : (k + 1) * 128], tiled)
    for k in range(0, patch.shape[0], 8):
        patch[k : k + 8, :] = tiled
    fields, rows, columns = ocean.shape
    base = EDGE * cy
    for k in range(columns // 128):
        lanes = slice(k * 128, (k + 1) * 128)
        for f in range(fields):
            n = DEEP[f]
            upper, lower = ocean[f, rows - n : rows, lanes], ocean[f, 0:n, lanes]
            pay_b[base : base + n, :] = jnp.where(odd, upper, lower)
            pay_a[base : base + n, :] = jnp.where(odd, lower, upper)
            base += n
    upper, lower = marks[rows - SIDE : rows, :], marks[0:SIDE, :]
    pay_b[base : base + SIDE, :] = jnp.where(odd, upper, lower)
    pay_a[base : base + SIDE, :] = jnp.where(odd, lower, upper)


def update_stress(v, s, lam, mu, from_b, from_a, from_s, s_out, rows_ref, each=None):
    odd, sec, _ = place()
    _, cx, cy, nz = s.shape
    fw, bw = depth_weights(nz)
    low, high = sides(odd, from_b, from_a, cy)
    fill_rows(rows_ref, VELOCITY_ROWS, lambda c, x: v[c, x], from_s, sec, cx, cy)
    vx = along(lambda x: v[0, x], cx, low, {-2: 0, -1: 1}, high, {cx: 0})
    vy = along(lambda x: v[1, x], cx, low, {-1: 2}, high, {cx: 1, cx + 1: 2})
    vz = along(lambda x: v[2, x], cx, low, {-1: 3}, high, {cx: 3, cx + 1: 4})
    for x in range(cx):
        shear = DT * mu[x]
        double = 2.0 * shear
        vx_rows, vy_rows, vz_rows = (rows_at(rows_ref, k, x, cy) for k in range(3))
        exx = backward(vx, x)
        eyy = backward(vy_rows, 0)
        ezz = backward_z(v[2, x], bw)
        volume = (DT * lam[x]) * (exx + eyy + ezz)
        s_out[0, x] = s[0, x] + (volume + double * exx)
        s_out[1, x] = s[1, x] + (volume + double * eyy)
        s_out[2, x] = s[2, x] + (volume + double * ezz)
        s_out[3, x] = s[3, x] + shear * (forward(vx_rows, 0) + forward(vy, x))
        s_out[4, x] = s[4, x] + shear * (forward_z(v[0, x], fw) + forward(vz, x))
        s_out[5, x] = s[5, x] + shear * (forward_z(v[1, x], fw) + forward(vz_rows, 0))
        if each is not None:
            each(x)


def step_stress(v, s, lam, mu, from_b, from_a, from_s, s_out, pay_b, pay_a, pay_s, rows_ref):
    odd, sec, _ = place()
    _, cx, cy, nz = s.shape
    update_stress(v, s, lam, mu, from_b, from_a, from_s, s_out, rows_ref)
    send_sides(odd, stress_up(cx), stress_down(cx), pay_b, pay_a, cy, lambda c, x: s_out[c, x])
    send_rows(sec, STRESS_ROWS, pay_s, lambda c, x, y: s_out[c, x, y : y + SIDE, :], cx, cy)


def last_stress(v, s, lam, mu, from_b, from_a, from_s, v_out, s_out, rows_ref, made, sems):
    cx = s.shape[1]
    copies = [pltpu.make_async_copy(v, v_out, sems.at[cx])]
    copies[0].start()

    def each(x):
        copy = pltpu.make_async_copy(made.at[:, x], s_out.at[:, x], sems.at[x])
        copy.start()
        copies.append(copy)

    update_stress(v, s, lam, mu, from_b, from_a, from_s, made, rows_ref, each)
    for copy in copies:
        copy.wait()


def ocean_steps(start, from_b, from_a, ocean, marks, patches, ocean_out, ocean_ref, marks_ref):
    odd, sec, tile = place()
    count = lax.axis_size("tile")
    fields, rows, columns = ocean.shape
    own = ocean_out.shape[2]
    top, bottom = slice(0, SIDE), slice(SIDE + rows, SIDE + rows + SIDE)
    at = start
    for f in range(fields):
        ocean_ref[f, SIDE : SIDE + rows, :] = ocean[f]
        ocean_ref[f, top, :] = jnp.zeros((SIDE, columns), F32)
        ocean_ref[f, bottom, :] = jnp.zeros((SIDE, columns), F32)
    for k in range(columns // 128):
        lanes = slice(k * 128, (k + 1) * 128)
        for f in range(fields):
            n = DEEP[f]
            b, a = from_b[at : at + n, :], from_a[at : at + n, :]
            ocean_ref[f, SIDE - n : SIDE, lanes] = jnp.where(odd, a, b)
            ocean_ref[f, SIDE + rows : SIDE + rows + n, lanes] = jnp.where(odd, b, a)
            at += n
    b, a = from_b[at : at + SIDE, :], from_a[at : at + SIDE, :]
    marks_ref[SIDE : SIDE + rows, :] = marks[...]
    marks_ref[top, :] = jnp.where(odd, a, b)
    marks_ref[bottom, :] = jnp.where(odd, b, a)

    total = rows + 2 * SIDE
    lane = lax.broadcasted_iota(jnp.int32, (1, columns), 1)
    ahead = jnp.where((lane == own - 1) & (sec == 1), 0.0, 0.5).astype(F32)
    behind = jnp.where((lane == 0) & (sec == 0), 0.0, 0.5).astype(F32)
    line = lax.broadcasted_iota(jnp.int32, (total, 1), 0)
    inside = ((line >= SIDE) | (tile > 0)) & ((line < SIDE + rows) | (tile < count - 1))
    inside = inside.astype(F32)

    def across(f):
        return pltpu.roll(f, columns - 1, 1) * ahead - pltpu.roll(f, 1, 1) * behind

    def down(f):
        return 0.5 * (pltpu.roll(f, total - 1, 0) - pltpu.roll(f, 1, 0))

    eta, u, v_sea = ocean_ref[0], ocean_ref[1], ocean_ref[2]
    depth, wet = ocean_ref[3], ocean_ref[4]
    window = min(WINDOW, count)
    base = jnp.clip(tile - REACH - 1, 0, count - window)
    owner = jnp.broadcast_to(marks_ref[:, 0:1] - base.astype(F32), (total, 128))
    share = marks_ref[:, 1:2]
    pieces = own // 128
    parts = [(sec, k) for k in range(pieces)] + [(1 - sec, sec * (pieces - 1))]
    uplift = []
    for half, piece in parts:
        level = jnp.zeros((total, 128), F32)
        for k in range(window):
            row = (half * count + base + k) * pieces + piece
            level = jnp.where(owner == float(k), patches[pl.ds(row, 1), :], level)
        uplift.append(level)
    uplift = jnp.concatenate(uplift, axis=1)
    lift = ODT * (share * wet * uplift)
    for _ in range(2):
        u = wet * (u - ODT * down(eta))
        v_sea = wet * (v_sea - ODT * across(eta))
        eta = inside * (eta - ODT * (down(depth * u) + across(depth * v_sea)) + lift)
    part = slice(SIDE, SIDE + rows)
    ocean_out[0] = eta[part, :own]
    ocean_out[1] = u[part, :own]
    ocean_out[2] = v_sea[part, :own]


VMEM = pl.BlockSpec(memory_space=pltpu.VMEM)
ANY = pl.BlockSpec(memory_space=pl.ANY)


def call(body, name, outs, scratch, operands, weight=1, ins=VMEM, where=VMEM):
    shapes = [jax.ShapeDtypeStruct(o, F32) for o in outs]
    moved = sum(o.size for o in operands) * 4 + sum(o.size for o in shapes) * 4
    return pl.pallas_call(
        body,
        name=name,
        out_shape=shapes,
        in_specs=[ins] * len(operands),
        out_specs=[where] * len(outs),
        scratch_shapes=scratch,
        compiler_params=pltpu.CompilerParams(vmem_limit_bytes=32 * 1024 * 1024),
        cost_estimate=pl.CostEstimate(
            flops=moved, bytes_accessed=moved * weight, transcendentals=0
        ),
    )(*operands)


def exchange(pay_b, pay_a, count):
    def swap(pay, first):
        pairs = []
        for i in range(first, count - 1, 2):
            pairs += [(i, i + 1), (i + 1, i)]
        return lax.ppermute(pay, "tile", pairs)

    return swap(pay_b, 1), swap(pay_a, 0)


def across(pay):
    return lax.ppermute(pay, "sec", [(0, 1), (1, 0)])


def shards(
    velocity,
    stresses,
    buoyancy,
    lame_first,
    shear_mod,
    ocean_state,
    depth_map,
    wet_mask,
    intersection_src,
    intersection_share,
):
    count = lax.axis_size("tile")
    sec = lax.axis_index("sec")
    _, cx, cy, nz = stresses.shape
    _, rows, columns = ocean_state.shape
    side = (EDGE * cy, nz)
    strip = (3 * cx * SIDE, nz)
    halo_rows = pltpu.VMEM((3, cx, cy + 2 * SIDE, nz), F32)

    pay_b, pay_a, pay_s = call(
        first_sides,
        "first_sides",
        [side, side, (3, cx, SIDE, nz)],
        [pltpu.SemaphoreType.DMA((2 * EDGE + 3,))],
        [stresses],
        ins=ANY,
    )
    from_b, from_a = exchange(pay_b, pay_a, count)
    from_s = across(pay_s.reshape(strip))

    fields = jnp.concatenate([ocean_state, depth_map[None], wet_mask.astype(F32)[None]])
    near = jnp.where(sec == 0, fields[:, :, columns - 128 :], fields[:, :, :128])
    ocean = jnp.concatenate([fields, across(near)], axis=2)
    lane = lax.broadcasted_iota(jnp.int32, (rows, 128), 1)
    marks = jnp.where(
        lane == 0,
        intersection_src.astype(F32)[:, None],
        jnp.where(lane == 1, intersection_share[:, None], 0.0),
    )

    velocity, pay_b, pay_a, pay_s = call(
        step_velocity,
        "velocity_step",
        [velocity.shape, side, side, strip],
        [halo_rows],
        [stresses, velocity, buoyancy, from_b, from_a, from_s],
    )
    from_b, from_a = exchange(pay_b, pay_a, count)
    from_s = across(pay_s)
    stresses, pay_b, pay_a, pay_s = call(
        step_stress,
        "stress_step",
        [stresses.shape, side, side, strip],
        [halo_rows],
        [velocity, stresses, lame_first, shear_mod, from_b, from_a, from_s],
    )
    from_b, from_a = exchange(pay_b, pay_a, count)
    from_s = across(pay_s)
    long_side = (EDGE * cy + ocean.shape[2] // 128 * PACK + SIDE, nz)
    pieces = cx * cy // 128
    velocity, pay_b, pay_a, pay_s, patch = call(
        last_velocity,
        "velocity_last",
        [velocity.shape, long_side, long_side, strip, (2 * count * pieces, 128)],
        [halo_rows],
        [stresses, velocity, buoyancy, from_b, from_a, from_s, ocean, marks],
    )
    from_b, from_a = exchange(pay_b, pay_a, count)
    from_s = across(pay_s)
    patches = lax.all_to_all(patch.reshape(2 * count, pieces, 128), ("sec", "tile"), 0, 0)
    velocity, stresses = call(
        last_stress,
        "stress_last",
        [velocity.shape, stresses.shape],
        [halo_rows, pltpu.VMEM(stresses.shape, F32), pltpu.SemaphoreType.DMA((cx + 1,))],
        [velocity, stresses, lame_first, shear_mod, from_b, from_a, from_s],
        weight=8,
        where=ANY,
    )
    (ocean_state,) = call(
        functools.partial(ocean_steps, EDGE * cy),
        "ocean_steps",
        [ocean_state.shape],
        [
            pltpu.VMEM((ocean.shape[0], rows + 2 * SIDE, ocean.shape[2]), F32),
            pltpu.VMEM((rows + 2 * SIDE, 128), F32),
        ],
        [from_b, from_a, ocean, marks, patches.reshape(-1, 128)],
    )
    return velocity, stresses, ocean_state


def solution(mesh):
    cube = P("tile", "sec", None)
    return jax.shard_map(
        shards,
        mesh=mesh,
        in_specs=(
            P(None, "tile", "sec", None),
            P(None, "tile", "sec", None),
            cube,
            cube,
            cube,
            P(None, "tile", "sec"),
            P("tile", "sec"),
            P("tile", "sec"),
            P("tile"),
            P("tile"),
        ),
        out_specs=(
            P(None, "tile", "sec", None),
            P(None, "tile", "sec", None),
            P(None, "tile", "sec"),
        ),
        check_vma=False,
    )
```

```python
import functools

import jax
import jax.numpy as jnp
from jax import lax
from jax.experimental import pallas as pl
from jax.experimental.pallas import tpu as pltpu
from jax.sharding import PartitionSpec as P

STEPS = 2
REACH = 2
NEAR = 9.0 / 8.0
FAR = 1.0 / 24.0
DT = 0.15
ODT = 0.3
F32 = jnp.float32
EDGE = 5
SIDE = 8
WINDOW = 8
DEEP = (4, 3, 3, 3, 3)
PACK = sum(DEEP)


def depth_weights(width):
    lane = lax.broadcasted_iota(jnp.int32, (1, width), 1)

    def weight(value, first, last):
        return jnp.where((lane >= first) & (lane < last), value, 0.0).astype(F32)

    forward = (weight(NEAR, 0, width - 1), weight(-FAR, 0, width - 2), weight(FAR, 1, width))
    backward = (weight(-NEAR, 1, width), weight(-FAR, 0, width - 1), weight(FAR, 2, width))
    return forward, backward


def forward_z(f, weights):
    near, far, behind = weights
    n = f.shape[-1]
    return (
        pltpu.roll(f, n - 1, 1) * near
        - NEAR * f
        + pltpu.roll(f, n - 2, 1) * far
        + pltpu.roll(f, 1, 1) * behind
    )


def backward_z(f, weights):
    near, far, behind = weights
    n = f.shape[-1]
    return (
        NEAR * f
        + pltpu.roll(f, 1, 1) * near
        + pltpu.roll(f, n - 1, 1) * far
        + pltpu.roll(f, 2, 1) * behind
    )


def forward(at, i):
    return NEAR * (at(i + 1) - at(i)) - FAR * (at(i + 2) - at(i - 1))


def backward(at, i):
    return NEAR * (at(i) - at(i - 1)) - FAR * (at(i + 1) - at(i - 2))


def place():
    tile, sec = lax.axis_index("tile"), lax.axis_index("sec")
    return lax.rem(tile, 2) == 1, sec, tile


def sides(odd, from_a, from_b, rows):
    def low(k):
        part = slice(k * rows, (k + 1) * rows)
        return jnp.where(odd, from_a[part, :], from_b[part, :])

    def high(k):
        part = slice(k * rows, (k + 1) * rows)
        return jnp.where(odd, from_b[part, :], from_a[part, :])

    return low, high


def along(own, count, low, low_from, high, high_from):
    def at(x):
        if x < 0:
            return low(low_from[x])
        if x >= count:
            return high(high_from[x])
        return own(x)

    return at


def fill_rows(rows_ref, comps, own, side_ref, sec, cx, cy):
    low_on = (sec == 1).astype(F32)
    high_on = (sec == 0).astype(F32)
    for k, comp in enumerate(comps):
        for x in range(cx):
            rows_ref[k, x, SIDE : SIDE + cy, :] = own(comp, x)
            got = side_ref[(k * cx + x) * SIDE : (k * cx + x + 1) * SIDE, :]
            rows_ref[k, x, 0:SIDE, :] = got * low_on
            rows_ref[k, x, SIDE + cy : SIDE + cy + SIDE, :] = got * high_on


def rows_at(rows_ref, k, x, cy):
    return lambda shift: rows_ref[k, x, SIDE + shift : SIDE + shift + cy, :]


def send_sides(odd, up, down, pay_a, pay_b, rows, get):
    for k, (u, d) in enumerate(zip(up, down)):
        part = slice(k * rows, (k + 1) * rows)
        upper, lower = get(*u), get(*d)
        pay_b[part, :] = jnp.where(odd, upper, lower)
        pay_a[part, :] = jnp.where(odd, lower, upper)


def send_rows(sec, comps, pay_s, get_rows, cx, cy):
    for k, comp in enumerate(comps):
        for x in range(cx):
            part = slice((k * cx + x) * SIDE, (k * cx + x + 1) * SIDE)
            pay_s[part, :] = jnp.where(
                sec == 0, get_rows(comp, x, cy - SIDE), get_rows(comp, x, 0)
            )


STRESS_ROWS = (1, 3, 5)
VELOCITY_ROWS = (0, 1, 2)


def stress_up(cx):
    return [(0, cx - 1), (3, cx - 2), (3, cx - 1), (4, cx - 2), (4, cx - 1)]


def stress_down(cx):
    return [(0, 0), (0, 1), (3, 0), (4, 0), (4, 0)]


def velocity_up(cx):
    return [(0, cx - 2), (0, cx - 1), (1, cx - 1), (2, cx - 1), (2, cx - 1)]


def velocity_down(cx):
    return [(0, 0), (1, 0), (1, 1), (2, 0), (2, 1)]


def first_sides(s, pay_a, pay_b, pay_s, sems):
    odd, sec, _ = place()
    _, cx, cy, _ = s.shape
    copies = []
    for k, (u, d) in enumerate(zip(stress_up(cx), stress_down(cx))):
        part = pl.ds(k * cy, cy)
        for pay, (p, q) in ((pay_a, (d, u)), (pay_b, (u, d))):
            source = s.at[jnp.where(odd, p[0], q[0]), jnp.where(odd, p[1], q[1])]
            copies.append(pltpu.make_async_copy(source, pay.at[part], sems.at[len(copies)]))
    begin = pl.multiple_of(jnp.where(sec == 0, cy - SIDE, 0), SIDE)
    for k, comp in enumerate(STRESS_ROWS):
        source = s.at[comp, :, pl.ds(begin, SIDE), :]
        copies.append(pltpu.make_async_copy(source, pay_s.at[k], sems.at[len(copies)]))
    for copy in copies:
        copy.start()
    for copy in copies:
        copy.wait()


def step_velocity(s, v, b, from_a, from_b, from_s, v_out, pay_a, pay_b, pay_s, rows_ref):
    odd, sec, _ = place()
    _, cx, cy, nz = s.shape
    fw, bw = depth_weights(nz)
    low, high = sides(odd, from_a, from_b, cy)
    fill_rows(rows_ref, STRESS_ROWS, lambda c, x: s[c, x], from_s, sec, cx, cy)
    xx = along(lambda x: s[0, x], cx, low, {-1: 0}, high, {cx: 0, cx + 1: 1})
    xy = along(lambda x: s[3, x], cx, low, {-2: 1, -1: 2}, high, {cx: 2})
    xz = along(lambda x: s[4, x], cx, low, {-2: 3, -1: 4}, high, {cx: 3})
    for x in range(cx):
        scale = DT * b[x]
        yy = rows_at(rows_ref, 0, x, cy)
        xy_rows = rows_at(rows_ref, 1, x, cy)
        yz = rows_at(rows_ref, 2, x, cy)
        v_out[0, x] = v[0, x] + scale * (
            forward(xx, x) + backward(xy_rows, 0) + backward_z(s[4, x], bw)
        )
        v_out[1, x] = v[1, x] + scale * (
            backward(xy, x) + forward(yy, 0) + backward_z(s[5, x], bw)
        )
        v_out[2, x] = v[2, x] + scale * (
            backward(xz, x) + backward(yz, 0) + forward_z(s[2, x], fw)
        )
    send_sides(odd, velocity_up(cx), velocity_down(cx), pay_a, pay_b, cy, lambda c, x: v_out[c, x])
    send_rows(sec, VELOCITY_ROWS, pay_s, lambda c, x, y: v_out[c, x, y : y + SIDE, :], cx, cy)


def last_velocity(
    s, v, b, from_a, from_b, from_s, ocean, marks, v_out, pay_a, pay_b, pay_s, patch, rows_ref
):
    step_velocity(s, v, b, from_a, from_b, from_s, v_out, pay_a, pay_b, pay_s, rows_ref)
    odd, _, _ = place()
    _, cx, cy, nz = s.shape
    first = (lax.broadcasted_iota(jnp.int32, (8, nz), 1) == 0).astype(F32)
    floor = jnp.concatenate([v_out[2, x] for x in range(cx)], axis=0)
    line = lax.dot_general(
        first,
        floor,
        (((1,), (1,)), ((), ())),
        precision=lax.Precision.HIGHEST,
        preferred_element_type=F32,
    )
    pieces = cx * cy // 128
    turn = lax.rem(lax.broadcasted_iota(jnp.int32, (8, 128), 0), pieces)
    tiled = line[:, 0:128]
    for k in range(1, pieces):
        tiled = jnp.where(turn == k, line[:, k * 128 : (k + 1) * 128], tiled)
    for k in range(0, patch.shape[0], 8):
        patch[k : k + 8, :] = tiled
    fields, rows, columns = ocean.shape
    base = EDGE * cy
    for k in range(columns // 128):
        lanes = slice(k * 128, (k + 1) * 128)
        for f in range(fields):
            n = DEEP[f]
            upper, lower = ocean[f, rows - n : rows, lanes], ocean[f, 0:n, lanes]
            pay_b[base : base + n, :] = jnp.where(odd, upper, lower)
            pay_a[base : base + n, :] = jnp.where(odd, lower, upper)
            base += n
    upper, lower = marks[rows - SIDE : rows, :], marks[0:SIDE, :]
    pay_b[base : base + SIDE, :] = jnp.where(odd, upper, lower)
    pay_a[base : base + SIDE, :] = jnp.where(odd, lower, upper)


def update_stress(v, s, lam, mu, from_a, from_b, from_s, s_out, rows_ref, each=None):
    odd, sec, _ = place()
    _, cx, cy, nz = s.shape
    fw, bw = depth_weights(nz)
    low, high = sides(odd, from_a, from_b, cy)
    fill_rows(rows_ref, VELOCITY_ROWS, lambda c, x: v[c, x], from_s, sec, cx, cy)
    vx = along(lambda x: v[0, x], cx, low, {-2: 0, -1: 1}, high, {cx: 0})
    vy = along(lambda x: v[1, x], cx, low, {-1: 2}, high, {cx: 1, cx + 1: 2})
    vz = along(lambda x: v[2, x], cx, low, {-1: 3}, high, {cx: 3, cx + 1: 4})
    for x in range(cx):
        shear = DT * mu[x]
        double = 2.0 * shear
        vx_rows, vy_rows, vz_rows = (rows_at(rows_ref, k, x, cy) for k in range(3))
        exx = backward(vx, x)
        eyy = backward(vy_rows, 0)
        ezz = backward_z(v[2, x], bw)
        volume = (DT * lam[x]) * (exx + eyy + ezz)
        s_out[0, x] = s[0, x] + (volume + double * exx)
        s_out[1, x] = s[1, x] + (volume + double * eyy)
        s_out[2, x] = s[2, x] + (volume + double * ezz)
        s_out[3, x] = s[3, x] + shear * (forward(vx_rows, 0) + forward(vy, x))
        s_out[4, x] = s[4, x] + shear * (forward_z(v[0, x], fw) + forward(vz, x))
        s_out[5, x] = s[5, x] + shear * (forward_z(v[1, x], fw) + forward(vz_rows, 0))
        if each is not None:
            each(x)


def step_stress(v, s, lam, mu, from_a, from_b, from_s, s_out, pay_a, pay_b, pay_s, rows_ref):
    odd, sec, _ = place()
    _, cx, cy, nz = s.shape
    update_stress(v, s, lam, mu, from_a, from_b, from_s, s_out, rows_ref)
    send_sides(odd, stress_up(cx), stress_down(cx), pay_a, pay_b, cy, lambda c, x: s_out[c, x])
    send_rows(sec, STRESS_ROWS, pay_s, lambda c, x, y: s_out[c, x, y : y + SIDE, :], cx, cy)


def last_stress(
    v, s, lam, mu, from_a, from_b, from_s, v_out, s_out, done, rows_ref, made, sems
):
    done[...] = jnp.zeros(done.shape, F32)
    cx = s.shape[1]
    copies = [pltpu.make_async_copy(v, v_out, sems.at[cx])]
    copies[0].start()

    def each(x):
        copy = pltpu.make_async_copy(made.at[:, x], s_out.at[:, x], sems.at[x])
        copy.start()
        copies.append(copy)

    update_stress(v, s, lam, mu, from_a, from_b, from_s, made, rows_ref, each)
    for copy in copies:
        copy.wait()


def ocean_steps(
    start, from_a, from_b, ocean, marks, patches, _, ocean_out, ocean_ref, marks_ref
):
    odd, sec, tile = place()
    count = lax.axis_size("tile")
    fields, rows, columns = ocean.shape
    own = ocean_out.shape[2]
    top, bottom = slice(0, SIDE), slice(SIDE + rows, SIDE + rows + SIDE)
    at = start
    for f in range(fields):
        ocean_ref[f, SIDE : SIDE + rows, :] = ocean[f]
        ocean_ref[f, top, :] = jnp.zeros((SIDE, columns), F32)
        ocean_ref[f, bottom, :] = jnp.zeros((SIDE, columns), F32)
    for k in range(columns // 128):
        lanes = slice(k * 128, (k + 1) * 128)
        for f in range(fields):
            n = DEEP[f]
            b, a = from_b[at : at + n, :], from_a[at : at + n, :]
            ocean_ref[f, SIDE - n : SIDE, lanes] = jnp.where(odd, a, b)
            ocean_ref[f, SIDE + rows : SIDE + rows + n, lanes] = jnp.where(odd, b, a)
            at += n
    b, a = from_b[at : at + SIDE, :], from_a[at : at + SIDE, :]
    marks_ref[SIDE : SIDE + rows, :] = marks[...]
    marks_ref[top, :] = jnp.where(odd, a, b)
    marks_ref[bottom, :] = jnp.where(odd, b, a)

    total = rows + 2 * SIDE
    lane = lax.broadcasted_iota(jnp.int32, (1, columns), 1)
    ahead = jnp.where((lane == own - 1) & (sec == 1), 0.0, 0.5).astype(F32)
    behind = jnp.where((lane == 0) & (sec == 0), 0.0, 0.5).astype(F32)
    line = lax.broadcasted_iota(jnp.int32, (total, 1), 0)
    inside = ((line >= SIDE) | (tile > 0)) & ((line < SIDE + rows) | (tile < count - 1))
    inside = inside.astype(F32)

    def across(f):
        return pltpu.roll(f, columns - 1, 1) * ahead - pltpu.roll(f, 1, 1) * behind

    def down(f):
        return 0.5 * (pltpu.roll(f, total - 1, 0) - pltpu.roll(f, 1, 0))

    eta, u, v_sea = ocean_ref[0], ocean_ref[1], ocean_ref[2]
    depth, wet = ocean_ref[3], ocean_ref[4]
    window = min(WINDOW, count)
    base = jnp.clip(tile - REACH - 1, 0, count - window)
    owner = jnp.broadcast_to(marks_ref[:, 0:1] - base.astype(F32), (total, 128))
    share = marks_ref[:, 1:2]
    pieces = own // 128
    parts = [(sec, k) for k in range(pieces)] + [(1 - sec, sec * (pieces - 1))]
    uplift = []
    for half, piece in parts:
        level = jnp.zeros((total, 128), F32)
        for k in range(window):
            row = (half * count + base + k) * pieces + piece
            level = jnp.where(owner == float(k), patches[pl.ds(row, 1), :], level)
        uplift.append(level)
    uplift = jnp.concatenate(uplift, axis=1)
    lift = ODT * (share * wet * uplift)
    for _ in range(2):
        u = wet * (u - ODT * down(eta))
        v_sea = wet * (v_sea - ODT * across(eta))
        eta = inside * (eta - ODT * (down(depth * u) + across(depth * v_sea)) + lift)
    part = slice(SIDE, SIDE + rows)
    ocean_out[0] = eta[part, :own]
    ocean_out[1] = u[part, :own]
    ocean_out[2] = v_sea[part, :own]


VMEM = pl.BlockSpec(memory_space=pltpu.VMEM)
ANY = pl.BlockSpec(memory_space=pl.ANY)


def call(body, name, outs, scratch, operands, weight=1, ins=VMEM, where=VMEM, grant=32):
    shapes = [jax.ShapeDtypeStruct(o, F32) for o in outs]
    moved = sum(o.size for o in operands) * 4 + sum(o.size for o in shapes) * 4
    return pl.pallas_call(
        body,
        name=name,
        out_shape=shapes,
        in_specs=ins if isinstance(ins, list) else [ins] * len(operands),
        out_specs=where if isinstance(where, list) else [where] * len(outs),
        scratch_shapes=scratch,
        compiler_params=pltpu.CompilerParams(vmem_limit_bytes=grant * 1024 * 1024),
        cost_estimate=pl.CostEstimate(
            flops=moved, bytes_accessed=moved * weight, transcendentals=0
        ),
    )(*operands)


def exchange(pay_a, pay_b, count):
    def swap(pay, first):
        pairs = []
        for i in range(first, count - 1, 2):
            pairs += [(i, i + 1), (i + 1, i)]
        return lax.ppermute(pay, "tile", pairs)

    from_a = swap(pay_a, 0)
    return from_a, swap(pay_b, 1)


def across(pay):
    return lax.ppermute(pay, "sec", [(0, 1), (1, 0)])


def shards(
    velocity,
    stresses,
    buoyancy,
    lame_first,
    shear_mod,
    ocean_state,
    depth_map,
    wet_mask,
    intersection_src,
    intersection_share,
):
    count = lax.axis_size("tile")
    sec = lax.axis_index("sec")
    _, cx, cy, nz = stresses.shape
    _, rows, columns = ocean_state.shape
    side = (EDGE * cy, nz)
    strip = (3 * cx * SIDE, nz)
    halo_rows = pltpu.VMEM((3, cx, cy + 2 * SIDE, nz), F32)

    pay_a, pay_b, pay_s = call(
        first_sides,
        "first_sides",
        [side, side, (3, cx, SIDE, nz)],
        [pltpu.SemaphoreType.DMA((2 * EDGE + 3,))],
        [stresses],
        ins=ANY,
        grant=60,
    )
    from_a, from_b = exchange(pay_a, pay_b, count)
    from_s = across(pay_s.reshape(strip))

    fields = jnp.concatenate([ocean_state, depth_map[None], wet_mask.astype(F32)[None]])
    near = jnp.where(sec == 0, fields[:, :, columns - 128 :], fields[:, :, :128])
    ocean = jnp.concatenate([fields, across(near)], axis=2)
    lane = lax.broadcasted_iota(jnp.int32, (rows, 128), 1)
    marks = jnp.where(
        lane == 0,
        intersection_src.astype(F32)[:, None],
        jnp.where(lane == 1, intersection_share[:, None], 0.0),
    )

    velocity, pay_a, pay_b, pay_s = call(
        step_velocity,
        "velocity_step",
        [velocity.shape, side, side, strip],
        [halo_rows],
        [stresses, velocity, buoyancy, from_a, from_b, from_s],
    )
    from_a, from_b = exchange(pay_a, pay_b, count)
    from_s = across(pay_s)
    stresses, pay_a, pay_b, pay_s = call(
        step_stress,
        "stress_step",
        [stresses.shape, side, side, strip],
        [halo_rows],
        [velocity, stresses, lame_first, shear_mod, from_a, from_b, from_s],
    )
    from_a, from_b = exchange(pay_a, pay_b, count)
    from_s = across(pay_s)
    long_side = (EDGE * cy + ocean.shape[2] // 128 * PACK + SIDE, nz)
    pieces = cx * cy // 128
    velocity, pay_a, pay_b, pay_s, patch = call(
        last_velocity,
        "velocity_last",
        [velocity.shape, long_side, long_side, strip, (2 * count * pieces, 128)],
        [halo_rows],
        [stresses, velocity, buoyancy, from_a, from_b, from_s, ocean, marks],
    )
    from_a, from_b = exchange(pay_a, pay_b, count)
    from_s = across(pay_s)
    patches = lax.all_to_all(patch.reshape(2 * count, pieces, 128), ("sec", "tile"), 0, 0)
    velocity, stresses, done = call(
        last_stress,
        "stress_last",
        [velocity.shape, stresses.shape, (8, 128)],
        [halo_rows, pltpu.VMEM(stresses.shape, F32), pltpu.SemaphoreType.DMA((cx + 1,))],
        [velocity, stresses, lame_first, shear_mod, from_a, from_b, from_s],
        weight=8,
        where=[ANY, ANY, VMEM],
    )
    (ocean_state,) = call(
        functools.partial(ocean_steps, EDGE * cy),
        "ocean_steps",
        [ocean_state.shape],
        [
            pltpu.VMEM((ocean.shape[0], rows + 2 * SIDE, ocean.shape[2]), F32),
            pltpu.VMEM((rows + 2 * SIDE, 128), F32),
        ],
        [from_a, from_b, ocean, marks, patches.reshape(-1, 128), done],
    )
    return velocity, stresses, ocean_state


def solution(mesh):
    cube = P("tile", "sec", None)
    return jax.shard_map(
        shards,
        mesh=mesh,
        in_specs=(
            P(None, "tile", "sec", None),
            P(None, "tile", "sec", None),
            cube,
            cube,
            cube,
            P(None, "tile", "sec"),
            P("tile", "sec"),
            P("tile", "sec"),
            P("tile"),
            P("tile"),
        ),
        out_specs=(
            P(None, "tile", "sec", None),
            P(None, "tile", "sec", None),
            P(None, "tile", "sec"),
        ),
        check_vma=False,
    )
```

```python
import functools

import jax
import jax.numpy as jnp
from jax import lax
from jax.experimental import pallas as pl
from jax.experimental.pallas import tpu as pltpu
from jax.sharding import PartitionSpec as P

STEPS = 2
REACH = 2
NEAR = 9.0 / 8.0
FAR = 1.0 / 24.0
DT = 0.15
ODT = 0.3
F32 = jnp.float32
EDGE = 5
SIDE = 8
WINDOW = 8
DEEP = (4, 3, 3, 3, 3)
PACK = sum(DEEP)


def depth_weights(width):
    lane = lax.broadcasted_iota(jnp.int32, (1, width), 1)

    def weight(value, first, last):
        return jnp.where((lane >= first) & (lane < last), value, 0.0).astype(F32)

    forward = (weight(NEAR, 0, width - 1), weight(-FAR, 0, width - 2), weight(FAR, 1, width))
    backward = (weight(-NEAR, 1, width), weight(-FAR, 0, width - 1), weight(FAR, 2, width))
    return forward, backward


def forward_z(f, weights):
    near, far, behind = weights
    n = f.shape[-1]
    return (
        pltpu.roll(f, n - 1, 1) * near
        - NEAR * f
        + pltpu.roll(f, n - 2, 1) * far
        + pltpu.roll(f, 1, 1) * behind
    )


def backward_z(f, weights):
    near, far, behind = weights
    n = f.shape[-1]
    return (
        NEAR * f
        + pltpu.roll(f, 1, 1) * near
        + pltpu.roll(f, n - 1, 1) * far
        + pltpu.roll(f, 2, 1) * behind
    )


def forward(at, i):
    return NEAR * (at(i + 1) - at(i)) - FAR * (at(i + 2) - at(i - 1))


def backward(at, i):
    return NEAR * (at(i) - at(i - 1)) - FAR * (at(i + 1) - at(i - 2))


def place():
    tile, sec = lax.axis_index("tile"), lax.axis_index("sec")
    return lax.rem(tile, 2) == 1, sec, tile


def sides(odd, from_a, from_b, rows):
    def low(k):
        part = slice(k * rows, (k + 1) * rows)
        return jnp.where(odd, from_a[part, :], from_b[part, :])

    def high(k):
        part = slice(k * rows, (k + 1) * rows)
        return jnp.where(odd, from_b[part, :], from_a[part, :])

    return low, high


def along(own, count, low, low_from, high, high_from):
    def at(x):
        if x < 0:
            return low(low_from[x])
        if x >= count:
            return high(high_from[x])
        return own(x)

    return at


def fill_rows(rows_ref, comps, own, side_ref, sec, cx, cy):
    low_on = (sec == 1).astype(F32)
    high_on = (sec == 0).astype(F32)
    for k, comp in enumerate(comps):
        for x in range(cx):
            rows_ref[k, x, SIDE : SIDE + cy, :] = own(comp, x)
            got = side_ref[(k * cx + x) * SIDE : (k * cx + x + 1) * SIDE, :]
            rows_ref[k, x, 0:SIDE, :] = got * low_on
            rows_ref[k, x, SIDE + cy : SIDE + cy + SIDE, :] = got * high_on


def rows_at(rows_ref, k, x, cy):
    return lambda shift: rows_ref[k, x, SIDE + shift : SIDE + shift + cy, :]


def send_sides(odd, up, down, pay_a, pay_b, rows, get):
    for k, (u, d) in enumerate(zip(up, down)):
        part = slice(k * rows, (k + 1) * rows)
        upper, lower = get(*u), get(*d)
        pay_b[part, :] = jnp.where(odd, upper, lower)
        pay_a[part, :] = jnp.where(odd, lower, upper)


def send_rows(sec, comps, pay_s, get_rows, cx, cy):
    for k, comp in enumerate(comps):
        for x in range(cx):
            part = slice((k * cx + x) * SIDE, (k * cx + x + 1) * SIDE)
            pay_s[part, :] = jnp.where(
                sec == 0, get_rows(comp, x, cy - SIDE), get_rows(comp, x, 0)
            )


STRESS_ROWS = (1, 3, 5)
VELOCITY_ROWS = (0, 1, 2)


def stress_up(cx):
    return [(0, cx - 1), (3, cx - 2), (3, cx - 1), (4, cx - 2), (4, cx - 1)]


def stress_down(cx):
    return [(0, 0), (0, 1), (3, 0), (4, 0), (4, 0)]


def velocity_up(cx):
    return [(0, cx - 2), (0, cx - 1), (1, cx - 1), (2, cx - 1), (2, cx - 1)]


def velocity_down(cx):
    return [(0, 0), (1, 0), (1, 1), (2, 0), (2, 1)]


def first_sides(s, pay_a, pay_b, pay_s, sems):
    odd, sec, _ = place()
    _, cx, cy, _ = s.shape
    copies = []
    for k, (u, d) in enumerate(zip(stress_up(cx), stress_down(cx))):
        part = pl.ds(k * cy, cy)
        for pay, (p, q) in ((pay_a, (d, u)), (pay_b, (u, d))):
            source = s.at[jnp.where(odd, p[0], q[0]), jnp.where(odd, p[1], q[1])]
            copies.append(pltpu.make_async_copy(source, pay.at[part], sems.at[len(copies)]))
    begin = pl.multiple_of(jnp.where(sec == 0, cy - SIDE, 0), SIDE)
    for k, comp in enumerate(STRESS_ROWS):
        source = s.at[comp, :, pl.ds(begin, SIDE), :]
        copies.append(pltpu.make_async_copy(source, pay_s.at[k], sems.at[len(copies)]))
    for copy in copies:
        copy.start()
    for copy in copies:
        copy.wait()


def step_velocity(s, v, b, from_a, from_b, from_s, v_out, pay_a, pay_b, pay_s, rows_ref):
    odd, sec, _ = place()
    _, cx, cy, nz = s.shape
    fw, bw = depth_weights(nz)
    low, high = sides(odd, from_a, from_b, cy)
    fill_rows(rows_ref, STRESS_ROWS, lambda c, x: s[c, x], from_s, sec, cx, cy)
    xx = along(lambda x: s[0, x], cx, low, {-1: 0}, high, {cx: 0, cx + 1: 1})
    xy = along(lambda x: s[3, x], cx, low, {-2: 1, -1: 2}, high, {cx: 2})
    xz = along(lambda x: s[4, x], cx, low, {-2: 3, -1: 4}, high, {cx: 3})
    for x in range(cx):
        scale = DT * b[x]
        yy = rows_at(rows_ref, 0, x, cy)
        xy_rows = rows_at(rows_ref, 1, x, cy)
        yz = rows_at(rows_ref, 2, x, cy)
        v_out[0, x] = v[0, x] + scale * (
            forward(xx, x) + backward(xy_rows, 0) + backward_z(s[4, x], bw)
        )
        v_out[1, x] = v[1, x] + scale * (
            backward(xy, x) + forward(yy, 0) + backward_z(s[5, x], bw)
        )
        v_out[2, x] = v[2, x] + scale * (
            backward(xz, x) + backward(yz, 0) + forward_z(s[2, x], fw)
        )
    send_sides(odd, velocity_up(cx), velocity_down(cx), pay_a, pay_b, cy, lambda c, x: v_out[c, x])
    send_rows(sec, VELOCITY_ROWS, pay_s, lambda c, x, y: v_out[c, x, y : y + SIDE, :], cx, cy)


def last_velocity(
    s, v, b, from_a, from_b, from_s, v_out, pay_a, pay_b, pay_s, patch, rows_ref
):
    step_velocity(s, v, b, from_a, from_b, from_s, v_out, pay_a, pay_b, pay_s, rows_ref)
    _, cx, cy, _ = s.shape
    pieces = cx * cy // 128
    row = lax.broadcasted_iota(jnp.int32, (cy, 128), 0)
    lane = lax.broadcasted_iota(jnp.int32, (cy, 128), 1)
    lines = []
    for x in range(cx):
        here = lane == row + x * cy % 128
        column = jnp.broadcast_to(v_out[2, x, :, 0:1], (cy, 128))
        lines.append(jnp.sum(jnp.where(here, column, 0.0), axis=0, keepdims=True))
    per = cx // pieces
    lines = [sum(lines[k * per + 1 : (k + 1) * per], lines[k * per]) for k in range(pieces)]
    turn = lax.rem(lax.broadcasted_iota(jnp.int32, (8, 128), 0), pieces)
    tiled = jnp.broadcast_to(lines[0], (8, 128))
    for k in range(1, pieces):
        tiled = jnp.where(turn == k, lines[k], tiled)
    for k in range(0, patch.shape[0], 8):
        patch[k : k + 8, :] = tiled


def update_stress(v, s, lam, mu, from_a, from_b, from_s, s_out, rows_ref, each=None):
    odd, sec, _ = place()
    _, cx, cy, nz = s.shape
    fw, bw = depth_weights(nz)
    low, high = sides(odd, from_a, from_b, cy)
    fill_rows(rows_ref, VELOCITY_ROWS, lambda c, x: v[c, x], from_s, sec, cx, cy)
    vx = along(lambda x: v[0, x], cx, low, {-2: 0, -1: 1}, high, {cx: 0})
    vy = along(lambda x: v[1, x], cx, low, {-1: 2}, high, {cx: 1, cx + 1: 2})
    vz = along(lambda x: v[2, x], cx, low, {-1: 3}, high, {cx: 3, cx + 1: 4})
    for x in range(cx):
        shear = DT * mu[x]
        double = 2.0 * shear
        vx_rows, vy_rows, vz_rows = (rows_at(rows_ref, k, x, cy) for k in range(3))
        exx = backward(vx, x)
        eyy = backward(vy_rows, 0)
        ezz = backward_z(v[2, x], bw)
        volume = (DT * lam[x]) * (exx + eyy + ezz)
        s_out[0, x] = s[0, x] + (volume + double * exx)
        s_out[1, x] = s[1, x] + (volume + double * eyy)
        s_out[2, x] = s[2, x] + (volume + double * ezz)
        s_out[3, x] = s[3, x] + shear * (forward(vx_rows, 0) + forward(vy, x))
        s_out[4, x] = s[4, x] + shear * (forward_z(v[0, x], fw) + forward(vz, x))
        s_out[5, x] = s[5, x] + shear * (forward_z(v[1, x], fw) + forward(vz_rows, 0))
        if each is not None:
            each(x)


def step_stress(
    v, s, lam, mu, from_a, from_b, from_s, ocean, marks, s_out, pay_a, pay_b, pay_s, rows_ref
):
    odd, sec, _ = place()
    _, cx, cy, nz = s.shape
    update_stress(v, s, lam, mu, from_a, from_b, from_s, s_out, rows_ref)
    send_sides(odd, stress_up(cx), stress_down(cx), pay_a, pay_b, cy, lambda c, x: s_out[c, x])
    send_rows(sec, STRESS_ROWS, pay_s, lambda c, x, y: s_out[c, x, y : y + SIDE, :], cx, cy)
    fields, rows, columns = ocean.shape
    base = EDGE * cy
    for k in range(columns // 128):
        lanes = slice(k * 128, (k + 1) * 128)
        for f in range(fields):
            n = DEEP[f]
            upper, lower = ocean[f, rows - n : rows, lanes], ocean[f, 0:n, lanes]
            pay_b[base : base + n, :] = jnp.where(odd, upper, lower)
            pay_a[base : base + n, :] = jnp.where(odd, lower, upper)
            base += n
    upper, lower = marks[rows - SIDE : rows, :], marks[0:SIDE, :]
    pay_b[base : base + SIDE, :] = jnp.where(odd, upper, lower)
    pay_a[base : base + SIDE, :] = jnp.where(odd, lower, upper)


def last_stress(
    v, s, lam, mu, from_a, from_b, from_s, _, v_out, s_out, rows_ref, made, sems
):
    cx = s.shape[1]
    copies = [pltpu.make_async_copy(v, v_out, sems.at[cx])]
    copies[0].start()

    def each(x):
        copy = pltpu.make_async_copy(made.at[:, x], s_out.at[:, x], sems.at[x])
        copy.start()
        copies.append(copy)

    update_stress(v, s, lam, mu, from_a, from_b, from_s, made, rows_ref, each)
    for copy in copies:
        copy.wait()


def ocean_steps(
    start, from_a, from_b, ocean, marks, patches, ocean_out, done, ocean_ref, marks_ref
):
    done[...] = jnp.zeros(done.shape, F32)
    odd, sec, tile = place()
    count = lax.axis_size("tile")
    fields, rows, columns = ocean.shape
    own = ocean_out.shape[2]
    top, bottom = slice(0, SIDE), slice(SIDE + rows, SIDE + rows + SIDE)
    at = start
    for f in range(fields):
        ocean_ref[f, SIDE : SIDE + rows, :] = ocean[f]
        ocean_ref[f, top, :] = jnp.zeros((SIDE, columns), F32)
        ocean_ref[f, bottom, :] = jnp.zeros((SIDE, columns), F32)
    for k in range(columns // 128):
        lanes = slice(k * 128, (k + 1) * 128)
        for f in range(fields):
            n = DEEP[f]
            b, a = from_b[at : at + n, :], from_a[at : at + n, :]
            ocean_ref[f, SIDE - n : SIDE, lanes] = jnp.where(odd, a, b)
            ocean_ref[f, SIDE + rows : SIDE + rows + n, lanes] = jnp.where(odd, b, a)
            at += n
    b, a = from_b[at : at + SIDE, :], from_a[at : at + SIDE, :]
    marks_ref[SIDE : SIDE + rows, :] = marks[...]
    marks_ref[top, :] = jnp.where(odd, a, b)
    marks_ref[bottom, :] = jnp.where(odd, b, a)

    total = rows + 2 * SIDE
    lane = lax.broadcasted_iota(jnp.int32, (1, columns), 1)
    ahead = jnp.where((lane == own - 1) & (sec == 1), 0.0, 0.5).astype(F32)
    behind = jnp.where((lane == 0) & (sec == 0), 0.0, 0.5).astype(F32)
    line = lax.broadcasted_iota(jnp.int32, (total, 1), 0)
    inside = ((line >= SIDE) | (tile > 0)) & ((line < SIDE + rows) | (tile < count - 1))
    inside = inside.astype(F32)

    def across(f):
        return pltpu.roll(f, columns - 1, 1) * ahead - pltpu.roll(f, 1, 1) * behind

    def down(f):
        return 0.5 * (pltpu.roll(f, total - 1, 0) - pltpu.roll(f, 1, 0))

    eta, u, v_sea = ocean_ref[0], ocean_ref[1], ocean_ref[2]
    depth, wet = ocean_ref[3], ocean_ref[4]
    window = min(WINDOW, count)
    base = jnp.clip(tile - REACH - 1, 0, count - window)
    owner = jnp.broadcast_to(marks_ref[:, 0:1] - base.astype(F32), (total, 128))
    share = marks_ref[:, 1:2]
    pieces = own // 128
    parts = [(sec, k) for k in range(pieces)] + [(1 - sec, sec * (pieces - 1))]
    uplift = []
    for half, piece in parts:
        level = jnp.zeros((total, 128), F32)
        for k in range(window):
            row = (half * count + base + k) * pieces + piece
            level = jnp.where(owner == float(k), patches[pl.ds(row, 1), :], level)
        uplift.append(level)
    uplift = jnp.concatenate(uplift, axis=1)
    lift = ODT * (share * wet * uplift)
    for _ in range(2):
        u = wet * (u - ODT * down(eta))
        v_sea = wet * (v_sea - ODT * across(eta))
        eta = inside * (eta - ODT * (down(depth * u) + across(depth * v_sea)) + lift)
    part = slice(SIDE, SIDE + rows)
    ocean_out[0] = eta[part, :own]
    ocean_out[1] = u[part, :own]
    ocean_out[2] = v_sea[part, :own]


VMEM = pl.BlockSpec(memory_space=pltpu.VMEM)
ANY = pl.BlockSpec(memory_space=pl.ANY)


def call(body, name, outs, scratch, operands, weight=1, ins=VMEM, where=VMEM, grant=32):
    shapes = [jax.ShapeDtypeStruct(o, F32) for o in outs]
    moved = sum(o.size for o in operands) * 4 + sum(o.size for o in shapes) * 4
    return pl.pallas_call(
        body,
        name=name,
        out_shape=shapes,
        in_specs=ins if isinstance(ins, list) else [ins] * len(operands),
        out_specs=where if isinstance(where, list) else [where] * len(outs),
        scratch_shapes=scratch,
        compiler_params=pltpu.CompilerParams(vmem_limit_bytes=grant * 1024 * 1024),
        cost_estimate=pl.CostEstimate(
            flops=moved * weight, bytes_accessed=moved * weight, transcendentals=0
        ),
    )(*operands)


def exchange(pay_a, pay_b, count):
    def swap(pay, first):
        pairs = []
        for i in range(first, count - 1, 2):
            pairs += [(i, i + 1), (i + 1, i)]
        return lax.ppermute(pay, "tile", pairs)

    from_a = swap(pay_a, 0)
    return from_a, swap(pay_b, 1)


def across(pay):
    return lax.ppermute(pay, "sec", [(0, 1), (1, 0)])


def shards(
    velocity,
    stresses,
    buoyancy,
    lame_first,
    shear_mod,
    ocean_state,
    depth_map,
    wet_mask,
    intersection_src,
    intersection_share,
):
    count = lax.axis_size("tile")
    sec = lax.axis_index("sec")
    _, cx, cy, nz = stresses.shape
    _, rows, columns = ocean_state.shape
    side = (EDGE * cy, nz)
    strip = (3 * cx * SIDE, nz)
    halo_rows = pltpu.VMEM((3, cx, cy + 2 * SIDE, nz), F32)

    pay_a, pay_b, pay_s = call(
        first_sides,
        "first_sides",
        [side, side, (3, cx, SIDE, nz)],
        [pltpu.SemaphoreType.DMA((2 * EDGE + 3,))],
        [stresses],
        ins=ANY,
        grant=60,
    )
    from_a, from_b = exchange(pay_a, pay_b, count)
    from_s = across(pay_s.reshape(strip))

    fields = jnp.concatenate([ocean_state, depth_map[None], wet_mask.astype(F32)[None]])
    near = jnp.where(sec == 0, fields[:, :, columns - 128 :], fields[:, :, :128])
    ocean = jnp.concatenate([fields, across(near)], axis=2)
    lane = lax.broadcasted_iota(jnp.int32, (rows, 128), 1)
    marks = jnp.where(
        lane == 0,
        intersection_src.astype(F32)[:, None],
        jnp.where(lane == 1, intersection_share[:, None], 0.0),
    )

    velocity, pay_a, pay_b, pay_s = call(
        step_velocity,
        "velocity_step",
        [velocity.shape, side, side, strip],
        [halo_rows],
        [stresses, velocity, buoyancy, from_a, from_b, from_s],
    )
    from_a, from_b = exchange(pay_a, pay_b, count)
    from_s = across(pay_s)
    long_side = (EDGE * cy + ocean.shape[2] // 128 * PACK + SIDE, nz)
    stresses, pay_a, pay_b, pay_s = call(
        step_stress,
        "stress_step",
        [stresses.shape, long_side, long_side, strip],
        [halo_rows],
        [velocity, stresses, lame_first, shear_mod, from_a, from_b, from_s, ocean, marks],
    )
    from_a, from_b = exchange(pay_a, pay_b, count)
    sea_a, sea_b = from_a, from_b
    from_s = across(pay_s)
    pieces = cx * cy // 128
    velocity, pay_a, pay_b, pay_s, patch = call(
        last_velocity,
        "velocity_last",
        [velocity.shape, side, side, strip, (2 * count * pieces, 128)],
        [halo_rows],
        [stresses, velocity, buoyancy, from_a, from_b, from_s],
    )
    patches = lax.all_to_all(patch.reshape(2 * count, pieces, 128), ("sec", "tile"), 0, 0)
    from_a, from_b = exchange(pay_a, pay_b, count)
    from_s = across(pay_s)
    ocean_state, done = call(
        functools.partial(ocean_steps, EDGE * cy),
        "ocean_steps",
        [ocean_state.shape, (8, 128)],
        [
            pltpu.VMEM((ocean.shape[0], rows + 2 * SIDE, ocean.shape[2]), F32),
            pltpu.VMEM((rows + 2 * SIDE, 128), F32),
        ],
        [sea_a, sea_b, ocean, marks, patches.reshape(-1, 128)],
        weight=2000,
    )
    velocity, stresses = call(
        last_stress,
        "stress_last",
        [velocity.shape, stresses.shape],
        [halo_rows, pltpu.VMEM(stresses.shape, F32), pltpu.SemaphoreType.DMA((cx + 1,))],
        [velocity, stresses, lame_first, shear_mod, from_a, from_b, from_s, done],
        where=ANY,
    )
    return velocity, stresses, ocean_state


def solution(mesh):
    cube = P("tile", "sec", None)
    return jax.shard_map(
        shards,
        mesh=mesh,
        in_specs=(
            P(None, "tile", "sec", None),
            P(None, "tile", "sec", None),
            cube,
            cube,
            cube,
            P(None, "tile", "sec"),
            P("tile", "sec"),
            P("tile", "sec"),
            P("tile"),
            P("tile"),
        ),
        out_specs=(
            P(None, "tile", "sec", None),
            P(None, "tile", "sec", None),
            P(None, "tile", "sec"),
        ),
        check_vma=False,
    )
```

```python
import functools

import jax
import jax.numpy as jnp
from jax import lax
from jax.experimental import pallas as pl
from jax.experimental.pallas import tpu as pltpu
from jax.sharding import PartitionSpec as P

REACH = 2
NEAR = 9.0 / 8.0
FAR = 1.0 / 24.0
DT = 0.15
ODT = 0.3
F32 = jnp.float32
SIDE = 8
WINDOW = 8
DEEP = (4, 3, 3, 3, 3)
PACK = sum(DEEP)
NEEDED = {"s": 5, "v": 3, "b": 3}
LAST_NEEDED = 2
LAYERS = 9
STRESS_X = ((0, True), (3, False), (4, False))


def depth_weights(width):
    lane = lax.broadcasted_iota(jnp.int32, (1, width), 1)

    def weight(value, first, last):
        return jnp.where((lane >= first) & (lane < last), value, 0.0).astype(F32)

    forward = (weight(NEAR, 0, width - 1), weight(-FAR, 0, width - 2), weight(FAR, 1, width))
    backward = (weight(-NEAR, 1, width), weight(-FAR, 0, width - 1), weight(FAR, 2, width))
    return forward, backward


def forward_z(f, weights):
    near, far, behind = weights
    n = f.shape[-1]
    return (
        pltpu.roll(f, n - 1, 1) * near
        - NEAR * f
        + pltpu.roll(f, n - 2, 1) * far
        + pltpu.roll(f, 1, 1) * behind
    )


def backward_z(f, weights):
    near, far, behind = weights
    n = f.shape[-1]
    return (
        NEAR * f
        + pltpu.roll(f, 1, 1) * near
        + pltpu.roll(f, n - 1, 1) * far
        + pltpu.roll(f, 2, 1) * behind
    )


def forward(at, i):
    return NEAR * (at(i + 1) - at(i)) - FAR * (at(i + 2) - at(i - 1))


def backward(at, i):
    return NEAR * (at(i) - at(i - 1)) - FAR * (at(i + 1) - at(i - 2))


def place():
    tile, sec = lax.axis_index("tile"), lax.axis_index("sec")
    return lax.rem(tile, 2) == 1, sec, tile


def along_x(ahead, i, get):
    if ahead:
        taps = ((i + 1, NEAR), (i, -NEAR), (i + 2, -FAR), (i - 1, FAR))
    else:
        taps = ((i, NEAR), (i - 1, -NEAR), (i + 1, -FAR), (i - 2, FAR))
    total = None
    for j, weight in taps:
        layer = get(j)
        if layer is not None:
            total = weight * layer if total is None else total + weight * layer
    return total


def up_layers(cx):
    stress = [(0, cx - 1), (3, cx - 2), (3, cx - 1), (4, cx - 2), (4, cx - 1)]
    return stress, [(0, cx - 2), (0, cx - 1), (1, cx - 1), (2, cx - 1)]


def down_layers(cx):
    return [(0, 0), (0, 1), (3, 0), (4, 0)], [(0, 0), (1, 0), (1, 1), (2, 0), (2, 1)]


def halo_stress(cx):
    low = [(c, x - cx) for c, x in up_layers(cx)[0]]
    return {key: k for k, key in enumerate(low + [(c, x + cx) for c, x in down_layers(cx)[0]])}


def halo_velocity(cx):
    low = [(c, x - cx) for c, x in up_layers(cx)[1]]
    return {key: k for k, key in enumerate(low + [(c, x + cx) for c, x in down_layers(cx)[1]])}


def strip(ref, k, x, cx):
    return ref[(k * cx + x) * SIDE : (k * cx + x + 1) * SIDE, :]


def with_strip(own, edge, sec):
    return jnp.concatenate(
        [jnp.where(sec == 1, edge, 0.0), own, jnp.where(sec == 0, edge, 0.0)], axis=0
    )


def far_strip(rows, sec):
    return jnp.where(sec == 0, rows[-SIDE:], rows[:SIDE])


def yz_terms(s, comp, x, base, rows, weights):
    fw, bw = weights
    here = slice(base, base + rows)

    def beside(c):
        return lambda shift: s[c, x, base + shift : base + shift + rows, :]

    if comp == 0:
        return backward(beside(3), 0) + backward_z(s[4, x, here, :], bw)
    if comp == 1:
        return forward(beside(1), 0) + backward_z(s[5, x, here, :], bw)
    return backward(beside(5), 0) + forward_z(s[2, x, here, :], fw)


def force(s, comp, x, base, rows, weights, halo=None):
    source, ahead = STRESS_X[comp]
    cx = s.shape[1]

    def get(j):
        if 0 <= j < cx:
            return s[source, j, base : base + rows, :]
        return None if halo is None else halo(source, j)

    return along_x(ahead, x, get) + yz_terms(s, comp, x, base, rows, weights)


def own_share(s, comp, i, base, rows):
    source, ahead = STRESS_X[comp]
    cx = s.shape[1]
    return along_x(
        ahead, i, lambda j: s[source, j, base : base + rows, :] if 0 <= j < cx else None
    )


def load_stress(s, strips, s_pad, sec):
    comps, cx, cy, nz = s.shape
    nothing = jnp.zeros((SIDE, nz), F32)
    for c in range(comps):
        for x in range(cx):
            s_pad[c, x, 0:SIDE, :] = nothing
            s_pad[c, x, SIDE : 3 * SIDE + cy, :] = with_strip(s[c, x], strip(strips, c, x, cx), sec)
            s_pad[c, x, 3 * SIDE + cy :, :] = nothing


def send(odd, upper, lower, pay_a, pay_b, at):
    part = slice(at, at + upper.shape[0])
    pay_a[part, :] = jnp.where(odd, lower, upper)
    pay_b[part, :] = jnp.where(odd, upper, lower)


def send_layers(odd, up, down, layer, pay_a, pay_b, at):
    for k, (upper, lower) in enumerate(zip(up, down)):
        rows = layer(*upper)
        send(odd, rows, layer(*lower), pay_a, pay_b, at)
        at += rows.shape[0]


def first_lists(cx):
    (up_s, up_v), (down_s, down_v) = up_layers(cx), down_layers(cx)
    up_s, down_s = [("s", *key) for key in up_s], [("s", *key) for key in down_s]
    up_v, down_v = [("v", *key) for key in up_v], [("v", *key) for key in down_v]
    early = up_s + [("b", 0, cx - 1)], down_s + [("b", 0, 0), ("b", 0, 1)]
    late = up_v + [("b", 0, cx - 2)], down_v
    return early, late


def second_lists(cx):
    (up_s, up_v), (down_s, down_v) = up_layers(cx), down_layers(cx)
    up_s, down_s = [("s", *key) for key in up_s], [("s", *key) for key in down_s]
    up = up_s + [("v", *key) for key in up_v]
    return (up, down_s + [("v", *key) for key in down_v]), (up_s, down_s + down_s[-1:])


def thin_counts(lists):
    return [max(NEEDED[upper[0]], NEEDED[lower[0]]) for upper, lower in zip(*lists)]


def send_thin(odd, sec, lists, counts, edge, pay_a, pay_b, at):
    for upper, lower, n in zip(*lists, counts):

        def rows(key):
            whole = edge(*key)
            return jnp.where(sec == 0, whole[:n], whole[SIDE - n :])

        send(odd, rows(upper), rows(lower), pay_a, pay_b, at)
        at += n


def received(odd, lists, counts, pay_a, pay_b, cx, at):
    found = {}
    for upper, lower, n in zip(*lists, counts):
        part = slice(at, at + n)
        at += n
        for kind, c, x, below in ((*upper, True), (*lower, False)):

            def get(part=part, below=below):
                a, b = pay_a[part, :], pay_b[part, :]
                return jnp.where(odd, a, b) if below else jnp.where(odd, b, a)

            found[kind, c, x - cx if below else x + cx] = get
    return found


def put_layer(ref, k, own, thin, sec):
    cy, nz = own.shape
    n = thin.shape[0]
    ref[k, 0:SIDE, :] = jnp.zeros((SIDE, nz), F32)
    ref[k, SIDE : SIDE + cy, :] = own
    ref[k, SIDE + cy :, :] = jnp.zeros((SIDE, nz), F32)
    ref[k, SIDE - n : SIDE, :] = jnp.where(sec == 1, thin, 0.0)
    ref[k, SIDE + cy : SIDE + cy + n, :] = jnp.where(sec == 0, thin, 0.0)


def strains(velocity, halo, x, base, rows, weights):
    fw, bw = weights
    cx = velocity.shape[1]

    def layers(c):
        def get(j):
            if 0 <= j < cx:
                return velocity[c, j, base : base + rows, :]
            return halo(c, j)

        return get

    def beside(c):
        return lambda shift: velocity[c, x, base + shift : base + shift + rows, :]

    vx, vy, vz = (velocity[c, x, base : base + rows, :] for c in range(3))
    return (
        along_x(False, x, layers(0)),
        backward(beside(1), 0),
        backward_z(vz, bw),
        forward(beside(0), 0) + along_x(True, x, layers(1)),
        forward_z(vx, fw) + along_x(True, x, layers(2)),
        forward_z(vy, fw) + forward(beside(2), 0),
    )


def stress_change(lam, mu, parts):
    exx, eyy, ezz, xy, xz, yz = parts
    shear = DT * mu
    volume = (DT * lam) * (exx + eyy + ezz)
    double = 2.0 * shear
    return (
        volume + double * exx,
        volume + double * eyy,
        volume + double * ezz,
        shear * xy,
        shear * xz,
        shear * yz,
    )


def edge_rows(*refs):
    *fields, out = refs
    _, sec, _ = place()
    at = 0
    for field in fields:
        flat = field if len(field.shape) == 4 else None
        for c in range(field.shape[0] if flat is not None else 1):
            layers = field.shape[-3]
            for x in range(layers):
                rows = field[c, x] if flat is not None else field[x]
                out[at : at + SIDE, :] = jnp.where(sec == 0, rows[-SIDE:], rows[:SIDE])
                at += SIDE


def opening(s, v, b, pay_a, pay_b, edges, sems):
    odd, sec, _ = place()
    cx, cy, _ = b.shape
    up, down = first_lists(cx)[0]
    begin = pl.multiple_of(jnp.where(sec == 0, cy - SIDE, 0), SIDE)
    rows = [s.at[c, :, pl.ds(begin, SIDE), :] for c in range(6)]
    rows += [v.at[c, :, pl.ds(begin, SIDE), :] for c in range(3)]
    rows.append(b.at[:, pl.ds(begin, SIDE), :])
    rows = [pltpu.make_async_copy(r, edges.at[k], sems.at[k]) for k, r in enumerate(rows)]

    def run(above, below):
        copies = []
        for pay, layers in ((above, up), (below, down)):
            for k, (kind, c, x) in enumerate(layers):
                source = s.at[c, x] if kind == "s" else b.at[x]
                sem = sems.at[len(rows) + len(copies)]
                copies.append(pltpu.make_async_copy(source, pay.at[pl.ds(k * cy, cy)], sem))
        for copy in copies + rows:
            copy.start()
        for copy in copies:
            copy.wait()

    @pl.when(odd)
    def _():
        run(pay_b, pay_a)

    @pl.when(jnp.logical_not(odd))
    def _():
        run(pay_a, pay_b)

    for copy in rows:
        copy.wait()


def near_columns(state, depth, wet, out):
    _, sec, _ = place()
    rows, own = depth.shape
    for k, field in enumerate((state.at[0], state.at[1], state.at[2], depth, wet)):
        near = jnp.where(sec == 0, field[:, own - 128 :], field[:, :128])
        out[k * rows : (k + 1) * rows, :] = near.astype(F32)


def ocean_field(state, depth, wet, near, f, k):
    rows, own = depth.shape
    if k == own // 128:
        return near[f * rows : (f + 1) * rows, :]
    field = state.at[f] if f < 3 else depth if f == 3 else wet
    return field[:, k * 128 : (k + 1) * 128].astype(F32)


def ocean_edges(state, depth, wet, near, edges):
    rows, own = depth.shape
    at = 0
    for k in range(own // 128 + 1):
        for f, n in enumerate(DEEP):
            field = ocean_field(state, depth, wet, near, f, k)
            edges[0, at : at + n, :] = field[rows - n :]
            edges[1, at : at + n, :] = field[:n]
            at += n


def first_round(s, v, b, strips, pay_a, pay_b, s_pad):
    odd, sec, _ = place()
    _, cx, cy, nz = s.shape
    weights = depth_weights(nz)
    rows = cy + 2 * SIDE
    load_stress(s, strips, s_pad, sec)
    made = {}

    def velocity(c, x):
        if (c, x) not in made:
            old = with_strip(v[c, x], strip(strips, 6 + c, x, cx), sec)
            scale = DT * with_strip(b[x], strip(strips, 9, x, cx), sec)
            made[c, x] = old + scale * force(s_pad, c, x, SIDE, rows, weights)
        return made[c, x]

    def layer(kind, c, x):
        return velocity(c, x)[SIDE : SIDE + cy] if kind == "v" else b[x]

    def edge(kind, c, x):
        if kind == "v":
            return far_strip(velocity(c, x), sec)
        return strip(strips, c if kind == "s" else 9, x, cx)

    early, late = first_lists(cx)
    send_layers(odd, *late, layer, pay_a, pay_b, 0)
    at = len(late[0]) * cy
    for lists in (early, late):
        counts = thin_counts(lists)
        send_thin(odd, sec, lists, counts, edge, pay_a, pay_b, at)
        at += sum(counts)


def first_received(odd, cx, cy, early_a, early_b, late_a, late_b):
    early, late = first_lists(cx)
    own = received(odd, early, [cy] * len(early[0]), early_a, early_b, cx, 0)
    own.update(received(odd, late, [cy] * len(late[0]), late_a, late_b, cx, 0))
    at = len(late[0]) * cy
    rest = received(odd, early, thin_counts(early), late_a, late_b, cx, at)
    at += sum(thin_counts(early))
    rest.update(received(odd, late, thin_counts(late), late_a, late_b, cx, at))
    return own, rest


def whole_step(
    s,
    v,
    b,
    lam,
    mu,
    strips,
    more_strips,
    early_a,
    early_b,
    late_a,
    late_b,
    sea,
    v_out,
    s_out,
    pay_a,
    pay_b,
    b_near,
    s_pad,
    v_pad,
    halo_s,
    halo_v,
    halo_b,
):
    odd, sec, _ = place()
    _, cx, cy, nz = s.shape
    weights = depth_weights(nz)
    rows = cy + 2 * SIDE
    load_stress(s, strips, s_pad, sec)
    index_s, index_v = halo_stress(cx), halo_velocity(cx)
    own, rest = first_received(odd, cx, cy, early_a, early_b, late_a, late_b)
    for key, k in index_s.items():
        put_layer(halo_s, k, own["s", *key](), rest["s", *key](), sec)
    for key, k in index_v.items():
        put_layer(halo_v, k, own["v", *key](), rest["v", *key](), sec)
    index_b = {i: k for k, i in enumerate((-2, -1, cx, cx + 1))}
    for i, k in index_b.items():
        put_layer(halo_b, k, own["b", 0, i](), rest["b", 0, i](), sec)
        b_near[k * cy : (k + 1) * cy, :] = own["b", 0, i]()
    for x in range(cx):
        part = slice(4 * cy + x * SIDE, 4 * cy + (x + 1) * SIDE)
        b_near[part, :] = strip(strips, 9, x, cx)
    nothing = jnp.zeros((SIDE, nz), F32)
    for x in range(cx):
        scale = DT * with_strip(b[x], strip(strips, 9, x, cx), sec)
        for c in range(3):
            old = with_strip(v[c, x], strip(strips, 6 + c, x, cx), sec)
            terms = force(s_pad, c, x, SIDE, rows, weights, lambda k, j: halo_s[index_s[k, j]])
            new = old + scale * terms
            v_out[c, x] = new
            v_pad[c, x, 0:SIDE, :] = nothing
            v_pad[c, x, SIDE : SIDE + rows, :] = new
            v_pad[c, x, SIDE + rows :, :] = nothing
    for (c, i), k in index_v.items():
        halo_v[k] = halo_v[k] + DT * halo_b[index_b[i]] * own_share(s_pad, c, i, SIDE, rows)
    for x in range(cx):
        parts = strains(v_pad, lambda c, j: halo_v[index_v[c, j]], x, SIDE, rows, weights)
        lam_rows = with_strip(lam[x], strip(more_strips, 0, x, cx), sec)
        mu_rows = with_strip(mu[x], strip(more_strips, 1, x, cx), sec)
        for c, change in enumerate(stress_change(lam_rows, mu_rows, parts)):
            s_out[c, x] = s_pad[c, x, SIDE : SIDE + rows, :] + change

    def layer(kind, c, x):
        if kind == "s":
            return s_out[c, x, SIDE : SIDE + cy, :]
        old = v_out[c, x, SIDE : SIDE + cy, :]
        return old + DT * b[x] * force(s_out, c, x, SIDE, cy, weights)

    def edge(_, c, x):
        return jnp.where(sec == 0, s_out[c, x, SIDE + cy :, :], s_out[c, x, 0:SIDE, :])

    layers, edges = second_lists(cx)
    send_layers(odd, *layers, layer, pay_a, pay_b, 0)
    counts = [LAST_NEEDED] * len(edges[0])
    at = LAYERS * cy
    send(odd, sea[0], sea[1], pay_a, pay_b, at)
    send_thin(odd, sec, edges, counts, edge, pay_a, pay_b, at + sea.shape[1])


def last_step(
    sea_rows,
    s,
    v,
    b,
    lam,
    mu,
    b_near,
    from_a,
    from_b,
    v_out,
    s_out,
    done,
    v_rows,
    b_rows,
    halo_s,
    halo_v,
    made,
    sems,
):
    done[...] = jnp.zeros(done.shape, F32)
    odd, sec, _ = place()
    cx, cy, nz = b.shape
    weights = depth_weights(nz)
    half = SIDE // 2
    rows = cy + SIDE
    index_s, index_v = halo_stress(cx), halo_velocity(cx)
    layers, edges = second_lists(cx)
    own = received(odd, layers, [cy] * LAYERS, from_a, from_b, cx, 0)
    counts = [LAST_NEEDED] * len(edges[0])
    rest = received(odd, edges, counts, from_a, from_b, cx, LAYERS * cy + sea_rows)
    for key, k in index_s.items():
        put_layer(halo_s, k, own["s", *key](), rest["s", *key](), sec)
    for x in range(cx):
        part = slice(4 * cy + x * SIDE, 4 * cy + (x + 1) * SIDE)
        b_rows[...] = with_strip(b[x], b_near[part, :], sec)
        scale = DT * b_rows[half : half + rows, :]
        for c in range(3):
            terms = force(
                s, c, x, half, rows, weights, lambda k, j: halo_s[index_s[k, j], half : half + rows, :]
            )
            v_rows[c, x, half : half + rows, :] = v[c, x, half : half + rows, :] + scale * terms
    copies = [pltpu.make_async_copy(v_rows.at[:, :, pl.ds(SIDE, cy), :], v_out, sems.at[cx])]
    copies[0].start()
    for (c, i), k in index_v.items():
        at = (i + 2 if i < 0 else i - cx + 2) * cy
        scale = DT * b_near[at : at + cy, :]
        halo_v[k] = own["v", c, i]() + scale * own_share(s, c, i, SIDE, cy)
    for x in range(cx):
        parts = strains(v_rows, lambda c, j: halo_v[index_v[c, j]], x, SIDE, cy, weights)
        for c, change in enumerate(stress_change(lam[x], mu[x], parts)):
            made[c, x] = s[c, x, SIDE : SIDE + cy, :] + change
        copies.append(pltpu.make_async_copy(made.at[:, x], s_out.at[:, x], sems.at[x]))
        copies[-1].start()
    for copy in copies:
        copy.wait()


def floor_line(left, right):
    rows = left.shape[0]
    row = lax.broadcasted_iota(jnp.int32, (rows, 2 * rows), 0)
    lane = lax.broadcasted_iota(jnp.int32, (rows, 2 * rows), 1)
    picked = jnp.where(lane == row, left[:, 0:1], 0.0)
    picked = jnp.where(lane == row + rows, right[:, 0:1], picked)
    return jnp.sum(picked, axis=0, keepdims=True)


def floor_parts(s, v, b, info, parts):
    cx, cy, nz = b.shape
    weights = depth_weights(nz)
    own = slice(SIDE, SIDE + cy)
    layers = [
        v[2, x, own, :] + DT * b[x] * force(s, 2, x, SIDE, cy, weights) for x in range(cx)
    ]
    lines = [floor_line(layers[x], layers[x + 1]) for x in range(0, cx, 2)]
    last = s[4, cx - 1, own, :]
    lines.append(floor_line(last, last))
    lines.append(floor_line(s[4, cx - 2, own, :], s[4, 0, own, :]))
    lines.append(floor_line(DT * b[0], DT * b[1]))
    lines.append(floor_line(jnp.zeros((cy, nz), F32), (-FAR * DT) * b[cx - 1]))
    lines.append(info[...])
    row = lax.broadcasted_iota(jnp.int32, (SIDE, 2 * cy), 0)
    tiled = jnp.zeros((SIDE, 2 * cy), F32)
    for k, line in enumerate(lines):
        tiled = jnp.where(row == k, line, tiled)
    for k in range(parts.shape[0]):
        parts[k] = tiled


def column(line, first, count):
    wide = jnp.broadcast_to(line, (count, line.shape[1]))
    row = lax.broadcasted_iota(jnp.int32, wide.shape, 0)
    lane = lax.broadcasted_iota(jnp.int32, wide.shape, 1)
    return jnp.sum(jnp.where(lane == row + first, wide, 0.0), axis=1, keepdims=True)


def ocean_steps(
    start, from_a, from_b, near, state, depth, wet_ref, info, patches, _, ocean_out, ocean_ref
):
    odd, sec, tile = place()
    count = lax.axis_size("tile")
    rows, own = depth.shape
    columns = own + 128
    at = start
    for k in range(columns // 128):
        lanes = slice(k * 128, (k + 1) * 128)
        for f, n in enumerate(DEEP):
            here = ocean_field(state, depth, wet_ref, near, f, k)
            a, b = from_a[at : at + n, :], from_b[at : at + n, :]
            low, high = jnp.where(odd, a, b), jnp.where(odd, b, a)
            ocean_ref[f, 0:SIDE, lanes] = jnp.zeros((SIDE, 128), F32)
            ocean_ref[f, SIDE + rows :, lanes] = jnp.zeros((SIDE, 128), F32)
            ocean_ref[f, SIDE - n : SIDE, lanes] = low
            ocean_ref[f, SIDE : SIDE + rows, lanes] = here
            ocean_ref[f, SIDE + rows : SIDE + rows + n, lanes] = high
            at += n

    total = rows + 2 * SIDE
    lane = lax.broadcasted_iota(jnp.int32, (1, columns), 1)
    ahead = jnp.where((lane == own - 1) & (sec == 1), 0.0, 0.5).astype(F32)
    behind = jnp.where((lane == 0) & (sec == 0), 0.0, 0.5).astype(F32)
    line = lax.broadcasted_iota(jnp.int32, (total, 1), 0)
    inside = ((line >= SIDE) | (tile > 0)) & ((line < SIDE + rows) | (tile < count - 1))
    inside = inside.astype(F32)

    def across(f):
        return pltpu.roll(f, columns - 1, 1) * ahead - pltpu.roll(f, 1, 1) * behind

    def down(f):
        return 0.5 * (pltpu.roll(f, total - 1, 0) - pltpu.roll(f, 1, 0))

    eta, u, v_sea = ocean_ref[0], ocean_ref[1], ocean_ref[2]
    depth, wet = ocean_ref[3], ocean_ref[4]
    window = min(WINDOW, count)
    base = jnp.clip(tile - REACH - 1, 0, count - window)
    below = patches[sec * count + jnp.maximum(tile - 1, 0)][6:7]
    above = patches[sec * count + jnp.minimum(tile + 1, count - 1)][6:7]
    line = info[...]
    marks = [
        jnp.concatenate(
            [
                column(below, k * rows + rows - SIDE, SIDE),
                column(line, k * rows, rows),
                column(above, k * rows, SIDE),
            ],
            axis=0,
        )
        for k in range(2)
    ]
    owner = jnp.broadcast_to(marks[0] - base.astype(F32), (total, 128))
    share = marks[1]
    width = own // 4
    left = lax.broadcasted_iota(jnp.int32, (1, 128), 1) < width
    near = jnp.where(left, -NEAR, FAR).astype(F32)
    far = jnp.where(left, FAR, 0.0).astype(F32)
    uplift = []
    for half in (sec, 1 - sec):
        tiles = []
        for k in range(-1, window + 1):
            here = jnp.clip(base + k, 0, count - 1)
            there = (here == base + k).astype(F32)
            tiles.append(patches[half * count + here] * there)
        levels = [jnp.zeros((total, 128), F32) for _ in range(2)]
        for k in range(window):
            below, this, above = tiles[k], tiles[k + 1], tiles[k + 2]
            first = this[0:1] + this[4:5] * (near * below[2:3] + far * below[3:4])
            second = this[1:2] + this[5:6] * above[3:4]
            mine = owner == float(k)
            levels = [jnp.where(mine, q, level) for q, level in zip((first, second), levels)]
        uplift.append(levels)
    uplift = uplift[0] + [jnp.where(sec == 0, uplift[1][0], uplift[1][1])]
    uplift = jnp.concatenate(uplift, axis=1)
    lift = ODT * (share * wet * uplift)
    for _ in range(2):
        u = wet * (u - ODT * down(eta))
        v_sea = wet * (v_sea - ODT * across(eta))
        eta = inside * (eta - ODT * (down(depth * u) + across(depth * v_sea)) + lift)
    part = slice(SIDE, SIDE + rows)
    ocean_out[0] = eta[part, :own]
    ocean_out[1] = u[part, :own]
    ocean_out[2] = v_sea[part, :own]


VMEM = pl.BlockSpec(memory_space=pltpu.VMEM)
ANY = pl.BlockSpec(memory_space=pl.ANY)


def call(body, name, outs, scratch, operands, weight=1, ins=VMEM, where=VMEM, grant=8):
    shapes = [jax.ShapeDtypeStruct(o, F32) for o in outs]
    moved = sum(o.size for o in operands) * 4 + sum(o.size for o in shapes) * 4
    return pl.pallas_call(
        body,
        name=name,
        out_shape=shapes,
        in_specs=ins if isinstance(ins, list) else [ins] * len(operands),
        out_specs=where if isinstance(where, list) else [where] * len(outs),
        scratch_shapes=scratch,
        compiler_params=pltpu.CompilerParams(vmem_limit_bytes=grant * 1024 * 1024),
        cost_estimate=pl.CostEstimate(
            flops=moved * weight, bytes_accessed=moved * weight, transcendentals=0
        ),
    )(*operands)


def exchange(pay_a, pay_b, count):
    def swap(pay, first):
        pairs = []
        for i in range(first, count - 1, 2):
            pairs += [(i, i + 1), (i + 1, i)]
        return lax.ppermute(pay, "tile", pairs)

    from_a = swap(pay_a, 0)
    return from_a, swap(pay_b, 1)


def across(pay):
    return lax.ppermute(pay, "sec", [(0, 1), (1, 0)])


def shards(
    velocity,
    stresses,
    buoyancy,
    lame_first,
    shear_mod,
    ocean_state,
    depth_map,
    wet_mask,
    intersection_src,
    intersection_share,
):
    count = lax.axis_size("tile")
    sec = lax.axis_index("sec")
    _, cx, cy, nz = stresses.shape
    _, rows, columns = ocean_state.shape
    tall = cy + 2 * SIDE
    halo = pltpu.VMEM((LAYERS, tall, nz), F32)

    first = ((LAYERS + 2) // 2 + 1) * cy
    pay_a, pay_b, edges = call(
        opening,
        "opening",
        [(first, nz), (first, nz), (10, cx, SIDE, nz)],
        [pltpu.SemaphoreType.DMA((10 + 2 * (first // cy),))],
        [stresses, velocity, buoyancy],
        ins=ANY,
        grant=60,
    )
    early_a, early_b = exchange(pay_a, pay_b, count)
    strips = across(edges.reshape(10 * cx * SIDE, nz))
    early_list, late_list = first_lists(cx)
    per = (columns // 128 + 1) * PACK
    late = len(late_list[0]) * cy + sum(thin_counts(early_list) + thin_counts(late_list))
    pay_a, pay_b = call(
        first_round,
        "first_round",
        [(late, nz), (late, nz)],
        [pltpu.VMEM((6, cx, tall + 2 * SIDE, nz), F32)],
        [stresses, velocity, buoyancy, strips],
    )
    late_a, late_b = exchange(pay_a, pay_b, count)

    source, share, lame, shear, ocean_state, depth_map, wet_mask, _, _ = lax.optimization_barrier(
        (intersection_src, intersection_share, lame_first, shear_mod)
        + (ocean_state, depth_map, wet_mask, early_a, early_b)
    )
    (edges,) = call(edge_rows, "edge_rows", [(2 * cx * SIDE, nz)], [], [lame, shear])
    more_strips = across(edges)
    sea = [ocean_state, depth_map, wet_mask]
    (near,) = call(near_columns, "near_columns", [(len(DEEP) * rows, 128)], [], sea)
    near = across(near)
    (edges,) = call(ocean_edges, "ocean_edges", [(2, per, 128)], [], sea + [near])
    info = jnp.concatenate([source.astype(F32), share])[None]

    second = (LAYERS * cy + per + 5 * LAST_NEEDED, nz)
    velocity, stresses, pay_a, pay_b, b_near = call(
        whole_step,
        "whole_step",
        [(3, cx, tall, nz), (6, cx, tall, nz), second, second]
        + [(4 * cy + cx * SIDE, nz)],
        [
            pltpu.VMEM((6, cx, tall + 2 * SIDE, nz), F32),
            pltpu.VMEM((3, cx, tall + 2 * SIDE, nz), F32),
            halo,
            halo,
            pltpu.VMEM((4, tall, nz), F32),
        ],
        [stresses, velocity, buoyancy, lame_first, shear_mod, strips, more_strips]
        + [early_a, early_b, late_a, late_b, edges],
    )
    from_a, from_b = exchange(pay_a, pay_b, count)
    (parts,) = call(
        floor_parts,
        "floor_parts",
        [(2 * count, SIDE, 2 * cy)],
        [],
        [stresses, velocity, buoyancy, info],
    )
    patches = lax.all_to_all(parts, ("sec", "tile"), 0, 0)
    velocity, stresses, done = call(
        functools.partial(last_step, per),
        "last_step",
        [(3, cx, cy, nz), (6, cx, cy, nz), (8, 128)],
        [
            pltpu.VMEM((3, cx, tall, nz), F32),
            pltpu.VMEM((tall, nz), F32),
            halo,
            pltpu.VMEM((LAYERS, cy, nz), F32),
            pltpu.VMEM((6, cx, cy, nz), F32),
            pltpu.SemaphoreType.DMA((cx + 1,)),
        ],
        [stresses, velocity, buoyancy, lame_first, shear_mod, b_near]
        + [from_a, from_b],
        where=[ANY, ANY, VMEM],
    )
    (ocean_state,) = call(
        functools.partial(ocean_steps, LAYERS * cy),
        "ocean_steps",
        [ocean_state.shape],
        [pltpu.VMEM((len(DEEP), rows + 2 * SIDE, columns + 128), F32)],
        [from_a, from_b, near] + sea + [info, patches, done],
    )
    return velocity, stresses, ocean_state


def solution(mesh):
    cube = P("tile", "sec", None)
    return jax.shard_map(
        shards,
        mesh=mesh,
        in_specs=(
            P(None, "tile", "sec", None),
            P(None, "tile", "sec", None),
            cube,
            cube,
            cube,
            P(None, "tile", "sec"),
            P("tile", "sec"),
            P("tile", "sec"),
            P("tile"),
            P("tile"),
        ),
        out_specs=(
            P(None, "tile", "sec", None),
            P(None, "tile", "sec", None),
            P(None, "tile", "sec"),
        ),
        check_vma=False,
    )
```

```python
import functools

import jax
import jax.numpy as jnp
from jax import lax
from jax.experimental import pallas as pl
from jax.experimental.pallas import tpu as pltpu
from jax.sharding import PartitionSpec as P

REACH = 2
NEAR = 9.0 / 8.0
FAR = 1.0 / 24.0
DT = 0.15
ODT = 0.3
F32 = jnp.float32
SIDE = 8
WINDOW = 8
DEEP = (4, 3, 2, 3, 3)
CORNER = (2, 1, 2, 2, 2)
LINES = 6
NEEDED = {"s": 5, "v": 3, "b": 3}
LAST_NEEDED = 2
LAYERS = 9
STRESS_X = ((0, True), (3, False), (4, False))


def depth_weights(width):
    lane = lax.broadcasted_iota(jnp.int32, (1, width), 1)

    def weight(value, first, last):
        return jnp.where((lane >= first) & (lane < last), value, 0.0).astype(F32)

    forward = (weight(NEAR, 0, width - 1), weight(-FAR, 0, width - 2), weight(FAR, 1, width))
    backward = (weight(-NEAR, 1, width), weight(-FAR, 0, width - 1), weight(FAR, 2, width))
    return forward, backward


def forward_z(f, weights):
    near, far, behind = weights
    n = f.shape[-1]
    return (
        pltpu.roll(f, n - 1, 1) * near
        - NEAR * f
        + pltpu.roll(f, n - 2, 1) * far
        + pltpu.roll(f, 1, 1) * behind
    )


def backward_z(f, weights):
    near, far, behind = weights
    n = f.shape[-1]
    return (
        NEAR * f
        + pltpu.roll(f, 1, 1) * near
        + pltpu.roll(f, n - 1, 1) * far
        + pltpu.roll(f, 2, 1) * behind
    )


def forward(at, i):
    return NEAR * (at(i + 1) - at(i)) - FAR * (at(i + 2) - at(i - 1))


def backward(at, i):
    return NEAR * (at(i) - at(i - 1)) - FAR * (at(i + 1) - at(i - 2))


def place():
    tile, sec = lax.axis_index("tile"), lax.axis_index("sec")
    return lax.rem(tile, 2) == 1, sec, tile


def along_x(ahead, i, get):
    if ahead:
        taps = ((i + 1, NEAR), (i, -NEAR), (i + 2, -FAR), (i - 1, FAR))
    else:
        taps = ((i, NEAR), (i - 1, -NEAR), (i + 1, -FAR), (i - 2, FAR))
    total = None
    for j, weight in taps:
        layer = get(j)
        if layer is not None:
            total = weight * layer if total is None else total + weight * layer
    return total


def up_layers(cx):
    stress = [(0, cx - 1), (3, cx - 2), (3, cx - 1), (4, cx - 2), (4, cx - 1)]
    return stress, [(0, cx - 2), (0, cx - 1), (1, cx - 1), (2, cx - 1)]


def down_layers(cx):
    return [(0, 0), (0, 1), (3, 0), (4, 0)], [(0, 0), (1, 0), (1, 1), (2, 0), (2, 1)]


def halo_stress(cx):
    low = [(c, x - cx) for c, x in up_layers(cx)[0]]
    return {key: k for k, key in enumerate(low + [(c, x + cx) for c, x in down_layers(cx)[0]])}


def halo_velocity(cx):
    low = [(c, x - cx) for c, x in up_layers(cx)[1]]
    return {key: k for k, key in enumerate(low + [(c, x + cx) for c, x in down_layers(cx)[1]])}


def strip(ref, k, x, cx):
    return ref[(k * cx + x) * SIDE : (k * cx + x + 1) * SIDE, :]


def with_strip(own, edge, sec):
    return jnp.concatenate(
        [jnp.where(sec == 1, edge, 0.0), own, jnp.where(sec == 0, edge, 0.0)], axis=0
    )


def yz_terms(s, comp, x, base, rows, weights):
    fw, bw = weights
    here = slice(base, base + rows)

    def beside(c):
        return lambda shift: s[c, x, base + shift : base + shift + rows, :]

    if comp == 0:
        return backward(beside(3), 0) + backward_z(s[4, x, here, :], bw)
    if comp == 1:
        return forward(beside(1), 0) + backward_z(s[5, x, here, :], bw)
    return backward(beside(5), 0) + forward_z(s[2, x, here, :], fw)


def force(s, comp, x, base, rows, weights, halo=None):
    source, ahead = STRESS_X[comp]
    cx = s.shape[1]

    def get(j):
        if 0 <= j < cx:
            return s[source, j, base : base + rows, :]
        return None if halo is None else halo(source, j)

    return along_x(ahead, x, get) + yz_terms(s, comp, x, base, rows, weights)


def halo_share(comp, x, cx, halo):
    source, ahead = STRESS_X[comp]
    return along_x(ahead, x, lambda j: None if 0 <= j < cx else halo(source, j))


def own_share(s, comp, i, base, rows):
    source, ahead = STRESS_X[comp]
    cx = s.shape[1]
    return along_x(
        ahead, i, lambda j: s[source, j, base : base + rows, :] if 0 <= j < cx else None
    )


def load_stress(s, strips, s_pad, sec):
    comps, cx, cy, nz = s.shape
    nothing = jnp.zeros((SIDE, nz), F32)
    for c in range(comps):
        for x in range(cx):
            s_pad[c, x, 0:SIDE, :] = nothing
            s_pad[c, x, SIDE : 3 * SIDE + cy, :] = with_strip(s[c, x], strip(strips, c, x, cx), sec)
            s_pad[c, x, 3 * SIDE + cy :, :] = nothing


def send(odd, upper, lower, pay_a, pay_b, at):
    part = slice(at, at + upper.shape[0])
    pay_a[part, :] = jnp.where(odd, lower, upper)
    pay_b[part, :] = jnp.where(odd, upper, lower)


def send_layers(odd, up, down, layer, pay_a, pay_b, at):
    for k, (upper, lower) in enumerate(zip(up, down)):
        rows = layer(*upper)
        send(odd, rows, layer(*lower), pay_a, pay_b, at)
        at += rows.shape[0]


def first_lists(cx):
    (up_s, up_v), (down_s, down_v) = up_layers(cx), down_layers(cx)
    up_s, down_s = [("s", *key) for key in up_s], [("s", *key) for key in down_s]
    up_v, down_v = [("v", *key) for key in up_v], [("v", *key) for key in down_v]
    early = up_s + [("b", 0, cx - 1)], down_s + [("b", 0, 0), ("b", 0, 1)]
    late = up_v + [("b", 0, cx - 2)], down_v
    return early, late


def second_lists(cx):
    (up_s, up_v), (down_s, down_v) = up_layers(cx), down_layers(cx)
    up_s, down_s = [("s", *key) for key in up_s], [("s", *key) for key in down_s]
    up = up_s + [("v", *key) for key in up_v]
    return (up, down_s + [("v", *key) for key in down_v]), (up_s, down_s + down_s[-1:])


def thin_counts(lists):
    return [max(NEEDED[upper[0]], NEEDED[lower[0]]) for upper, lower in zip(*lists)]


def send_thin(odd, sec, lists, counts, edge, pay_a, pay_b, at):
    for upper, lower, n in zip(*lists, counts):

        def rows(key):
            whole = edge(*key)
            return jnp.where(sec == 0, whole[:n], whole[SIDE - n :])

        send(odd, rows(upper), rows(lower), pay_a, pay_b, at)
        at += n


def received(odd, lists, counts, pay_a, pay_b, cx, at):
    found = {}
    for upper, lower, n in zip(*lists, counts):
        part = slice(at, at + n)
        at += n
        for kind, c, x, below in ((*upper, True), (*lower, False)):

            def get(part=part, below=below):
                a, b = pay_a[part, :], pay_b[part, :]
                return jnp.where(odd, a, b) if below else jnp.where(odd, b, a)

            found[kind, c, x - cx if below else x + cx] = get
    return found


def put_layer(ref, k, own, thin, sec):
    cy, nz = own.shape
    n = thin.shape[0]
    ref[k, 0:SIDE, :] = jnp.zeros((SIDE, nz), F32)
    ref[k, SIDE : SIDE + cy, :] = own
    ref[k, SIDE + cy :, :] = jnp.zeros((SIDE, nz), F32)
    ref[k, SIDE - n : SIDE, :] = jnp.where(sec == 1, thin, 0.0)
    ref[k, SIDE + cy : SIDE + cy + n, :] = jnp.where(sec == 0, thin, 0.0)


def strains(velocity, halo, x, base, rows, weights):
    fw, bw = weights
    cx = velocity.shape[1]

    def layers(c):
        def get(j):
            if 0 <= j < cx:
                return velocity[c, j, base : base + rows, :]
            return halo(c, j)

        return get

    def beside(c):
        return lambda shift: velocity[c, x, base + shift : base + shift + rows, :]

    vx, vy, vz = (velocity[c, x, base : base + rows, :] for c in range(3))
    return (
        along_x(False, x, layers(0)),
        backward(beside(1), 0),
        backward_z(vz, bw),
        forward(beside(0), 0) + along_x(True, x, layers(1)),
        forward_z(vx, fw) + along_x(True, x, layers(2)),
        forward_z(vy, fw) + forward(beside(2), 0),
    )


def stress_change(lam, mu, parts):
    exx, eyy, ezz, xy, xz, yz = parts
    shear = DT * mu
    volume = (DT * lam) * (exx + eyy + ezz)
    double = 2.0 * shear
    return (
        volume + double * exx,
        volume + double * eyy,
        volume + double * ezz,
        shear * xy,
        shear * xz,
        shear * yz,
    )


def edge_rows(*refs):
    *fields, out = refs
    _, sec, _ = place()
    at = 0
    for field in fields:
        flat = field if len(field.shape) == 4 else None
        for c in range(field.shape[0] if flat is not None else 1):
            layers = field.shape[-3]
            for x in range(layers):
                rows = field[c, x] if flat is not None else field[x]
                out[at : at + SIDE, :] = jnp.where(sec == 0, rows[-SIDE:], rows[:SIDE])
                at += SIDE


def opening(s, v, b, pay_a, pay_b, edges, sems):
    odd, sec, _ = place()
    cx, cy, _ = b.shape
    up, down = first_lists(cx)[0]
    begin = pl.multiple_of(jnp.where(sec == 0, cy - SIDE, 0), SIDE)
    rows = [s.at[c, :, pl.ds(begin, SIDE), :] for c in range(6)]
    rows += [v.at[c, :, pl.ds(begin, SIDE), :] for c in range(3)]
    rows.append(b.at[:, pl.ds(begin, SIDE), :])
    rows = [pltpu.make_async_copy(r, edges.at[k], sems.at[k]) for k, r in enumerate(rows)]

    def run(above, below):
        copies = []
        for pay, layers in ((above, up), (below, down)):
            for k, (kind, c, x) in enumerate(layers):
                source = s.at[c, x] if kind == "s" else b.at[x]
                sem = sems.at[len(rows) + len(copies)]
                copies.append(pltpu.make_async_copy(source, pay.at[pl.ds(k * cy, cy)], sem))
        for copy in copies + rows:
            copy.start()
        for copy in copies:
            copy.wait()

    @pl.when(odd)
    def _():
        run(pay_b, pay_a)

    @pl.when(jnp.logical_not(odd))
    def _():
        run(pay_a, pay_b)

    for copy in rows:
        copy.wait()


def near_columns(state, depth, wet, out):
    _, sec, _ = place()
    rows, own = depth.shape
    for k, field in enumerate((state.at[0], state.at[1], state.at[2], depth, wet)):
        near = jnp.where(sec == 0, field[:, own - 128 :], field[:, :128])
        out[k * rows : (k + 1) * rows, :] = near.astype(F32)


def ocean_field(state, depth, wet, near, f, k):
    rows, own = depth.shape
    if k == own // 128:
        return near[f * rows : (f + 1) * rows, :]
    field = state.at[f] if f < 3 else depth if f == 3 else wet
    return field[:, k * 128 : (k + 1) * 128].astype(F32)


def ocean_edges(state, depth, wet, near, edges):
    rows, own = depth.shape
    at = 0
    for k in range(own // 128 + 1):
        for f, n in enumerate(DEEP if k < own // 128 else CORNER):
            field = ocean_field(state, depth, wet, near, f, k)
            edges[0, at : at + n, :] = field[rows - n :]
            edges[1, at : at + n, :] = field[:n]
            at += n


def first_round(s, v, b, strips, pay_a, pay_b, s_pad, v_part):
    odd, sec, _ = place()
    _, cx, cy, nz = s.shape
    weights = depth_weights(nz)
    rows = cy + 2 * SIDE
    load_stress(s, strips, s_pad, sec)
    for x in range(cx):
        scale = DT * with_strip(b[x], strip(strips, 9, x, cx), sec)
        for c in range(3):
            old = with_strip(v[c, x], strip(strips, 6 + c, x, cx), sec)
            v_part[c, x] = old + scale * force(s_pad, c, x, SIDE, rows, weights)

    def layer(kind, c, x):
        return v_part[c, x, SIDE : SIDE + cy, :] if kind == "v" else b[x]

    def edge(kind, c, x):
        if kind == "v":
            return jnp.where(sec == 0, v_part[c, x, SIDE + cy :, :], v_part[c, x, 0:SIDE, :])
        return strip(strips, c if kind == "s" else 9, x, cx)

    early, late = first_lists(cx)
    send_layers(odd, *late, layer, pay_a, pay_b, 0)
    at = len(late[0]) * cy
    for lists in (early, late):
        counts = thin_counts(lists)
        send_thin(odd, sec, lists, counts, edge, pay_a, pay_b, at)
        at += sum(counts)


def first_received(odd, cx, cy, early_a, early_b, late_a, late_b):
    early, late = first_lists(cx)
    own = received(odd, early, [cy] * len(early[0]), early_a, early_b, cx, 0)
    own.update(received(odd, late, [cy] * len(late[0]), late_a, late_b, cx, 0))
    at = len(late[0]) * cy
    rest = received(odd, early, thin_counts(early), late_a, late_b, cx, at)
    at += sum(thin_counts(early))
    rest.update(received(odd, late, thin_counts(late), late_a, late_b, cx, at))
    return own, rest


def whole_step(
    s_pad,
    v_part,
    b,
    lam,
    mu,
    strips,
    more_strips,
    early_a,
    early_b,
    late_a,
    late_b,
    sea,
    v_out,
    s_out,
    pay_a,
    pay_b,
    b_near,
    v_pad,
    halo_s,
    halo_v,
    halo_b,
):
    odd, sec, _ = place()
    cx, cy, nz = b.shape
    weights = depth_weights(nz)
    rows = cy + 2 * SIDE
    index_s, index_v = halo_stress(cx), halo_velocity(cx)
    own, rest = first_received(odd, cx, cy, early_a, early_b, late_a, late_b)
    for key, k in index_s.items():
        put_layer(halo_s, k, own["s", *key](), rest["s", *key](), sec)
    for key, k in index_v.items():
        put_layer(halo_v, k, own["v", *key](), rest["v", *key](), sec)
    index_b = {i: k for k, i in enumerate((-2, -1, cx, cx + 1))}
    for i, k in index_b.items():
        put_layer(halo_b, k, own["b", 0, i](), rest["b", 0, i](), sec)
        b_near[k * cy : (k + 1) * cy, :] = own["b", 0, i]()
    for x in range(cx):
        part = slice(4 * cy + x * SIDE, 4 * cy + (x + 1) * SIDE)
        b_near[part, :] = strip(strips, 9, x, cx)
    nothing = jnp.zeros((SIDE, nz), F32)
    for x in range(cx):
        scale = DT * with_strip(b[x], strip(strips, 9, x, cx), sec)
        for c in range(3):
            new = v_part[c, x]
            terms = halo_share(c, x, cx, lambda k, j: halo_s[index_s[k, j]])
            if terms is not None:
                new = new + scale * terms
            v_out[c, x] = new
            v_pad[c, x, 0:SIDE, :] = nothing
            v_pad[c, x, SIDE : SIDE + rows, :] = new
            v_pad[c, x, SIDE + rows :, :] = nothing
    for (c, i), k in index_v.items():
        halo_v[k] = halo_v[k] + DT * halo_b[index_b[i]] * own_share(s_pad, c, i, SIDE, rows)
    for x in range(cx):
        parts = strains(v_pad, lambda c, j: halo_v[index_v[c, j]], x, SIDE, rows, weights)
        lam_rows = with_strip(lam[x], strip(more_strips, 0, x, cx), sec)
        mu_rows = with_strip(mu[x], strip(more_strips, 1, x, cx), sec)
        for c, change in enumerate(stress_change(lam_rows, mu_rows, parts)):
            s_out[c, x] = s_pad[c, x, SIDE : SIDE + rows, :] + change

    def layer(kind, c, x):
        if kind == "s":
            return s_out[c, x, SIDE : SIDE + cy, :]
        old = v_out[c, x, SIDE : SIDE + cy, :]
        return old + DT * b[x] * force(s_out, c, x, SIDE, cy, weights)

    def edge(_, c, x):
        return jnp.where(sec == 0, s_out[c, x, SIDE + cy :, :], s_out[c, x, 0:SIDE, :])

    layers, edges = second_lists(cx)
    send_layers(odd, *layers, layer, pay_a, pay_b, 0)
    counts = [LAST_NEEDED] * len(edges[0])
    at = LAYERS * cy
    send(odd, sea[0], sea[1], pay_a, pay_b, at)
    send_thin(odd, sec, edges, counts, edge, pay_a, pay_b, at + sea.shape[1])


def last_step(
    sea_rows,
    s,
    v,
    b,
    lam,
    mu,
    b_near,
    from_a,
    from_b,
    v_out,
    s_out,
    done,
    v_rows,
    b_rows,
    halo_s,
    halo_v,
    made,
    sems,
):
    done[...] = jnp.zeros(done.shape, F32)
    odd, sec, _ = place()
    cx, cy, nz = b.shape
    weights = depth_weights(nz)
    half = SIDE // 2
    rows = cy + SIDE
    index_s, index_v = halo_stress(cx), halo_velocity(cx)
    layers, edges = second_lists(cx)
    own = received(odd, layers, [cy] * LAYERS, from_a, from_b, cx, 0)
    counts = [LAST_NEEDED] * len(edges[0])
    rest = received(odd, edges, counts, from_a, from_b, cx, LAYERS * cy + sea_rows)
    for key, k in index_s.items():
        put_layer(halo_s, k, own["s", *key](), rest["s", *key](), sec)
    for x in range(cx):
        part = slice(4 * cy + x * SIDE, 4 * cy + (x + 1) * SIDE)
        b_rows[...] = with_strip(b[x], b_near[part, :], sec)
        scale = DT * b_rows[half : half + rows, :]
        for c in range(3):
            terms = force(
                s, c, x, half, rows, weights, lambda k, j: halo_s[index_s[k, j], half : half + rows, :]
            )
            v_rows[c, x, half : half + rows, :] = v[c, x, half : half + rows, :] + scale * terms
    copies = [pltpu.make_async_copy(v_rows.at[:, :, pl.ds(SIDE, cy), :], v_out, sems.at[cx])]
    copies[0].start()
    for (c, i), k in index_v.items():
        at = (i + 2 if i < 0 else i - cx + 2) * cy
        scale = DT * b_near[at : at + cy, :]
        halo_v[k] = own["v", c, i]() + scale * own_share(s, c, i, SIDE, cy)
    for x in range(cx):
        parts = strains(v_rows, lambda c, j: halo_v[index_v[c, j]], x, SIDE, cy, weights)
        for c, change in enumerate(stress_change(lam[x], mu[x], parts)):
            made[c, x] = s[c, x, SIDE : SIDE + cy, :] + change
        copies.append(pltpu.make_async_copy(made.at[:, x], s_out.at[:, x], sems.at[x]))
        copies[-1].start()
    for copy in copies:
        copy.wait()


def floor_line(left, right):
    rows = left.shape[0]
    row = lax.broadcasted_iota(jnp.int32, (rows, 2 * rows), 0)
    lane = lax.broadcasted_iota(jnp.int32, (rows, 2 * rows), 1)
    picked = jnp.where(lane == row, left[:, 0:1], 0.0)
    picked = jnp.where(lane == row + rows, right[:, 0:1], picked)
    return jnp.sum(picked, axis=0, keepdims=True)


def floor_parts(s, v, b, info, parts):
    cx, cy, nz = b.shape
    weights = depth_weights(nz)
    own = slice(SIDE, SIDE + cy)
    layers = [
        v[2, x, own, :] + DT * b[x] * force(s, 2, x, SIDE, cy, weights) for x in range(cx)
    ]
    lines = [floor_line(layers[x], layers[x + 1]) for x in range(0, cx, 2)]
    lines.append(floor_line(s[4, cx - 1, own, :], s[4, cx - 2, own, :]))
    lines.append(floor_line(s[4, 0, own, :], (-FAR * DT) * b[cx - 1]))
    lines.append(floor_line(DT * b[0], DT * b[1]))
    lines.append(info[...])
    row = lax.broadcasted_iota(jnp.int32, (SIDE, 2 * cy), 0)
    period = 3 * SIDE
    for k in range(0, period, SIDE):
        tiled = jnp.zeros((SIDE, 2 * cy), F32)
        for j in range(SIDE):
            tiled = jnp.where(row == j, lines[(k + j) % LINES], tiled)
        for at in range(k, parts.shape[0], period):
            parts[at : at + SIDE, :] = tiled


def column(line, first, count):
    wide = jnp.broadcast_to(line, (count, line.shape[1]))
    row = lax.broadcasted_iota(jnp.int32, wide.shape, 0)
    lane = lax.broadcasted_iota(jnp.int32, wide.shape, 1)
    return jnp.sum(jnp.where(lane == row + first, wide, 0.0), axis=1, keepdims=True)


def ocean_steps(
    start, from_a, from_b, near, state, depth, wet_ref, info, patches, _, ocean_out, ocean_ref
):
    odd, sec, tile = place()
    count = lax.axis_size("tile")
    rows, own = depth.shape
    columns = own + 128
    at = start
    for k in range(columns // 128):
        lanes = slice(k * 128, (k + 1) * 128)
        for f, n in enumerate(DEEP if k < own // 128 else CORNER):
            here = ocean_field(state, depth, wet_ref, near, f, k)
            a, b = from_a[at : at + n, :], from_b[at : at + n, :]
            low, high = jnp.where(odd, a, b), jnp.where(odd, b, a)
            ocean_ref[f, 0:SIDE, lanes] = jnp.zeros((SIDE, 128), F32)
            ocean_ref[f, SIDE + rows :, lanes] = jnp.zeros((SIDE, 128), F32)
            ocean_ref[f, SIDE - n : SIDE, lanes] = low
            ocean_ref[f, SIDE : SIDE + rows, lanes] = here
            ocean_ref[f, SIDE + rows : SIDE + rows + n, lanes] = high
            at += n

    total = rows + 2 * SIDE
    lane = lax.broadcasted_iota(jnp.int32, (1, columns), 1)
    ahead = jnp.where((lane == own - 1) & (sec == 1), 0.0, 0.5).astype(F32)
    behind = jnp.where((lane == 0) & (sec == 0), 0.0, 0.5).astype(F32)
    line = lax.broadcasted_iota(jnp.int32, (total, 1), 0)
    inside = ((line >= SIDE) | (tile > 0)) & ((line < SIDE + rows) | (tile < count - 1))
    inside = inside.astype(F32)

    def across(f):
        return pltpu.roll(f, columns - 1, 1) * ahead - pltpu.roll(f, 1, 1) * behind

    def down(f):
        return 0.5 * (pltpu.roll(f, total - 1, 0) - pltpu.roll(f, 1, 0))

    eta, u, v_sea = ocean_ref[0], ocean_ref[1], ocean_ref[2]
    depth, wet = ocean_ref[3], ocean_ref[4]
    window = min(WINDOW, count)
    base = jnp.clip(tile - REACH - 1, 0, count - window)

    def told(half, k):
        return patches[pl.ds((half * count + k) * LINES, LINES), :]

    below = told(sec, jnp.maximum(tile - 1, 0))[5:6]
    above = told(sec, jnp.minimum(tile + 1, count - 1))[5:6]
    line = info[...]
    marks = [
        jnp.concatenate(
            [
                column(below, k * rows + rows - SIDE, SIDE),
                column(line, k * rows, rows),
                column(above, k * rows, SIDE),
            ],
            axis=0,
        )
        for k in range(2)
    ]
    owner = jnp.broadcast_to(marks[0] - base.astype(F32), (total, 128))
    share = marks[1]
    width = own // 4
    left = lax.broadcasted_iota(jnp.int32, (1, 128), 1) < width
    near = jnp.where(left, -NEAR, FAR).astype(F32)
    far = jnp.where(left, FAR, 0.0).astype(F32)
    uplift = []
    for half in (sec, 1 - sec):
        tiles = []
        for k in range(-1, window + 1):
            here = jnp.clip(base + k, 0, count - 1)
            there = (here == base + k).astype(F32)
            tiles.append(told(half, here) * there)
        levels = [jnp.zeros((total, 128), F32) for _ in range(2)]
        for k in range(window):
            below, this, above = tiles[k], tiles[k + 1], tiles[k + 2]
            last = pltpu.roll(below[2:3], width, 1)
            last = near * jnp.where(left, below[2:3], last) + far * last
            first = this[0:1] + this[4:5] * last
            second = this[1:2] + jnp.where(left, 0.0, this[3:4]) * pltpu.roll(above[3:4], width, 1)
            mine = owner == float(k)
            levels = [jnp.where(mine, q, level) for q, level in zip((first, second), levels)]
        uplift.append(levels)
    uplift = uplift[0] + [jnp.where(sec == 0, uplift[1][0], uplift[1][1])]
    uplift = jnp.concatenate(uplift, axis=1)
    lift = ODT * (share * wet * uplift)
    for _ in range(2):
        u = wet * (u - ODT * down(eta))
        v_sea = wet * (v_sea - ODT * across(eta))
        eta = inside * (eta - ODT * (down(depth * u) + across(depth * v_sea)) + lift)
    part = slice(SIDE, SIDE + rows)
    ocean_out[0] = eta[part, :own]
    ocean_out[1] = u[part, :own]
    ocean_out[2] = v_sea[part, :own]


VMEM = pl.BlockSpec(memory_space=pltpu.VMEM)
ANY = pl.BlockSpec(memory_space=pl.ANY)


def call(body, name, outs, scratch, operands, weight=1, ins=VMEM, where=VMEM, grant=8):
    shapes = [jax.ShapeDtypeStruct(o, F32) for o in outs]
    moved = sum(o.size for o in operands) * 4 + sum(o.size for o in shapes) * 4
    return pl.pallas_call(
        body,
        name=name,
        out_shape=shapes,
        in_specs=ins if isinstance(ins, list) else [ins] * len(operands),
        out_specs=where if isinstance(where, list) else [where] * len(outs),
        scratch_shapes=scratch,
        compiler_params=pltpu.CompilerParams(vmem_limit_bytes=int(grant * 1024 * 1024)),
        cost_estimate=pl.CostEstimate(
            flops=moved * weight, bytes_accessed=moved * weight, transcendentals=0
        ),
    )(*operands)


def exchange(pay_a, pay_b, count):
    def swap(pay, first):
        pairs = []
        for i in range(first, count - 1, 2):
            pairs += [(i, i + 1), (i + 1, i)]
        return lax.ppermute(pay, "tile", pairs)

    from_a = swap(pay_a, 0)
    return from_a, swap(pay_b, 1)


def across(pay):
    return lax.ppermute(pay, "sec", [(0, 1), (1, 0)])


def shards(
    velocity,
    stresses,
    buoyancy,
    lame_first,
    shear_mod,
    ocean_state,
    depth_map,
    wet_mask,
    intersection_src,
    intersection_share,
):
    count = lax.axis_size("tile")
    sec = lax.axis_index("sec")
    _, cx, cy, nz = stresses.shape
    _, rows, columns = ocean_state.shape
    tall = cy + 2 * SIDE
    halo = pltpu.VMEM((LAYERS, tall, nz), F32)

    first = ((LAYERS + 2) // 2 + 1) * cy
    pay_a, pay_b, edges = call(
        opening,
        "opening",
        [(first, nz), (first, nz), (10, cx, SIDE, nz)],
        [pltpu.SemaphoreType.DMA((10 + 2 * (first // cy),))],
        [stresses, velocity, buoyancy],
        ins=ANY,
        grant=60,
    )
    strips = across(edges.reshape(10 * cx * SIDE, nz))
    early_a, early_b = exchange(pay_a, pay_b, count)
    early_list, late_list = first_lists(cx)
    per = columns // 128 * sum(DEEP) + sum(CORNER)
    late = len(late_list[0]) * cy + sum(thin_counts(early_list) + thin_counts(late_list))
    pay_a, pay_b, stresses, velocity = call(
        first_round,
        "first_round",
        [(late, nz), (late, nz), (6, cx, tall + 2 * SIDE, nz), (3, cx, tall, nz)],
        [],
        [stresses, velocity, buoyancy, strips],
    )
    late_a, late_b = exchange(pay_a, pay_b, count)

    source, share, lame, shear, _ = lax.optimization_barrier(
        (intersection_src, intersection_share, lame_first, shear_mod, early_b)
    )
    ocean_state, depth_map, wet_mask, _ = lax.optimization_barrier(
        (ocean_state, depth_map, wet_mask, early_a)
    )
    (edges,) = call(edge_rows, "edge_rows", [(2 * cx * SIDE, nz)], [], [lame, shear])
    more_strips = across(edges)
    sea = [ocean_state, depth_map, wet_mask]
    (near,) = call(near_columns, "near_columns", [(len(DEEP) * rows, 128)], [], sea)
    near = across(near)
    (edges,) = call(ocean_edges, "ocean_edges", [(2, per, 128)], [], sea + [near])
    info = jnp.concatenate([source.astype(F32), share])[None]

    second = (LAYERS * cy + per + 5 * LAST_NEEDED, nz)
    velocity, stresses, pay_a, pay_b, b_near = call(
        whole_step,
        "whole_step",
        [(3, cx, tall, nz), (6, cx, tall, nz), second, second]
        + [(4 * cy + cx * SIDE, nz)],
        [
            pltpu.VMEM((3, cx, tall + 2 * SIDE, nz), F32),
            halo,
            halo,
            pltpu.VMEM((4, tall, nz), F32),
        ],
        [stresses, velocity, buoyancy, lame_first, shear_mod, strips, more_strips]
        + [early_a, early_b, late_a, late_b, edges],
    )
    from_a, from_b = exchange(pay_a, pay_b, count)
    (parts,) = call(
        floor_parts,
        "floor_parts",
        [(2 * count * LINES, 2 * cy)],
        [],
        [stresses, velocity, buoyancy, info],
    )
    parts = parts.reshape(2 * count * LINES // 2, 2, 2 * cy)
    patches = lax.all_to_all(parts, ("sec", "tile"), 0, 0, tiled=True).reshape(-1, 2 * cy)
    velocity, stresses, done = call(
        functools.partial(last_step, per),
        "last_step",
        [(3, cx, cy, nz), (6, cx, cy, nz), (8, 128)],
        [
            pltpu.VMEM((3, cx, tall, nz), F32),
            pltpu.VMEM((tall, nz), F32),
            halo,
            pltpu.VMEM((LAYERS, cy, nz), F32),
            pltpu.VMEM((6, cx, cy, nz), F32),
            pltpu.SemaphoreType.DMA((cx + 1,)),
        ],
        [stresses, velocity, buoyancy, lame_first, shear_mod, b_near]
        + [from_a, from_b],
        where=[ANY, ANY, VMEM],
    )
    (ocean_state,) = call(
        functools.partial(ocean_steps, LAYERS * cy),
        "ocean_steps",
        [ocean_state.shape],
        [pltpu.VMEM((len(DEEP), rows + 2 * SIDE, columns + 128), F32)],
        [from_a, from_b, near] + sea + [info, patches, done],
    )
    return velocity, stresses, ocean_state


def solution(mesh):
    cube = P("tile", "sec", None)
    return jax.shard_map(
        shards,
        mesh=mesh,
        in_specs=(
            P(None, "tile", "sec", None),
            P(None, "tile", "sec", None),
            cube,
            cube,
            cube,
            P(None, "tile", "sec"),
            P("tile", "sec"),
            P("tile", "sec"),
            P("tile"),
            P("tile"),
        ),
        out_specs=(
            P(None, "tile", "sec", None),
            P(None, "tile", "sec", None),
            P(None, "tile", "sec"),
        ),
        check_vma=False,
    )
```

```python
import functools

import jax
import jax.numpy as jnp
from jax import lax
from jax.experimental import pallas as pl
from jax.experimental.pallas import tpu as pltpu
from jax.sharding import PartitionSpec as P

REACH = 2
NEAR = 9.0 / 8.0
FAR = 1.0 / 24.0
DT = 0.15
ODT = 0.3
F32 = jnp.float32
EDGE = 4
SIDE = 8
WINDOW = 8
DEEP = (4, 3, 2, 3, 3)
CORNER = (2, 1, 2, 2, 2)
LINES = 6
NEEDED = {"s": 5, "v": 3, "b": 3}
LAST_NEEDED = 2
LAYERS = 9
STRESS_X = ((0, True), (3, False), (4, False))


def depth_weights(width):
    lane = lax.broadcasted_iota(jnp.int32, (1, width), 1)

    def weight(value, first, last):
        return jnp.where((lane >= first) & (lane < last), value, 0.0).astype(F32)

    forward = (weight(NEAR, 0, width - 1), weight(-FAR, 0, width - 2), weight(FAR, 1, width))
    backward = (weight(-NEAR, 1, width), weight(-FAR, 0, width - 1), weight(FAR, 2, width))
    return forward, backward


def forward_z(f, weights):
    near, far, behind = weights
    n = f.shape[-1]
    return (
        pltpu.roll(f, n - 1, 1) * near
        - NEAR * f
        + pltpu.roll(f, n - 2, 1) * far
        + pltpu.roll(f, 1, 1) * behind
    )


def backward_z(f, weights):
    near, far, behind = weights
    n = f.shape[-1]
    return (
        NEAR * f
        + pltpu.roll(f, 1, 1) * near
        + pltpu.roll(f, n - 1, 1) * far
        + pltpu.roll(f, 2, 1) * behind
    )


def forward(at, i):
    return NEAR * (at(i + 1) - at(i)) - FAR * (at(i + 2) - at(i - 1))


def backward(at, i):
    return NEAR * (at(i) - at(i - 1)) - FAR * (at(i + 1) - at(i - 2))


def place():
    tile, sec = lax.axis_index("tile"), lax.axis_index("sec")
    return lax.rem(tile, 2) == 1, sec, tile


def along_x(ahead, i, get):
    if ahead:
        taps = ((i + 1, NEAR), (i, -NEAR), (i + 2, -FAR), (i - 1, FAR))
    else:
        taps = ((i, NEAR), (i - 1, -NEAR), (i + 1, -FAR), (i - 2, FAR))
    total = None
    for j, weight in taps:
        layer = get(j)
        if layer is not None:
            total = weight * layer if total is None else total + weight * layer
    return total


def up_layers(cx):
    stress = [(0, cx - 1), (3, cx - 2), (3, cx - 1), (4, cx - 2), (4, cx - 1)]
    return stress, [(0, cx - 2), (0, cx - 1), (1, cx - 1), (2, cx - 1)]


def down_layers(cx):
    return [(0, 0), (0, 1), (3, 0), (4, 0)], [(0, 0), (1, 0), (1, 1), (2, 0), (2, 1)]


def halo_stress(cx):
    low = [(c, x - cx) for c, x in up_layers(cx)[0]]
    return {key: k for k, key in enumerate(low + [(c, x + cx) for c, x in down_layers(cx)[0]])}


def halo_velocity(cx):
    low = [(c, x - cx) for c, x in up_layers(cx)[1]]
    return {key: k for k, key in enumerate(low + [(c, x + cx) for c, x in down_layers(cx)[1]])}


def strip(ref, k, x, cx):
    return ref[(k * cx + x) * SIDE : (k * cx + x + 1) * SIDE, :]


def with_strip(own, edge, sec):
    return jnp.concatenate(
        [jnp.where(sec == 1, edge, 0.0), own, jnp.where(sec == 0, edge, 0.0)], axis=0
    )


def yz_terms(s, comp, x, base, rows, weights):
    fw, bw = weights
    here = slice(base, base + rows)

    def beside(c):
        return lambda shift: s[c, x, base + shift : base + shift + rows, :]

    if comp == 0:
        return backward(beside(3), 0) + backward_z(s[4, x, here, :], bw)
    if comp == 1:
        return forward(beside(1), 0) + backward_z(s[5, x, here, :], bw)
    return backward(beside(5), 0) + forward_z(s[2, x, here, :], fw)


def force(s, comp, x, base, rows, weights, halo=None):
    source, ahead = STRESS_X[comp]
    cx = s.shape[1]

    def get(j):
        if 0 <= j < cx:
            return s[source, j, base : base + rows, :]
        return None if halo is None else halo(source, j)

    return along_x(ahead, x, get) + yz_terms(s, comp, x, base, rows, weights)


def halo_share(comp, x, cx, halo):
    source, ahead = STRESS_X[comp]
    return along_x(ahead, x, lambda j: None if 0 <= j < cx else halo(source, j))


def own_share(s, comp, i, base, rows):
    source, ahead = STRESS_X[comp]
    cx = s.shape[1]
    return along_x(
        ahead, i, lambda j: s[source, j, base : base + rows, :] if 0 <= j < cx else None
    )


def load_stress(s, strips, s_pad, sec):
    comps, cx, cy, nz = s.shape
    nothing = jnp.zeros((SIDE, nz), F32)
    for c in range(comps):
        for x in range(cx):
            s_pad[c, x, 0:SIDE, :] = nothing
            s_pad[c, x, SIDE : 3 * SIDE + cy, :] = with_strip(s[c, x], strip(strips, c, x, cx), sec)
            s_pad[c, x, 3 * SIDE + cy :, :] = nothing


def send(odd, upper, lower, pay_a, pay_b, at):
    part = slice(at, at + upper.shape[0])
    pay_a[part, :] = jnp.where(odd, lower, upper)
    pay_b[part, :] = jnp.where(odd, upper, lower)


def send_layers(odd, up, down, layer, pay_a, pay_b, at):
    for k, (upper, lower) in enumerate(zip(up, down)):
        rows = layer(*upper)
        send(odd, rows, layer(*lower), pay_a, pay_b, at)
        at += rows.shape[0]


def first_lists(cx):
    (up_s, up_v), (down_s, down_v) = up_layers(cx), down_layers(cx)
    up_s, down_s = [("s", *key) for key in up_s], [("s", *key) for key in down_s]
    up_v, down_v = [("v", *key) for key in up_v], [("v", *key) for key in down_v]
    early = up_s + [("b", 0, cx - 1)], down_s + [("b", 0, 0), ("b", 0, 1)]
    late = up_v + [("b", 0, cx - 2)], down_v
    return early, late


def second_lists(cx):
    (up_s, up_v), (down_s, down_v) = up_layers(cx), down_layers(cx)
    up_s, down_s = [("s", *key) for key in up_s], [("s", *key) for key in down_s]
    up = up_s + [("v", *key) for key in up_v]
    return (up, down_s + [("v", *key) for key in down_v]), (up_s, down_s + down_s[-1:])


def thin_counts(lists):
    return [max(NEEDED[upper[0]], NEEDED[lower[0]]) for upper, lower in zip(*lists)]


def send_thin(odd, lists, counts, edge, pay_a, pay_b, at):
    for upper, lower, n in zip(*lists, counts):

        send(odd, edge(*upper, n), edge(*lower, n), pay_a, pay_b, at)
        at += n


def received(odd, lists, counts, pay_a, pay_b, cx, at):
    found = {}
    for upper, lower, n in zip(*lists, counts):
        part = slice(at, at + n)
        at += n
        for kind, c, x, below in ((*upper, True), (*lower, False)):

            def get(part=part, below=below):
                a, b = pay_a[part, :], pay_b[part, :]
                return jnp.where(odd, a, b) if below else jnp.where(odd, b, a)

            found[kind, c, x - cx if below else x + cx] = get
    return found


def put_layer(ref, k, own, thin, sec):
    cy, nz = own.shape
    n = thin.shape[0]
    ref[k, 0:SIDE, :] = jnp.zeros((SIDE, nz), F32)
    ref[k, SIDE : SIDE + cy, :] = own
    ref[k, SIDE + cy :, :] = jnp.zeros((SIDE, nz), F32)
    ref[k, SIDE - n : SIDE, :] = jnp.where(sec == 1, thin, 0.0)
    ref[k, SIDE + cy : SIDE + cy + n, :] = jnp.where(sec == 0, thin, 0.0)


def strains(velocity, halo, x, base, rows, weights):
    fw, bw = weights
    cx = velocity.shape[1]

    def layers(c):
        def get(j):
            if 0 <= j < cx:
                return velocity[c, j, base : base + rows, :]
            return halo(c, j)

        return get

    def beside(c):
        return lambda shift: velocity[c, x, base + shift : base + shift + rows, :]

    vx, vy, vz = (velocity[c, x, base : base + rows, :] for c in range(3))
    return (
        along_x(False, x, layers(0)),
        backward(beside(1), 0),
        backward_z(vz, bw),
        forward(beside(0), 0) + along_x(True, x, layers(1)),
        forward_z(vx, fw) + along_x(True, x, layers(2)),
        forward_z(vy, fw) + forward(beside(2), 0),
    )


def stress_change(lam, mu, parts):
    exx, eyy, ezz, xy, xz, yz = parts
    shear = DT * mu
    volume = (DT * lam) * (exx + eyy + ezz)
    double = 2.0 * shear
    return (
        volume + double * exx,
        volume + double * eyy,
        volume + double * ezz,
        shear * xy,
        shear * xz,
        shear * yz,
    )


def edge_rows(*refs):
    *fields, out = refs
    _, sec, _ = place()
    at = 0
    for field in fields:
        flat = field if len(field.shape) == 4 else None
        for c in range(field.shape[0] if flat is not None else 1):
            layers = field.shape[-3]
            for x in range(layers):
                rows = field[c, x] if flat is not None else field[x]
                out[at : at + SIDE, :] = jnp.where(sec == 0, rows[-SIDE:], rows[:SIDE])
                at += SIDE


def opening(s, v, b, pay_a, pay_b, edges, sems):
    odd, sec, _ = place()
    cx, cy, _ = b.shape
    up, down = first_lists(cx)[0]
    begin = pl.multiple_of(jnp.where(sec == 0, cy - SIDE, 0), SIDE)
    rows = [s.at[c, :, pl.ds(begin, SIDE), :] for c in range(6)]
    rows += [v.at[c, :, pl.ds(begin, SIDE), :] for c in range(3)]
    rows.append(b.at[:, pl.ds(begin, SIDE), :])
    rows = [pltpu.make_async_copy(r, edges.at[k], sems.at[k]) for k, r in enumerate(rows)]

    def run(above, below):
        copies = []
        for pay, layers in ((above, up), (below, down)):
            for k, (kind, c, x) in enumerate(layers):
                source = s.at[c, x] if kind == "s" else b.at[x]
                sem = sems.at[len(rows) + len(copies)]
                copies.append(pltpu.make_async_copy(source, pay.at[pl.ds(k * cy, cy)], sem))
        for copy in copies + rows:
            copy.start()
        for copy in copies:
            copy.wait()

    @pl.when(odd)
    def _():
        run(pay_b, pay_a)

    @pl.when(jnp.logical_not(odd))
    def _():
        run(pay_a, pay_b)

    for copy in rows:
        copy.wait()


def near_columns(state, depth, wet, out):
    _, sec, _ = place()
    rows, own = depth.shape
    for k, field in enumerate((state.at[0], state.at[1], state.at[2], depth, wet)):
        near = jnp.where(sec == 0, field[:, own - 128 :], field[:, :128])
        out[k * rows : (k + 1) * rows, :] = near.astype(F32)


def ocean_field(state, depth, wet, near, f, k):
    rows, own = depth.shape
    if k == own // 128:
        return near[f * rows : (f + 1) * rows, :]
    field = state.at[f] if f < 3 else depth if f == 3 else wet
    return field[:, k * 128 : (k + 1) * 128].astype(F32)


def ocean_edges(state, depth, wet, near, edges):
    rows, own = depth.shape
    at = 0
    for k in range(own // 128 + 1):
        for f, n in enumerate(DEEP if k < own // 128 else CORNER):
            field = ocean_field(state, depth, wet, near, f, k)
            edges[0, at : at + n, :] = field[rows - n :]
            edges[1, at : at + n, :] = field[:n]
            at += n


def first_round(s, v, b, strips, pay_a, pay_b, s_pad, v_part):
    odd, sec, _ = place()
    _, cx, cy, nz = s.shape
    weights = depth_weights(nz)
    rows = cy + 2 * SIDE
    load_stress(s, strips, s_pad, sec)
    for x in range(cx):
        scale = DT * with_strip(b[x], strip(strips, 9, x, cx), sec)
        for c in range(3):
            old = with_strip(v[c, x], strip(strips, 6 + c, x, cx), sec)
            v_part[c, x] = old + scale * force(s_pad, c, x, SIDE, rows, weights)

    def layer(kind, c, x):
        return v_part[c, x, SIDE : SIDE + cy, :] if kind == "v" else b[x]

    def edge(kind, c, x, n):
        if kind == "v":
            past = slice(SIDE + cy, SIDE + cy + n)
            return jnp.where(sec == 0, v_part[c, x, past, :], v_part[c, x, SIDE - n : SIDE, :])
        whole = strip(strips, c if kind == "s" else 9, x, cx)
        return jnp.where(sec == 0, whole[:n], whole[SIDE - n :])

    early, late = first_lists(cx)
    send_layers(odd, *late, layer, pay_a, pay_b, 0)
    at = len(late[0]) * cy
    for lists in (early, late):
        counts = thin_counts(lists)
        send_thin(odd, lists, counts, edge, pay_a, pay_b, at)
        at += sum(counts)


def first_received(odd, cx, cy, early_a, early_b, late_a, late_b):
    early, late = first_lists(cx)
    own = received(odd, early, [cy] * len(early[0]), early_a, early_b, cx, 0)
    own.update(received(odd, late, [cy] * len(late[0]), late_a, late_b, cx, 0))
    at = len(late[0]) * cy
    rest = received(odd, early, thin_counts(early), late_a, late_b, cx, at)
    at += sum(thin_counts(early))
    rest.update(received(odd, late, thin_counts(late), late_a, late_b, cx, at))
    return own, rest


def whole_step(
    s_pad,
    v_part,
    b,
    lam,
    mu,
    strips,
    more_strips,
    early_a,
    early_b,
    late_a,
    late_b,
    sea,
    v_out,
    s_out,
    pay_a,
    pay_b,
    b_near,
    v_pad,
    halo_s,
    halo_v,
    halo_b,
    materials,
):
    odd, sec, _ = place()
    cx, cy, nz = b.shape
    weights = depth_weights(nz)
    rows = cy + 2 * SIDE
    index_s, index_v = halo_stress(cx), halo_velocity(cx)
    own, rest = first_received(odd, cx, cy, early_a, early_b, late_a, late_b)
    for key, k in index_s.items():
        put_layer(halo_s, k, own["s", *key](), rest["s", *key](), sec)
    for key, k in index_v.items():
        put_layer(halo_v, k, own["v", *key](), rest["v", *key](), sec)
    index_b = {i: k for k, i in enumerate((-2, -1, cx, cx + 1))}
    for i, k in index_b.items():
        put_layer(halo_b, k, own["b", 0, i](), rest["b", 0, i](), sec)
        b_near[k * cy : (k + 1) * cy, :] = own["b", 0, i]()
    for x in range(cx):
        part = slice(4 * cy + x * SIDE, 4 * cy + (x + 1) * SIDE)
        b_near[part, :] = strip(strips, 9, x, cx)
    nothing = jnp.zeros((SIDE, nz), F32)
    for x in range(cx):
        scale = DT * with_strip(b[x], strip(strips, 9, x, cx), sec)
        for c in range(3):
            new = v_part[c, x]
            terms = halo_share(c, x, cx, lambda k, j: halo_s[index_s[k, j]])
            if terms is not None:
                new = new + scale * terms
            v_pad[c, x, 0:SIDE, :] = nothing
            v_pad[c, x, SIDE : SIDE + rows, :] = new
            v_pad[c, x, SIDE + rows :, :] = nothing
            v_out[c, x] = v_pad[c, x, SIDE + EDGE : SIDE + rows - EDGE, :]
    for (c, i), k in index_v.items():
        halo_v[k] = halo_v[k] + DT * halo_b[index_b[i]] * own_share(s_pad, c, i, SIDE, rows)
    kept = slice(EDGE, rows - EDGE)
    base, fewer = SIDE + EDGE, rows - 2 * EDGE
    halo = lambda c, j: halo_v[index_v[c, j], kept, :]
    for x in range(cx):
        parts = strains(v_pad, halo, x, base, fewer, weights)
        materials[0] = with_strip(lam[x], strip(more_strips, 0, x, cx), sec)
        materials[1] = with_strip(mu[x], strip(more_strips, 1, x, cx), sec)
        changes = stress_change(materials[0, kept, :], materials[1, kept, :], parts)
        for c, change in enumerate(changes):
            s_out[c, x] = s_pad[c, x, base : base + fewer, :] + change

    def layer(kind, c, x):
        if kind == "s":
            return s_out[c, x, EDGE : EDGE + cy, :]
        old = v_out[c, x, EDGE : EDGE + cy, :]
        return old + DT * b[x] * force(s_out, c, x, EDGE, cy, weights)

    def edge(_, c, x, n):
        past = slice(EDGE + cy, EDGE + cy + n)
        return jnp.where(sec == 0, s_out[c, x, past, :], s_out[c, x, EDGE - n : EDGE, :])

    layers, edges = second_lists(cx)
    send_layers(odd, *layers, layer, pay_a, pay_b, 0)
    counts = [LAST_NEEDED] * len(edges[0])
    at = LAYERS * cy
    send(odd, sea[0], sea[1], pay_a, pay_b, at)
    send_thin(odd, edges, counts, edge, pay_a, pay_b, at + sea.shape[1])


def last_step(
    sea_rows,
    s,
    v,
    b,
    lam,
    mu,
    b_near,
    from_a,
    from_b,
    v_out,
    s_out,
    v_rows,
    b_rows,
    halo_s,
    halo_v,
    made,
    sems,
):
    odd, sec, _ = place()
    cx, cy, nz = b.shape
    weights = depth_weights(nz)
    first, rows = EDGE - LAST_NEEDED, cy + 2 * LAST_NEEDED
    here = slice(SIDE - LAST_NEEDED, SIDE - LAST_NEEDED + rows)
    index_s, index_v = halo_stress(cx), halo_velocity(cx)
    layers, edges = second_lists(cx)
    own = received(odd, layers, [cy] * LAYERS, from_a, from_b, cx, 0)
    counts = [LAST_NEEDED] * len(edges[0])
    rest = received(odd, edges, counts, from_a, from_b, cx, LAYERS * cy + sea_rows)
    for key, k in index_s.items():
        put_layer(halo_s, k, own["s", *key](), rest["s", *key](), sec)
    for x in range(cx):
        part = slice(4 * cy + x * SIDE, 4 * cy + (x + 1) * SIDE)
        b_rows[...] = with_strip(b[x], b_near[part, :], sec)
        scale = DT * b_rows[here, :]
        for c in range(3):
            halo = lambda k, j: halo_s[index_s[k, j], here, :]
            terms = force(s, c, x, first, rows, weights, halo)
            v_rows[c, x, here, :] = v[c, x, first : first + rows, :] + scale * terms
    copies = [pltpu.make_async_copy(v_rows.at[:, :, pl.ds(SIDE, cy), :], v_out, sems.at[cx])]
    copies[0].start()
    for (c, i), k in index_v.items():
        at = (i + 2 if i < 0 else i - cx + 2) * cy
        scale = DT * b_near[at : at + cy, :]
        halo_v[k] = own["v", c, i]() + scale * own_share(s, c, i, EDGE, cy)
    for x in range(cx):
        parts = strains(v_rows, lambda c, j: halo_v[index_v[c, j]], x, SIDE, cy, weights)
        for c, change in enumerate(stress_change(lam[x], mu[x], parts)):
            made[c, x] = s[c, x, EDGE : EDGE + cy, :] + change
        copies.append(pltpu.make_async_copy(made.at[:, x], s_out.at[:, x], sems.at[x]))
        copies[-1].start()
    return copies


def floor_line(left, right):
    rows = left.shape[0]
    row = lax.broadcasted_iota(jnp.int32, (rows, 2 * rows), 0)
    lane = lax.broadcasted_iota(jnp.int32, (rows, 2 * rows), 1)
    picked = jnp.where(lane == row, left[:, 0:1], 0.0)
    picked = jnp.where(lane == row + rows, right[:, 0:1], picked)
    return jnp.sum(picked, axis=0, keepdims=True)


def floor_parts(s, v, b, info, parts):
    cx, cy, nz = b.shape
    weights = depth_weights(nz)
    own = slice(EDGE, EDGE + cy)
    layers = [
        v[2, x, own, :] + DT * b[x] * force(s, 2, x, EDGE, cy, weights) for x in range(cx)
    ]
    lines = [floor_line(layers[x], layers[x + 1]) for x in range(0, cx, 2)]
    lines.append(floor_line(s[4, cx - 1, own, :], s[4, cx - 2, own, :]))
    lines.append(floor_line(s[4, 0, own, :], (-FAR * DT) * b[cx - 1]))
    lines.append(floor_line(DT * b[0], DT * b[1]))
    lines.append(info[...])
    row = lax.broadcasted_iota(jnp.int32, (SIDE, 2 * cy), 0)
    period = 3 * SIDE
    for k in range(0, period, SIDE):
        tiled = jnp.zeros((SIDE, 2 * cy), F32)
        for j in range(SIDE):
            tiled = jnp.where(row == j, lines[(k + j) % LINES], tiled)
        for at in range(k, parts.shape[0], period):
            parts[at : at + SIDE, :] = tiled


def column(line, first, count):
    wide = jnp.broadcast_to(line, (count, line.shape[1]))
    row = lax.broadcasted_iota(jnp.int32, wide.shape, 0)
    lane = lax.broadcasted_iota(jnp.int32, wide.shape, 1)
    return jnp.sum(jnp.where(lane == row + first, wide, 0.0), axis=1, keepdims=True)


def ocean_steps(
    start, from_a, from_b, near, state, depth, wet_ref, info, patches, ocean_out, ocean_ref, send_out
):
    odd, sec, tile = place()
    count = lax.axis_size("tile")
    rows, own = depth.shape
    columns = own + 128
    at = start
    for k in range(columns // 128):
        lanes = slice(k * 128, (k + 1) * 128)
        for f, n in enumerate(DEEP if k < own // 128 else CORNER):
            here = ocean_field(state, depth, wet_ref, near, f, k)
            a, b = from_a[at : at + n, :], from_b[at : at + n, :]
            low, high = jnp.where(odd, a, b), jnp.where(odd, b, a)
            ocean_ref[f, 0:SIDE, lanes] = jnp.zeros((SIDE, 128), F32)
            ocean_ref[f, SIDE + rows :, lanes] = jnp.zeros((SIDE, 128), F32)
            ocean_ref[f, SIDE - n : SIDE, lanes] = low
            ocean_ref[f, SIDE : SIDE + rows, lanes] = here
            ocean_ref[f, SIDE + rows : SIDE + rows + n, lanes] = high
            at += n

    total = rows + 2 * SIDE
    lane = lax.broadcasted_iota(jnp.int32, (1, columns), 1)
    ahead = jnp.where((lane == own - 1) & (sec == 1), 0.0, 0.5).astype(F32)
    behind = jnp.where((lane == 0) & (sec == 0), 0.0, 0.5).astype(F32)
    line = lax.broadcasted_iota(jnp.int32, (total, 1), 0)
    inside = ((line >= SIDE) | (tile > 0)) & ((line < SIDE + rows) | (tile < count - 1))
    inside = inside.astype(F32)

    def across(f):
        return pltpu.roll(f, columns - 1, 1) * ahead - pltpu.roll(f, 1, 1) * behind

    def down(f):
        return 0.5 * (pltpu.roll(f, total - 1, 0) - pltpu.roll(f, 1, 0))

    eta, u, v_sea = ocean_ref[0], ocean_ref[1], ocean_ref[2]
    depth, wet = ocean_ref[3], ocean_ref[4]
    window = min(WINDOW, count)
    base = jnp.clip(tile - REACH - 1, 0, count - window)

    def told(half, k):
        return patches[pl.ds((half * count + k) * LINES, LINES), :]

    below = told(sec, jnp.maximum(tile - 1, 0))[5:6]
    above = told(sec, jnp.minimum(tile + 1, count - 1))[5:6]
    line = info[...]
    marks = [
        jnp.concatenate(
            [
                column(below, k * rows + rows - SIDE, SIDE),
                column(line, k * rows, rows),
                column(above, k * rows, SIDE),
            ],
            axis=0,
        )
        for k in range(2)
    ]
    owner = jnp.broadcast_to(marks[0] - base.astype(F32), (total, 128))
    share = marks[1]
    width = own // 4
    left = lax.broadcasted_iota(jnp.int32, (1, 128), 1) < width
    near = jnp.where(left, -NEAR, FAR).astype(F32)
    far = jnp.where(left, FAR, 0.0).astype(F32)
    uplift = []
    for half in (sec, 1 - sec):
        tiles = []
        for k in range(-1, window + 1):
            here = jnp.clip(base + k, 0, count - 1)
            there = (here == base + k).astype(F32)
            tiles.append(told(half, here) * there)
        levels = [jnp.zeros((total, 128), F32) for _ in range(2)]
        for k in range(window):
            below, this, above = tiles[k], tiles[k + 1], tiles[k + 2]
            last = pltpu.roll(below[2:3], width, 1)
            last = near * jnp.where(left, below[2:3], last) + far * last
            first = this[0:1] + this[4:5] * last
            second = this[1:2] + jnp.where(left, 0.0, this[3:4]) * pltpu.roll(above[3:4], width, 1)
            mine = owner == float(k)
            levels = [jnp.where(mine, q, level) for q, level in zip((first, second), levels)]
        uplift.append(levels)
    uplift = uplift[0] + [jnp.where(sec == 0, uplift[1][0], uplift[1][1])]
    uplift = jnp.concatenate(uplift, axis=1)
    lift = ODT * (share * wet * uplift)
    part = slice(SIDE, SIDE + rows)
    for step in range(2):
        u = wet * (u - ODT * down(eta))
        v_sea = wet * (v_sea - ODT * across(eta))
        if step == 1:
            ocean_out[1] = u[part, :own]
            ocean_out[2] = v_sea[part, :own]
            send_out(slice(1, 3))
        eta = inside * (eta - ODT * (down(depth * u) + across(depth * v_sea)) + lift)
    ocean_out[0] = eta[part, :own]
    send_out(slice(0, 1))


def finish(
    sea_rows,
    s,
    v,
    b,
    lam,
    mu,
    b_near,
    from_a,
    from_b,
    near,
    state,
    depth,
    wet,
    info,
    patches,
    v_out,
    s_out,
    ocean_out,
    v_rows,
    b_rows,
    halo_s,
    halo_v,
    made,
    ocean_ref,
    ocean_made,
    sems,
    ocean_sems,
):
    cx, cy, _ = b.shape
    copies = last_step(
        sea_rows,
        s,
        v,
        b,
        lam,
        mu,
        b_near,
        from_a,
        from_b,
        v_out,
        s_out,
        v_rows,
        b_rows,
        halo_s,
        halo_v,
        made,
        sems,
    )

    def send_out(part):
        size = part.stop - part.start
        here = (pl.ds(part.start, size),)
        copies.append(
            pltpu.make_async_copy(
                ocean_made.at[here], ocean_out.at[here], ocean_sems.at[part.start]
            )
        )
        copies[-1].start()

    ocean_steps(
        LAYERS * cy,
        from_a,
        from_b,
        near,
        state,
        depth,
        wet,
        info,
        patches,
        ocean_made,
        ocean_ref,
        send_out,
    )
    for copy in copies:
        copy.wait()


VMEM = pl.BlockSpec(memory_space=pltpu.VMEM)
ANY = pl.BlockSpec(memory_space=pl.ANY)


def call(body, name, outs, scratch, operands, weight=1, ins=VMEM, where=VMEM, grant=8):
    shapes = [jax.ShapeDtypeStruct(o, F32) for o in outs]
    moved = sum(o.size for o in operands) * 4 + sum(o.size for o in shapes) * 4
    return pl.pallas_call(
        body,
        name=name,
        out_shape=shapes,
        in_specs=ins if isinstance(ins, list) else [ins] * len(operands),
        out_specs=where if isinstance(where, list) else [where] * len(outs),
        scratch_shapes=scratch,
        compiler_params=pltpu.CompilerParams(vmem_limit_bytes=int(grant * 1024 * 1024)),
        cost_estimate=pl.CostEstimate(
            flops=moved * weight, bytes_accessed=moved * weight, transcendentals=0
        ),
    )(*operands)


def exchange(pay_a, pay_b, count):
    def swap(pay, first):
        pairs = []
        for i in range(first, count - 1, 2):
            pairs += [(i, i + 1), (i + 1, i)]
        return lax.ppermute(pay, "tile", pairs)

    from_a = swap(pay_a, 0)
    return from_a, swap(pay_b, 1)


def across(pay):
    return lax.ppermute(pay, "sec", [(0, 1), (1, 0)])


def shards(
    velocity,
    stresses,
    buoyancy,
    lame_first,
    shear_mod,
    ocean_state,
    depth_map,
    wet_mask,
    intersection_src,
    intersection_share,
):
    count = lax.axis_size("tile")
    sec = lax.axis_index("sec")
    _, cx, cy, nz = stresses.shape
    _, rows, columns = ocean_state.shape
    tall = cy + 2 * SIDE
    halo = pltpu.VMEM((LAYERS, tall, nz), F32)

    first = ((LAYERS + 2) // 2 + 1) * cy
    pay_a, pay_b, edges = call(
        opening,
        "opening",
        [(first, nz), (first, nz), (10, cx, SIDE, nz)],
        [pltpu.SemaphoreType.DMA((10 + 2 * (first // cy),))],
        [stresses, velocity, buoyancy],
        ins=ANY,
        grant=60,
    )
    strips = across(edges.reshape(10 * cx * SIDE, nz))
    early_a, early_b = exchange(pay_a, pay_b, count)
    early_list, late_list = first_lists(cx)
    per = columns // 128 * sum(DEEP) + sum(CORNER)
    late = len(late_list[0]) * cy + sum(thin_counts(early_list) + thin_counts(late_list))
    pay_a, pay_b, stresses, velocity = call(
        first_round,
        "first_round",
        [(late, nz), (late, nz), (6, cx, tall + 2 * SIDE, nz), (3, cx, tall, nz)],
        [],
        [stresses, velocity, buoyancy, strips],
    )
    late_a, late_b = exchange(pay_a, pay_b, count)

    source, share, lame, shear, _ = lax.optimization_barrier(
        (intersection_src, intersection_share, lame_first, shear_mod, early_b)
    )
    ocean_state, depth_map, wet_mask, _ = lax.optimization_barrier(
        (ocean_state, depth_map, wet_mask, early_a)
    )
    (edges,) = call(edge_rows, "edge_rows", [(2 * cx * SIDE, nz)], [], [lame, shear])
    more_strips = across(edges)
    sea = [ocean_state, depth_map, wet_mask]
    (near,) = call(near_columns, "near_columns", [(len(DEEP) * rows, 128)], [], sea)
    near = across(near)
    (edges,) = call(ocean_edges, "ocean_edges", [(2, per, 128)], [], sea + [near])
    info = jnp.concatenate([source.astype(F32), share])[None]

    second = (LAYERS * cy + per + 5 * LAST_NEEDED, nz)
    velocity, stresses, pay_a, pay_b, b_near = call(
        whole_step,
        "whole_step",
        [(3, cx, cy + 2 * EDGE, nz), (6, cx, cy + 2 * EDGE, nz), second, second]
        + [(4 * cy + cx * SIDE, nz)],
        [
            pltpu.VMEM((3, cx, tall + 2 * SIDE, nz), F32),
            halo,
            halo,
            pltpu.VMEM((4, tall, nz), F32),
            pltpu.VMEM((2, tall, nz), F32),
        ],
        [stresses, velocity, buoyancy, lame_first, shear_mod, strips, more_strips]
        + [early_a, early_b, late_a, late_b, edges],
    )
    from_a, from_b = exchange(pay_a, pay_b, count)
    (parts,) = call(
        floor_parts,
        "floor_parts",
        [(2 * count * LINES, 2 * cy)],
        [],
        [stresses, velocity, buoyancy, info],
    )
    parts = parts.reshape(2 * count * LINES // 2, 2, 2 * cy)
    patches = lax.all_to_all(parts, ("sec", "tile"), 0, 0, tiled=True).reshape(-1, 2 * cy)
    velocity, stresses, ocean_state = call(
        functools.partial(finish, per),
        "finish",
        [(3, cx, cy, nz), (6, cx, cy, nz), ocean_state.shape],
        [
            pltpu.VMEM((3, cx, tall, nz), F32),
            pltpu.VMEM((tall, nz), F32),
            halo,
            pltpu.VMEM((LAYERS, cy, nz), F32),
            pltpu.VMEM((6, cx, cy, nz), F32),
            pltpu.VMEM((len(DEEP), rows + 2 * SIDE, columns + 128), F32),
            pltpu.VMEM(ocean_state.shape, F32),
            pltpu.SemaphoreType.DMA((cx + 1,)),
            pltpu.SemaphoreType.DMA((2,)),
        ],
        [stresses, velocity, buoyancy, lame_first, shear_mod, b_near]
        + [from_a, from_b, near] + sea + [info, patches],
        where=ANY,
    )
    return velocity, stresses, ocean_state


def solution(mesh):
    cube = P("tile", "sec", None)
    return jax.shard_map(
        shards,
        mesh=mesh,
        in_specs=(
            P(None, "tile", "sec", None),
            P(None, "tile", "sec", None),
            cube,
            cube,
            cube,
            P(None, "tile", "sec"),
            P("tile", "sec"),
            P("tile", "sec"),
            P("tile"),
            P("tile"),
        ),
        out_specs=(
            P(None, "tile", "sec", None),
            P(None, "tile", "sec", None),
            P(None, "tile", "sec"),
        ),
        check_vma=False,
    )
```

```python
import functools

import jax
import jax.numpy as jnp
from jax import lax
from jax.experimental import pallas as pl
from jax.experimental.pallas import tpu as pltpu
from jax.sharding import PartitionSpec as P

REACH = 2
NEAR = 9.0 / 8.0
FAR = 1.0 / 24.0
DT = 0.15
ODT = 0.3
F32 = jnp.float32
EDGE = 4
SIDE = 8
WINDOW = 8
DEEP = (4, 3, 2, 3, 3)
CORNER = (2, 1, 2, 2, 2)
LINES = 6
NEEDED = {"s": 5, "v": 3, "b": 3}
LAST_NEEDED = 2
LAYERS = 9
STRESS_X = ((0, True), (3, False), (4, False))


def depth_weights(width):
    lane = lax.broadcasted_iota(jnp.int32, (1, width), 1)

    def weight(value, first, last):
        return jnp.where((lane >= first) & (lane < last), value, 0.0).astype(F32)

    forward = (weight(NEAR, 0, width - 1), weight(-FAR, 0, width - 2), weight(FAR, 1, width))
    backward = (weight(-NEAR, 1, width), weight(-FAR, 0, width - 1), weight(FAR, 2, width))
    return forward, backward


def forward_z(f, weights):
    near, far, behind = weights
    n = f.shape[-1]
    return (
        pltpu.roll(f, n - 1, 1) * near
        - NEAR * f
        + pltpu.roll(f, n - 2, 1) * far
        + pltpu.roll(f, 1, 1) * behind
    )


def backward_z(f, weights):
    near, far, behind = weights
    n = f.shape[-1]
    return (
        NEAR * f
        + pltpu.roll(f, 1, 1) * near
        + pltpu.roll(f, n - 1, 1) * far
        + pltpu.roll(f, 2, 1) * behind
    )


def forward(at, i):
    return NEAR * (at(i + 1) - at(i)) - FAR * (at(i + 2) - at(i - 1))


def backward(at, i):
    return NEAR * (at(i) - at(i - 1)) - FAR * (at(i + 1) - at(i - 2))


def place():
    tile, sec = lax.axis_index("tile"), lax.axis_index("sec")
    return lax.rem(tile, 2) == 1, sec, tile


def along_x(ahead, i, get):
    if ahead:
        taps = ((i + 1, NEAR), (i, -NEAR), (i + 2, -FAR), (i - 1, FAR))
    else:
        taps = ((i, NEAR), (i - 1, -NEAR), (i + 1, -FAR), (i - 2, FAR))
    total = None
    for j, weight in taps:
        layer = get(j)
        if layer is not None:
            total = weight * layer if total is None else total + weight * layer
    return total


def up_layers(cx):
    stress = [(0, cx - 1), (3, cx - 2), (3, cx - 1), (4, cx - 2), (4, cx - 1)]
    return stress, [(0, cx - 2), (0, cx - 1), (1, cx - 1), (2, cx - 1)]


def down_layers(cx):
    return [(0, 0), (0, 1), (3, 0), (4, 0)], [(0, 0), (1, 0), (1, 1), (2, 0), (2, 1)]


def halo_stress(cx):
    low = [(c, x - cx) for c, x in up_layers(cx)[0]]
    return {key: k for k, key in enumerate(low + [(c, x + cx) for c, x in down_layers(cx)[0]])}


def halo_velocity(cx):
    low = [(c, x - cx) for c, x in up_layers(cx)[1]]
    return {key: k for k, key in enumerate(low + [(c, x + cx) for c, x in down_layers(cx)[1]])}


def strip(ref, k, x, cx):
    return ref[(k * cx + x) * SIDE : (k * cx + x + 1) * SIDE, :]


def with_strip(own, edge, sec):
    return jnp.concatenate(
        [jnp.where(sec == 1, edge, 0.0), own, jnp.where(sec == 0, edge, 0.0)], axis=0
    )


def yz_terms(s, comp, x, base, rows, weights):
    fw, bw = weights
    here = slice(base, base + rows)

    def beside(c):
        return lambda shift: s[c, x, base + shift : base + shift + rows, :]

    if comp == 0:
        return backward(beside(3), 0) + backward_z(s[4, x, here, :], bw)
    if comp == 1:
        return forward(beside(1), 0) + backward_z(s[5, x, here, :], bw)
    return backward(beside(5), 0) + forward_z(s[2, x, here, :], fw)


def force(s, comp, x, base, rows, weights, halo=None):
    source, ahead = STRESS_X[comp]
    cx = s.shape[1]

    def get(j):
        if 0 <= j < cx:
            return s[source, j, base : base + rows, :]
        return None if halo is None else halo(source, j)

    return along_x(ahead, x, get) + yz_terms(s, comp, x, base, rows, weights)


def halo_share(comp, x, cx, halo):
    source, ahead = STRESS_X[comp]
    return along_x(ahead, x, lambda j: None if 0 <= j < cx else halo(source, j))


def own_share(s, comp, i, base, rows):
    source, ahead = STRESS_X[comp]
    cx = s.shape[1]
    return along_x(
        ahead, i, lambda j: s[source, j, base : base + rows, :] if 0 <= j < cx else None
    )


def load_stress(s, strips, s_pad, sec):
    comps, cx, cy, nz = s.shape
    nothing = jnp.zeros((SIDE, nz), F32)
    for c in range(comps):
        for x in range(cx):
            s_pad[c, x, 0:SIDE, :] = nothing
            s_pad[c, x, SIDE : 3 * SIDE + cy, :] = with_strip(s[c, x], strip(strips, c, x, cx), sec)
            s_pad[c, x, 3 * SIDE + cy :, :] = nothing


def send(odd, upper, lower, pay_a, pay_b, at):
    part = slice(at, at + upper.shape[0])
    pay_a[part, :] = jnp.where(odd, lower, upper)
    pay_b[part, :] = jnp.where(odd, upper, lower)


def send_layers(odd, up, down, layer, pay_a, pay_b, at):
    for k, (upper, lower) in enumerate(zip(up, down)):
        rows = layer(*upper)
        send(odd, rows, layer(*lower), pay_a, pay_b, at)
        at += rows.shape[0]


def first_lists(cx):
    (up_s, up_v), (down_s, down_v) = up_layers(cx), down_layers(cx)
    up_s, down_s = [("s", *key) for key in up_s], [("s", *key) for key in down_s]
    up_v, down_v = [("v", *key) for key in up_v], [("v", *key) for key in down_v]
    early = up_s + [("b", 0, cx - 1)], down_s + [("b", 0, 0), ("b", 0, 1)]
    late = up_v + [("b", 0, cx - 2)], down_v
    return early, late


def second_lists(cx):
    (up_s, up_v), (down_s, down_v) = up_layers(cx), down_layers(cx)
    up_s, down_s = [("s", *key) for key in up_s], [("s", *key) for key in down_s]
    up = up_s + [("v", *key) for key in up_v]
    return (up, down_s + [("v", *key) for key in down_v]), (up_s, down_s + down_s[-1:])


def thin_counts(lists):
    return [max(NEEDED[upper[0]], NEEDED[lower[0]]) for upper, lower in zip(*lists)]


def send_thin(odd, lists, counts, edge, pay_a, pay_b, at):
    for upper, lower, n in zip(*lists, counts):

        send(odd, edge(*upper, n), edge(*lower, n), pay_a, pay_b, at)
        at += n


def received(odd, lists, counts, pay_a, pay_b, cx, at):
    found = {}
    for upper, lower, n in zip(*lists, counts):
        part = slice(at, at + n)
        at += n
        for kind, c, x, below in ((*upper, True), (*lower, False)):

            def get(part=part, below=below):
                a, b = pay_a[part, :], pay_b[part, :]
                return jnp.where(odd, a, b) if below else jnp.where(odd, b, a)

            found[kind, c, x - cx if below else x + cx] = get
    return found


def put_layer(ref, k, own, thin, sec):
    cy, nz = own.shape
    n = thin.shape[0]
    ref[k, 0:SIDE, :] = jnp.zeros((SIDE, nz), F32)
    ref[k, SIDE : SIDE + cy, :] = own
    ref[k, SIDE + cy :, :] = jnp.zeros((SIDE, nz), F32)
    ref[k, SIDE - n : SIDE, :] = jnp.where(sec == 1, thin, 0.0)
    ref[k, SIDE + cy : SIDE + cy + n, :] = jnp.where(sec == 0, thin, 0.0)


def strains(velocity, halo, x, base, rows, weights):
    fw, bw = weights
    cx = velocity.shape[1]

    def layers(c):
        def get(j):
            if 0 <= j < cx:
                return velocity[c, j, base : base + rows, :]
            return halo(c, j)

        return get

    def beside(c):
        return lambda shift: velocity[c, x, base + shift : base + shift + rows, :]

    vx, vy, vz = (velocity[c, x, base : base + rows, :] for c in range(3))
    return (
        along_x(False, x, layers(0)),
        backward(beside(1), 0),
        backward_z(vz, bw),
        forward(beside(0), 0) + along_x(True, x, layers(1)),
        forward_z(vx, fw) + along_x(True, x, layers(2)),
        forward_z(vy, fw) + forward(beside(2), 0),
    )


def stress_change(lam, mu, parts):
    exx, eyy, ezz, xy, xz, yz = parts
    shear = DT * mu
    volume = (DT * lam) * (exx + eyy + ezz)
    double = 2.0 * shear
    return (
        volume + double * exx,
        volume + double * eyy,
        volume + double * ezz,
        shear * xy,
        shear * xz,
        shear * yz,
    )


def edge_rows(*refs):
    *fields, out = refs
    _, sec, _ = place()
    at = 0
    for field in fields:
        flat = field if len(field.shape) == 4 else None
        for c in range(field.shape[0] if flat is not None else 1):
            layers = field.shape[-3]
            for x in range(layers):
                rows = field[c, x] if flat is not None else field[x]
                out[at : at + SIDE, :] = jnp.where(sec == 0, rows[-SIDE:], rows[:SIDE])
                at += SIDE


def opening(s, v, b, pay_a, pay_b, edges, sems):
    odd, sec, _ = place()
    cx, cy, _ = b.shape
    up, down = first_lists(cx)[0]
    begin = pl.multiple_of(jnp.where(sec == 0, cy - SIDE, 0), SIDE)
    rows = [s.at[c, :, pl.ds(begin, SIDE), :] for c in range(6)]
    rows += [v.at[c, :, pl.ds(begin, SIDE), :] for c in range(3)]
    rows.append(b.at[:, pl.ds(begin, SIDE), :])
    rows = [pltpu.make_async_copy(r, edges.at[k], sems.at[k]) for k, r in enumerate(rows)]

    def run(above, below):
        copies = []
        for pay, layers in ((above, up), (below, down)):
            for k, (kind, c, x) in enumerate(layers):
                source = s.at[c, x] if kind == "s" else b.at[x]
                sem = sems.at[len(rows) + len(copies)]
                copies.append(pltpu.make_async_copy(source, pay.at[pl.ds(k * cy, cy)], sem))
        for copy in copies + rows:
            copy.start()
        for copy in copies:
            copy.wait()

    @pl.when(odd)
    def _():
        run(pay_b, pay_a)

    @pl.when(jnp.logical_not(odd))
    def _():
        run(pay_a, pay_b)

    for copy in rows:
        copy.wait()


def near_columns(state, depth, wet, out):
    _, sec, _ = place()
    rows, own = depth.shape
    for k, field in enumerate((state.at[0], state.at[1], state.at[2], depth, wet)):
        near = jnp.where(sec == 0, field[:, own - 128 :], field[:, :128])
        out[k * rows : (k + 1) * rows, :] = near.astype(F32)


def ocean_field(state, depth, wet, near, f, k):
    rows, own = depth.shape
    if k == own // 128:
        return near[f * rows : (f + 1) * rows, :]
    field = state.at[f] if f < 3 else depth if f == 3 else wet
    return field[:, k * 128 : (k + 1) * 128].astype(F32)


def ocean_edges(state, depth, wet, near, edges):
    rows, own = depth.shape
    at = 0
    for k in range(own // 128 + 1):
        for f, n in enumerate(DEEP if k < own // 128 else CORNER):
            field = ocean_field(state, depth, wet, near, f, k)
            edges[0, at : at + n, :] = field[rows - n :]
            edges[1, at : at + n, :] = field[:n]
            at += n


def first_round(s, v, b, strips, pay_a, pay_b, s_pad, v_part):
    odd, sec, _ = place()
    _, cx, cy, nz = s.shape
    weights = depth_weights(nz)
    rows = cy + 2 * SIDE
    load_stress(s, strips, s_pad, sec)
    for x in range(cx):
        scale = DT * with_strip(b[x], strip(strips, 9, x, cx), sec)
        for c in range(3):
            old = with_strip(v[c, x], strip(strips, 6 + c, x, cx), sec)
            v_part[c, x] = old + scale * force(s_pad, c, x, SIDE, rows, weights)

    def layer(kind, c, x):
        return v_part[c, x, SIDE : SIDE + cy, :] if kind == "v" else b[x]

    def edge(kind, c, x, n):
        if kind == "v":
            past = slice(SIDE + cy, SIDE + cy + n)
            return jnp.where(sec == 0, v_part[c, x, past, :], v_part[c, x, SIDE - n : SIDE, :])
        whole = strip(strips, c if kind == "s" else 9, x, cx)
        return jnp.where(sec == 0, whole[:n], whole[SIDE - n :])

    early, late = first_lists(cx)
    send_layers(odd, *late, layer, pay_a, pay_b, 0)
    at = len(late[0]) * cy
    for lists in (early, late):
        counts = thin_counts(lists)
        send_thin(odd, lists, counts, edge, pay_a, pay_b, at)
        at += sum(counts)


def first_received(odd, cx, cy, early_a, early_b, late_a, late_b):
    early, late = first_lists(cx)
    own = received(odd, early, [cy] * len(early[0]), early_a, early_b, cx, 0)
    own.update(received(odd, late, [cy] * len(late[0]), late_a, late_b, cx, 0))
    at = len(late[0]) * cy
    rest = received(odd, early, thin_counts(early), late_a, late_b, cx, at)
    at += sum(thin_counts(early))
    rest.update(received(odd, late, thin_counts(late), late_a, late_b, cx, at))
    return own, rest


def whole_step(
    s_pad,
    v_part,
    b,
    lam,
    mu,
    strips,
    more_strips,
    early_a,
    early_b,
    late_a,
    late_b,
    sea,
    v_out,
    s_out,
    pay_a,
    pay_b,
    b_near,
    v_pad,
    halo_s,
    halo_v,
    halo_b,
    materials,
):
    odd, sec, _ = place()
    cx, cy, nz = b.shape
    weights = depth_weights(nz)
    rows = cy + 2 * SIDE
    index_s, index_v = halo_stress(cx), halo_velocity(cx)
    own, rest = first_received(odd, cx, cy, early_a, early_b, late_a, late_b)
    for key, k in index_s.items():
        put_layer(halo_s, k, own["s", *key](), rest["s", *key](), sec)
    for key, k in index_v.items():
        put_layer(halo_v, k, own["v", *key](), rest["v", *key](), sec)
    index_b = {i: k for k, i in enumerate((-2, -1, cx, cx + 1))}
    for i, k in index_b.items():
        put_layer(halo_b, k, own["b", 0, i](), rest["b", 0, i](), sec)
        b_near[k * cy : (k + 1) * cy, :] = own["b", 0, i]()
    for x in range(cx):
        part = slice(4 * cy + x * SIDE, 4 * cy + (x + 1) * SIDE)
        b_near[part, :] = strip(strips, 9, x, cx)
    nothing = jnp.zeros((SIDE, nz), F32)
    for x in range(cx):
        scale = DT * with_strip(b[x], strip(strips, 9, x, cx), sec)
        for c in range(3):
            new = v_part[c, x]
            terms = halo_share(c, x, cx, lambda k, j: halo_s[index_s[k, j]])
            if terms is not None:
                new = new + scale * terms
            v_pad[c, x, 0:SIDE, :] = nothing
            v_pad[c, x, SIDE : SIDE + rows, :] = new
            v_pad[c, x, SIDE + rows :, :] = nothing
            v_out[c, x] = v_pad[c, x, SIDE + EDGE : SIDE + rows - EDGE, :]
    for (c, i), k in index_v.items():
        halo_v[k] = halo_v[k] + DT * halo_b[index_b[i]] * own_share(s_pad, c, i, SIDE, rows)
    kept = slice(EDGE, rows - EDGE)
    base, fewer = SIDE + EDGE, rows - 2 * EDGE
    halo = lambda c, j: halo_v[index_v[c, j], kept, :]
    for x in range(cx):
        parts = strains(v_pad, halo, x, base, fewer, weights)
        materials[0] = with_strip(lam[x], strip(more_strips, 0, x, cx), sec)
        materials[1] = with_strip(mu[x], strip(more_strips, 1, x, cx), sec)
        changes = stress_change(materials[0, kept, :], materials[1, kept, :], parts)
        for c, change in enumerate(changes):
            s_out[c, x] = s_pad[c, x, base : base + fewer, :] + change

    def layer(kind, c, x):
        if kind == "s":
            return s_out[c, x, EDGE : EDGE + cy, :]
        old = v_out[c, x, EDGE : EDGE + cy, :]
        return old + DT * b[x] * force(s_out, c, x, EDGE, cy, weights)

    def edge(_, c, x, n):
        past = slice(EDGE + cy, EDGE + cy + n)
        return jnp.where(sec == 0, s_out[c, x, past, :], s_out[c, x, EDGE - n : EDGE, :])

    layers, edges = second_lists(cx)
    send_layers(odd, *layers, layer, pay_a, pay_b, 0)
    counts = [LAST_NEEDED] * len(edges[0])
    at = LAYERS * cy
    send(odd, sea[0], sea[1], pay_a, pay_b, at)
    send_thin(odd, edges, counts, edge, pay_a, pay_b, at + sea.shape[1])


def last_step(
    sea_rows,
    s,
    v,
    b,
    lam,
    mu,
    b_near,
    from_a,
    from_b,
    v_out,
    s_out,
    v_rows,
    b_rows,
    halo_s,
    halo_v,
    made,
    sems,
):
    odd, sec, _ = place()
    cx, cy, nz = b.shape
    weights = depth_weights(nz)
    rows = cy + 2 * LAST_NEEDED
    here = slice(SIDE - LAST_NEEDED, SIDE - LAST_NEEDED + rows)
    index_s, index_v = halo_stress(cx), halo_velocity(cx)
    layers, edges = second_lists(cx)
    own = received(odd, layers, [cy] * LAYERS, from_a, from_b, cx, 0)
    counts = [LAST_NEEDED] * len(edges[0])
    rest = received(odd, edges, counts, from_a, from_b, cx, LAYERS * cy + sea_rows)
    for key, k in index_s.items():
        put_layer(halo_s, k, own["s", *key](), rest["s", *key](), sec)
    for x in range(cx):
        part = slice(4 * cy + x * SIDE, 4 * cy + (x + 1) * SIDE)
        b_rows[...] = with_strip(b[x], b_near[part, :], sec)
        scale = DT * b_rows[here, :]
        for c in range(3):
            terms = halo_share(c, x, cx, lambda k, j: halo_s[index_s[k, j], here, :])
            new = v[c, x, here, :]
            v_rows[c, x, here, :] = new if terms is None else new + scale * terms
    copies = [pltpu.make_async_copy(v_rows.at[:, :, pl.ds(SIDE, cy), :], v_out, sems.at[cx])]
    copies[0].start()
    for (c, i), k in index_v.items():
        at = (i + 2 if i < 0 else i - cx + 2) * cy
        scale = DT * b_near[at : at + cy, :]
        halo_v[k] = own["v", c, i]() + scale * own_share(s, c, i, EDGE, cy)
    for x in range(cx):
        parts = strains(v_rows, lambda c, j: halo_v[index_v[c, j]], x, SIDE, cy, weights)
        for c, change in enumerate(stress_change(lam[x], mu[x], parts)):
            made[c, x] = s[c, x, EDGE : EDGE + cy, :] + change
        copies.append(pltpu.make_async_copy(made.at[:, x], s_out.at[:, x], sems.at[x]))
        copies[-1].start()
    return copies


def floor_line(left, right):
    rows = left.shape[0]
    row = lax.broadcasted_iota(jnp.int32, (rows, 2 * rows), 0)
    lane = lax.broadcasted_iota(jnp.int32, (rows, 2 * rows), 1)
    picked = jnp.where(lane == row, left[:, 0:1], 0.0)
    picked = jnp.where(lane == row + rows, right[:, 0:1], picked)
    return jnp.sum(picked, axis=0, keepdims=True)


def floor_parts(s, v, b, b_near, info, parts, v_part, b_rows):
    cx, cy, nz = b.shape
    weights = depth_weights(nz)
    _, sec, _ = place()
    own = slice(EDGE, EDGE + cy)
    first, rows = EDGE - LAST_NEEDED, cy + 2 * LAST_NEEDED
    here = slice(SIDE - LAST_NEEDED, SIDE - LAST_NEEDED + rows)
    for x in range(cx):
        part = slice(4 * cy + x * SIDE, 4 * cy + (x + 1) * SIDE)
        b_rows[...] = with_strip(b[x], b_near[part, :], sec)
        scale = DT * b_rows[here, :]
        for c in range(3):
            terms = force(s, c, x, first, rows, weights)
            v_part[c, x, here, :] = v[c, x, first : first + rows, :] + scale * terms
    layers = [v_part[2, x, SIDE : SIDE + cy, :] for x in range(cx)]
    lines = [floor_line(layers[x], layers[x + 1]) for x in range(0, cx, 2)]
    lines.append(floor_line(s[4, cx - 1, own, :], s[4, cx - 2, own, :]))
    lines.append(floor_line(s[4, 0, own, :], (-FAR * DT) * b[cx - 1]))
    lines.append(floor_line(DT * b[0], DT * b[1]))
    lines.append(info[...])
    row = lax.broadcasted_iota(jnp.int32, (SIDE, 2 * cy), 0)
    period = 3 * SIDE
    for k in range(0, period, SIDE):
        tiled = jnp.zeros((SIDE, 2 * cy), F32)
        for j in range(SIDE):
            tiled = jnp.where(row == j, lines[(k + j) % LINES], tiled)
        for at in range(k, parts.shape[0], period):
            parts[at : at + SIDE, :] = tiled


def column(line, first, count):
    wide = jnp.broadcast_to(line, (count, line.shape[1]))
    row = lax.broadcasted_iota(jnp.int32, wide.shape, 0)
    lane = lax.broadcasted_iota(jnp.int32, wide.shape, 1)
    return jnp.sum(jnp.where(lane == row + first, wide, 0.0), axis=1, keepdims=True)


def ocean_steps(
    start, from_a, from_b, near, state, depth, wet_ref, info, patches, ocean_out, ocean_ref, send_out
):
    odd, sec, tile = place()
    count = lax.axis_size("tile")
    rows, own = depth.shape
    columns = own + 128
    at = start
    for k in range(columns // 128):
        lanes = slice(k * 128, (k + 1) * 128)
        for f, n in enumerate(DEEP if k < own // 128 else CORNER):
            here = ocean_field(state, depth, wet_ref, near, f, k)
            a, b = from_a[at : at + n, :], from_b[at : at + n, :]
            low, high = jnp.where(odd, a, b), jnp.where(odd, b, a)
            ocean_ref[f, 0:SIDE, lanes] = jnp.zeros((SIDE, 128), F32)
            ocean_ref[f, SIDE + rows :, lanes] = jnp.zeros((SIDE, 128), F32)
            ocean_ref[f, SIDE - n : SIDE, lanes] = low
            ocean_ref[f, SIDE : SIDE + rows, lanes] = here
            ocean_ref[f, SIDE + rows : SIDE + rows + n, lanes] = high
            at += n

    total = rows + 2 * SIDE
    lane = lax.broadcasted_iota(jnp.int32, (1, columns), 1)
    ahead = jnp.where((lane == own - 1) & (sec == 1), 0.0, 0.5).astype(F32)
    behind = jnp.where((lane == 0) & (sec == 0), 0.0, 0.5).astype(F32)
    line = lax.broadcasted_iota(jnp.int32, (total, 1), 0)
    inside = ((line >= SIDE) | (tile > 0)) & ((line < SIDE + rows) | (tile < count - 1))
    inside = inside.astype(F32)

    def across(f):
        return pltpu.roll(f, columns - 1, 1) * ahead - pltpu.roll(f, 1, 1) * behind

    def down(f):
        return 0.5 * (pltpu.roll(f, total - 1, 0) - pltpu.roll(f, 1, 0))

    eta, u, v_sea = ocean_ref[0], ocean_ref[1], ocean_ref[2]
    depth, wet = ocean_ref[3], ocean_ref[4]
    window = min(WINDOW, count)
    base = jnp.clip(tile - REACH - 1, 0, count - window)

    def told(half, k):
        return patches[pl.ds((half * count + k) * LINES, LINES), :]

    below = told(sec, jnp.maximum(tile - 1, 0))[5:6]
    above = told(sec, jnp.minimum(tile + 1, count - 1))[5:6]
    line = info[...]
    marks = [
        jnp.concatenate(
            [
                column(below, k * rows + rows - SIDE, SIDE),
                column(line, k * rows, rows),
                column(above, k * rows, SIDE),
            ],
            axis=0,
        )
        for k in range(2)
    ]
    owner = jnp.broadcast_to(marks[0] - base.astype(F32), (total, 128))
    share = marks[1]
    width = own // 4
    left = lax.broadcasted_iota(jnp.int32, (1, 128), 1) < width
    near = jnp.where(left, -NEAR, FAR).astype(F32)
    far = jnp.where(left, FAR, 0.0).astype(F32)
    uplift = []
    for half in (sec, 1 - sec):
        tiles = []
        for k in range(-1, window + 1):
            here = jnp.clip(base + k, 0, count - 1)
            there = (here == base + k).astype(F32)
            tiles.append(told(half, here) * there)
        levels = [jnp.zeros((total, 128), F32) for _ in range(2)]
        for k in range(window):
            below, this, above = tiles[k], tiles[k + 1], tiles[k + 2]
            last = pltpu.roll(below[2:3], width, 1)
            last = near * jnp.where(left, below[2:3], last) + far * last
            first = this[0:1] + this[4:5] * last
            second = this[1:2] + jnp.where(left, 0.0, this[3:4]) * pltpu.roll(above[3:4], width, 1)
            mine = owner == float(k)
            levels = [jnp.where(mine, q, level) for q, level in zip((first, second), levels)]
        uplift.append(levels)
    uplift = uplift[0] + [jnp.where(sec == 0, uplift[1][0], uplift[1][1])]
    uplift = jnp.concatenate(uplift, axis=1)
    lift = ODT * (share * wet * uplift)
    part = slice(SIDE, SIDE + rows)
    for step in range(2):
        u = wet * (u - ODT * down(eta))
        v_sea = wet * (v_sea - ODT * across(eta))
        if step == 1:
            ocean_out[1] = u[part, :own]
            ocean_out[2] = v_sea[part, :own]
            send_out(slice(1, 3))
        eta = inside * (eta - ODT * (down(depth * u) + across(depth * v_sea)) + lift)
    ocean_out[0] = eta[part, :own]
    send_out(slice(0, 1))


def finish(
    sea_rows,
    s,
    v,
    b,
    lam,
    mu,
    b_near,
    from_a,
    from_b,
    near,
    state,
    depth,
    wet,
    info,
    patches,
    v_out,
    s_out,
    ocean_out,
    v_rows,
    b_rows,
    halo_s,
    halo_v,
    made,
    ocean_ref,
    ocean_made,
    sems,
    ocean_sems,
):
    cx, cy, _ = b.shape
    copies = last_step(
        sea_rows,
        s,
        v,
        b,
        lam,
        mu,
        b_near,
        from_a,
        from_b,
        v_out,
        s_out,
        v_rows,
        b_rows,
        halo_s,
        halo_v,
        made,
        sems,
    )

    def send_out(part):
        size = part.stop - part.start
        here = (pl.ds(part.start, size),)
        copies.append(
            pltpu.make_async_copy(
                ocean_made.at[here], ocean_out.at[here], ocean_sems.at[part.start]
            )
        )
        copies[-1].start()

    ocean_steps(
        LAYERS * cy,
        from_a,
        from_b,
        near,
        state,
        depth,
        wet,
        info,
        patches,
        ocean_made,
        ocean_ref,
        send_out,
    )
    for copy in copies:
        copy.wait()


VMEM = pl.BlockSpec(memory_space=pltpu.VMEM)
ANY = pl.BlockSpec(memory_space=pl.ANY)


def call(body, name, outs, scratch, operands, weight=1, ins=VMEM, where=VMEM, grant=8):
    shapes = [jax.ShapeDtypeStruct(o, F32) for o in outs]
    moved = sum(o.size for o in operands) * 4 + sum(o.size for o in shapes) * 4
    return pl.pallas_call(
        body,
        name=name,
        out_shape=shapes,
        in_specs=ins if isinstance(ins, list) else [ins] * len(operands),
        out_specs=where if isinstance(where, list) else [where] * len(outs),
        scratch_shapes=scratch,
        compiler_params=pltpu.CompilerParams(vmem_limit_bytes=int(grant * 1024 * 1024)),
        cost_estimate=pl.CostEstimate(
            flops=moved * weight, bytes_accessed=moved * weight, transcendentals=0
        ),
    )(*operands)


def exchange(pay_a, pay_b, count):
    def swap(pay, first):
        pairs = []
        for i in range(first, count - 1, 2):
            pairs += [(i, i + 1), (i + 1, i)]
        return lax.ppermute(pay, "tile", pairs)

    from_a = swap(pay_a, 0)
    return from_a, swap(pay_b, 1)


def across(pay):
    return lax.ppermute(pay, "sec", [(0, 1), (1, 0)])


def shards(
    velocity,
    stresses,
    buoyancy,
    lame_first,
    shear_mod,
    ocean_state,
    depth_map,
    wet_mask,
    intersection_src,
    intersection_share,
):
    count = lax.axis_size("tile")
    sec = lax.axis_index("sec")
    _, cx, cy, nz = stresses.shape
    _, rows, columns = ocean_state.shape
    tall = cy + 2 * SIDE
    halo = pltpu.VMEM((LAYERS, tall, nz), F32)

    first = ((LAYERS + 2) // 2 + 1) * cy
    pay_a, pay_b, edges = call(
        opening,
        "opening",
        [(first, nz), (first, nz), (10, cx, SIDE, nz)],
        [pltpu.SemaphoreType.DMA((10 + 2 * (first // cy),))],
        [stresses, velocity, buoyancy],
        ins=ANY,
        grant=60,
    )
    strips = across(edges.reshape(10 * cx * SIDE, nz))
    early_a, early_b = exchange(pay_a, pay_b, count)
    early_list, late_list = first_lists(cx)
    per = columns // 128 * sum(DEEP) + sum(CORNER)
    late = len(late_list[0]) * cy + sum(thin_counts(early_list) + thin_counts(late_list))
    pay_a, pay_b, stresses, velocity = call(
        first_round,
        "first_round",
        [(late, nz), (late, nz), (6, cx, tall + 2 * SIDE, nz), (3, cx, tall, nz)],
        [],
        [stresses, velocity, buoyancy, strips],
    )
    late_a, late_b = exchange(pay_a, pay_b, count)

    source, share, lame, shear, _ = lax.optimization_barrier(
        (intersection_src, intersection_share, lame_first, shear_mod, early_b)
    )
    ocean_state, depth_map, wet_mask, _ = lax.optimization_barrier(
        (ocean_state, depth_map, wet_mask, early_a)
    )
    (edges,) = call(edge_rows, "edge_rows", [(2 * cx * SIDE, nz)], [], [lame, shear])
    more_strips = across(edges)
    sea = [ocean_state, depth_map, wet_mask]
    (near,) = call(near_columns, "near_columns", [(len(DEEP) * rows, 128)], [], sea)
    near = across(near)
    (edges,) = call(ocean_edges, "ocean_edges", [(2, per, 128)], [], sea + [near])
    info = jnp.concatenate([source.astype(F32), share])[None]

    second = (LAYERS * cy + per + 5 * LAST_NEEDED, nz)
    velocity, stresses, pay_a, pay_b, b_near = call(
        whole_step,
        "whole_step",
        [(3, cx, cy + 2 * EDGE, nz), (6, cx, cy + 2 * EDGE, nz), second, second]
        + [(4 * cy + cx * SIDE, nz)],
        [
            pltpu.VMEM((3, cx, tall + 2 * SIDE, nz), F32),
            halo,
            halo,
            pltpu.VMEM((4, tall, nz), F32),
            pltpu.VMEM((2, tall, nz), F32),
        ],
        [stresses, velocity, buoyancy, lame_first, shear_mod, strips, more_strips]
        + [early_a, early_b, late_a, late_b, edges],
    )
    from_a, from_b = exchange(pay_a, pay_b, count)
    parts, velocity = call(
        floor_parts,
        "floor_parts",
        [(2 * count * LINES, 2 * cy), (3, cx, tall, nz)],
        [pltpu.VMEM((tall, nz), F32)],
        [stresses, velocity, buoyancy, b_near, info],
    )
    parts = parts.reshape(2 * count * LINES // 2, 2, 2 * cy)
    patches = lax.all_to_all(parts, ("sec", "tile"), 0, 0, tiled=True).reshape(-1, 2 * cy)
    velocity, stresses, ocean_state = call(
        functools.partial(finish, per),
        "finish",
        [(3, cx, cy, nz), (6, cx, cy, nz), ocean_state.shape],
        [
            pltpu.VMEM((3, cx, tall, nz), F32),
            pltpu.VMEM((tall, nz), F32),
            halo,
            pltpu.VMEM((LAYERS, cy, nz), F32),
            pltpu.VMEM((6, cx, cy, nz), F32),
            pltpu.VMEM((len(DEEP), rows + 2 * SIDE, columns + 128), F32),
            pltpu.VMEM(ocean_state.shape, F32),
            pltpu.SemaphoreType.DMA((cx + 1,)),
            pltpu.SemaphoreType.DMA((2,)),
        ],
        [stresses, velocity, buoyancy, lame_first, shear_mod, b_near]
        + [from_a, from_b, near] + sea + [info, patches],
        where=ANY,
    )
    return velocity, stresses, ocean_state


def solution(mesh):
    cube = P("tile", "sec", None)
    return jax.shard_map(
        shards,
        mesh=mesh,
        in_specs=(
            P(None, "tile", "sec", None),
            P(None, "tile", "sec", None),
            cube,
            cube,
            cube,
            P(None, "tile", "sec"),
            P("tile", "sec"),
            P("tile", "sec"),
            P("tile"),
            P("tile"),
        ),
        out_specs=(
            P(None, "tile", "sec", None),
            P(None, "tile", "sec", None),
            P(None, "tile", "sec"),
        ),
        check_vma=False,
    )
```

```python
import functools

import jax
import jax.numpy as jnp
from jax import lax
from jax.experimental import pallas as pl
from jax.experimental.pallas import tpu as pltpu
from jax.sharding import PartitionSpec as P

REACH = 2
NEAR = 9.0 / 8.0
FAR = 1.0 / 24.0
DT = 0.15
ODT = 0.3
F32 = jnp.float32
EDGE = 4
SIDE = 8
WINDOW = 8
DEEP = (4, 3, 2, 3, 3)
CORNER = (2, 1, 2, 2, 2)
LINES = 6
NEEDED = {"s": 5, "v": 3, "b": 3}
LAST_NEEDED = 2
LAYERS = 9
STRESS_X = ((0, True), (3, False), (4, False))


def depth_weights(width):
    lane = lax.broadcasted_iota(jnp.int32, (1, width), 1)

    def weight(value, first, last):
        return jnp.where((lane >= first) & (lane < last), value, 0.0).astype(F32)

    forward = (weight(NEAR, 0, width - 1), weight(-FAR, 0, width - 2), weight(FAR, 1, width))
    backward = (weight(-NEAR, 1, width), weight(-FAR, 0, width - 1), weight(FAR, 2, width))
    return forward, backward


def forward_z(f, weights):
    near, far, behind = weights
    n = f.shape[-1]
    return (
        pltpu.roll(f, n - 1, 1) * near
        - NEAR * f
        + pltpu.roll(f, n - 2, 1) * far
        + pltpu.roll(f, 1, 1) * behind
    )


def backward_z(f, weights):
    near, far, behind = weights
    n = f.shape[-1]
    return (
        NEAR * f
        + pltpu.roll(f, 1, 1) * near
        + pltpu.roll(f, n - 1, 1) * far
        + pltpu.roll(f, 2, 1) * behind
    )


def forward(at, i):
    return NEAR * (at(i + 1) - at(i)) - FAR * (at(i + 2) - at(i - 1))


def backward(at, i):
    return NEAR * (at(i) - at(i - 1)) - FAR * (at(i + 1) - at(i - 2))


def rounded(rows):
    return -(-rows // 8) * 8


def place():
    tile, sec = lax.axis_index("tile"), lax.axis_index("sec")
    return lax.rem(tile, 2) == 1, sec, tile


def along_x(ahead, i, get):
    if ahead:
        taps = ((i + 1, NEAR), (i, -NEAR), (i + 2, -FAR), (i - 1, FAR))
    else:
        taps = ((i, NEAR), (i - 1, -NEAR), (i + 1, -FAR), (i - 2, FAR))
    total = None
    for j, weight in taps:
        layer = get(j)
        if layer is not None:
            total = weight * layer if total is None else total + weight * layer
    return total


def up_layers(cx):
    stress = [(0, cx - 1), (3, cx - 2), (3, cx - 1), (4, cx - 2), (4, cx - 1)]
    return stress, [(0, cx - 2), (0, cx - 1), (1, cx - 1), (2, cx - 1)]


def down_layers(cx):
    return [(0, 0), (0, 1), (3, 0), (4, 0)], [(0, 0), (1, 0), (1, 1), (2, 0), (2, 1)]


def halo_stress(cx):
    low = [(c, x - cx) for c, x in up_layers(cx)[0]]
    return {key: k for k, key in enumerate(low + [(c, x + cx) for c, x in down_layers(cx)[0]])}


def halo_velocity(cx):
    low = [(c, x - cx) for c, x in up_layers(cx)[1]]
    return {key: k for k, key in enumerate(low + [(c, x + cx) for c, x in down_layers(cx)[1]])}


def strip(ref, k, x, cx):
    return ref[(k * cx + x) * SIDE : (k * cx + x + 1) * SIDE, :]


def with_strip(own, edge, sec):
    return jnp.concatenate(
        [jnp.where(sec == 1, edge, 0.0), own, jnp.where(sec == 0, edge, 0.0)], axis=0
    )


def yz_terms(s, comp, x, base, rows, weights):
    fw, bw = weights
    here = slice(base, base + rows)

    def beside(c):
        return lambda shift: s[c, x, base + shift : base + shift + rows, :]

    if comp == 0:
        return backward(beside(3), 0) + backward_z(s[4, x, here, :], bw)
    if comp == 1:
        return forward(beside(1), 0) + backward_z(s[5, x, here, :], bw)
    return backward(beside(5), 0) + forward_z(s[2, x, here, :], fw)


def force(s, comp, x, base, rows, weights, halo=None):
    source, ahead = STRESS_X[comp]
    cx = s.shape[1]

    def get(j):
        if 0 <= j < cx:
            return s[source, j, base : base + rows, :]
        return None if halo is None else halo(source, j)

    return along_x(ahead, x, get) + yz_terms(s, comp, x, base, rows, weights)


def halo_share(comp, x, cx, halo):
    source, ahead = STRESS_X[comp]
    return along_x(ahead, x, lambda j: None if 0 <= j < cx else halo(source, j))


def own_share(s, comp, i, base, rows):
    source, ahead = STRESS_X[comp]
    cx = s.shape[1]
    return along_x(
        ahead, i, lambda j: s[source, j, base : base + rows, :] if 0 <= j < cx else None
    )


def load_stress(s, strips, s_pad, sec):
    comps, cx, cy, nz = s.shape
    nothing = jnp.zeros((SIDE, nz), F32)
    for c in range(comps):
        for x in range(cx):
            s_pad[c, x, 0:SIDE, :] = nothing
            s_pad[c, x, SIDE : 3 * SIDE + cy, :] = with_strip(s[c, x], strip(strips, c, x, cx), sec)
            s_pad[c, x, 3 * SIDE + cy :, :] = nothing


def send(odd, upper, lower, pay_a, pay_b, at):
    part = slice(at, at + upper.shape[0])
    pay_a[part, :] = jnp.where(odd, lower, upper)
    pay_b[part, :] = jnp.where(odd, upper, lower)


def send_layers(odd, up, down, layer, pay_a, pay_b, at):
    for k, (upper, lower) in enumerate(zip(up, down)):
        rows = layer(*upper)
        send(odd, rows, layer(*lower), pay_a, pay_b, at)
        at += rows.shape[0]


def first_lists(cx):
    (up_s, up_v), (down_s, down_v) = up_layers(cx), down_layers(cx)
    up_s, down_s = [("s", *key) for key in up_s], [("s", *key) for key in down_s]
    up_v, down_v = [("v", *key) for key in up_v], [("v", *key) for key in down_v]
    early = up_s + [("b", 0, cx - 1)], down_s + [("b", 0, 0), ("b", 0, 1)]
    late = up_v + [("b", 0, cx - 2)], down_v
    return early, late


def second_lists(cx):
    (up_s, up_v), (down_s, down_v) = up_layers(cx), down_layers(cx)
    up_s, down_s = [("s", *key) for key in up_s], [("s", *key) for key in down_s]
    up = up_s + [("v", *key) for key in up_v]
    return (up, down_s + [("v", *key) for key in down_v]), (up_s, down_s + down_s[-1:])


def thin_counts(lists):
    return [max(NEEDED[upper[0]], NEEDED[lower[0]]) for upper, lower in zip(*lists)]


def send_thin(odd, lists, counts, edge, pay_a, pay_b, at):
    for upper, lower, n in zip(*lists, counts):

        send(odd, edge(*upper, n), edge(*lower, n), pay_a, pay_b, at)
        at += n


def received(odd, lists, counts, pay_a, pay_b, cx, at):
    found = {}
    for upper, lower, n in zip(*lists, counts):
        part = slice(at, at + n)
        at += n
        for kind, c, x, below in ((*upper, True), (*lower, False)):

            def get(part=part, below=below):
                a, b = pay_a[part, :], pay_b[part, :]
                return jnp.where(odd, a, b) if below else jnp.where(odd, b, a)

            found[kind, c, x - cx if below else x + cx] = get
    return found


def put_layer(ref, k, own, thin, sec):
    cy, nz = own.shape
    n = thin.shape[0]
    ref[k, 0:SIDE, :] = jnp.zeros((SIDE, nz), F32)
    ref[k, SIDE : SIDE + cy, :] = own
    ref[k, SIDE + cy :, :] = jnp.zeros((SIDE, nz), F32)
    ref[k, SIDE - n : SIDE, :] = jnp.where(sec == 1, thin, 0.0)
    ref[k, SIDE + cy : SIDE + cy + n, :] = jnp.where(sec == 0, thin, 0.0)


def strains(velocity, halo, x, base, rows, weights):
    fw, bw = weights
    cx = velocity.shape[1]

    def layers(c):
        def get(j):
            if 0 <= j < cx:
                return velocity[c, j, base : base + rows, :]
            return halo(c, j)

        return get

    def beside(c):
        return lambda shift: velocity[c, x, base + shift : base + shift + rows, :]

    vx, vy, vz = (velocity[c, x, base : base + rows, :] for c in range(3))
    return (
        along_x(False, x, layers(0)),
        backward(beside(1), 0),
        backward_z(vz, bw),
        forward(beside(0), 0) + along_x(True, x, layers(1)),
        forward_z(vx, fw) + along_x(True, x, layers(2)),
        forward_z(vy, fw) + forward(beside(2), 0),
    )


def stress_change(lam, mu, parts):
    exx, eyy, ezz, xy, xz, yz = parts
    shear = DT * mu
    volume = (DT * lam) * (exx + eyy + ezz)
    double = 2.0 * shear
    return (
        volume + double * exx,
        volume + double * eyy,
        volume + double * ezz,
        shear * xy,
        shear * xz,
        shear * yz,
    )


def edge_rows(*refs):
    *fields, out = refs
    _, sec, _ = place()
    at = 0
    for field in fields:
        flat = field if len(field.shape) == 4 else None
        for c in range(field.shape[0] if flat is not None else 1):
            layers = field.shape[-3]
            for x in range(layers):
                rows = field[c, x] if flat is not None else field[x]
                out[at : at + SIDE, :] = jnp.where(sec == 0, rows[-SIDE:], rows[:SIDE])
                at += SIDE


def opening(s, v, b, pay_a, pay_b, edges, sems):
    odd, sec, _ = place()
    cx, cy, _ = b.shape
    up, down = first_lists(cx)[0]
    begin = pl.multiple_of(jnp.where(sec == 0, cy - SIDE, 0), SIDE)
    rows = [s.at[c, :, pl.ds(begin, SIDE), :] for c in range(6)]
    rows += [v.at[c, :, pl.ds(begin, SIDE), :] for c in range(3)]
    rows.append(b.at[:, pl.ds(begin, SIDE), :])
    rows = [pltpu.make_async_copy(r, edges.at[k], sems.at[k]) for k, r in enumerate(rows)]

    def run(above, below):
        copies = []
        for pay, layers in ((above, up), (below, down)):
            for k, (kind, c, x) in enumerate(layers):
                source = s.at[c, x] if kind == "s" else b.at[x]
                sem = sems.at[len(rows) + len(copies)]
                copies.append(pltpu.make_async_copy(source, pay.at[pl.ds(k * cy, cy)], sem))
        for copy in copies + rows:
            copy.start()
        for copy in copies:
            copy.wait()

    @pl.when(odd)
    def _():
        run(pay_b, pay_a)

    @pl.when(jnp.logical_not(odd))
    def _():
        run(pay_a, pay_b)

    for copy in rows:
        copy.wait()


def near_columns(state, depth, wet, out):
    _, sec, _ = place()
    rows, own = depth.shape
    for k, field in enumerate((state.at[0], state.at[1], state.at[2], depth, wet)):
        near = jnp.where(sec == 0, field[:, own - 128 :], field[:, :128])
        out[k * rows : (k + 1) * rows, :] = near.astype(F32)


def ocean_field(state, depth, wet, near, f, k):
    rows, own = depth.shape
    if k == own // 128:
        return near[f * rows : (f + 1) * rows, :]
    field = state.at[f] if f < 3 else depth if f == 3 else wet
    return field[:, k * 128 : (k + 1) * 128].astype(F32)


def ocean_edges(state, depth, wet, near, edges):
    rows, own = depth.shape
    at = 0
    for k in range(own // 128 + 1):
        for f, n in enumerate(DEEP if k < own // 128 else CORNER):
            field = ocean_field(state, depth, wet, near, f, k)
            edges[0, at : at + n, :] = field[rows - n :]
            edges[1, at : at + n, :] = field[:n]
            at += n


def first_round(s, v, b, strips, pay_a, pay_b, s_pad, v_part):
    odd, sec, _ = place()
    _, cx, cy, nz = s.shape
    weights = depth_weights(nz)
    rows = cy + 2 * SIDE
    load_stress(s, strips, s_pad, sec)
    for x in range(cx):
        scale = DT * with_strip(b[x], strip(strips, 9, x, cx), sec)
        for c in range(3):
            old = with_strip(v[c, x], strip(strips, 6 + c, x, cx), sec)
            v_part[c, x] = old + scale * force(s_pad, c, x, SIDE, rows, weights)

    def layer(kind, c, x):
        return v_part[c, x, SIDE : SIDE + cy, :] if kind == "v" else b[x]

    def edge(kind, c, x, n):
        if kind == "v":
            past = slice(SIDE + cy, SIDE + cy + n)
            return jnp.where(sec == 0, v_part[c, x, past, :], v_part[c, x, SIDE - n : SIDE, :])
        whole = strip(strips, c if kind == "s" else 9, x, cx)
        return jnp.where(sec == 0, whole[:n], whole[SIDE - n :])

    early, late = first_lists(cx)
    pay_a[-8:, :] = pay_b[-8:, :] = jnp.zeros((8, nz), F32)
    send_layers(odd, *late, layer, pay_a, pay_b, 0)
    at = len(late[0]) * cy
    for lists in (early, late):
        counts = thin_counts(lists)
        send_thin(odd, lists, counts, edge, pay_a, pay_b, at)
        at += sum(counts)


def first_received(odd, cx, cy, early_a, early_b, late_a, late_b):
    early, late = first_lists(cx)
    own = received(odd, early, [cy] * len(early[0]), early_a, early_b, cx, 0)
    own.update(received(odd, late, [cy] * len(late[0]), late_a, late_b, cx, 0))
    at = len(late[0]) * cy
    rest = received(odd, early, thin_counts(early), late_a, late_b, cx, at)
    at += sum(thin_counts(early))
    rest.update(received(odd, late, thin_counts(late), late_a, late_b, cx, at))
    return own, rest


def whole_step(
    sea_rows,
    s_pad,
    v_part,
    b,
    lam,
    mu,
    strips,
    more_strips,
    early_a,
    early_b,
    late_a,
    late_b,
    sea,
    v_out,
    s_out,
    pay_a,
    pay_b,
    b_near,
    v_pad,
    halo_s,
    halo_v,
    halo_b,
    materials,
):
    odd, sec, _ = place()
    cx, cy, nz = b.shape
    weights = depth_weights(nz)
    rows = cy + 2 * SIDE
    index_s, index_v = halo_stress(cx), halo_velocity(cx)
    own, rest = first_received(odd, cx, cy, early_a, early_b, late_a, late_b)
    for key, k in index_s.items():
        put_layer(halo_s, k, own["s", *key](), rest["s", *key](), sec)
    for key, k in index_v.items():
        put_layer(halo_v, k, own["v", *key](), rest["v", *key](), sec)
    index_b = {i: k for k, i in enumerate((-2, -1, cx, cx + 1))}
    for i, k in index_b.items():
        put_layer(halo_b, k, own["b", 0, i](), rest["b", 0, i](), sec)
        b_near[k * cy : (k + 1) * cy, :] = own["b", 0, i]()
    for x in range(cx):
        part = slice(4 * cy + x * SIDE, 4 * cy + (x + 1) * SIDE)
        b_near[part, :] = strip(strips, 9, x, cx)
    nothing = jnp.zeros((SIDE, nz), F32)
    for x in range(cx):
        scale = DT * with_strip(b[x], strip(strips, 9, x, cx), sec)
        for c in range(3):
            new = v_part[c, x]
            terms = halo_share(c, x, cx, lambda k, j: halo_s[index_s[k, j]])
            if terms is not None:
                new = new + scale * terms
            v_pad[c, x, 0:SIDE, :] = nothing
            v_pad[c, x, SIDE : SIDE + rows, :] = new
            v_pad[c, x, SIDE + rows :, :] = nothing
            v_out[c, x, 0 : rows - 2 * EDGE, :] = v_pad[c, x, SIDE + EDGE : SIDE + rows - EDGE, :]
            v_out[c, x, rows - 2 * EDGE :, :] = nothing
    for (c, i), k in index_v.items():
        halo_v[k] = halo_v[k] + DT * halo_b[index_b[i]] * own_share(s_pad, c, i, SIDE, rows)
    kept = slice(EDGE, rows - EDGE)
    base, fewer = SIDE + EDGE, rows - 2 * EDGE
    halo = lambda c, j: halo_v[index_v[c, j], kept, :]
    for x in range(cx):
        parts = strains(v_pad, halo, x, base, fewer, weights)
        materials[0] = with_strip(lam[x], strip(more_strips, 0, x, cx), sec)
        materials[1] = with_strip(mu[x], strip(more_strips, 1, x, cx), sec)
        changes = stress_change(materials[0, kept, :], materials[1, kept, :], parts)
        for c, change in enumerate(changes):
            s_out[c, x, 0:fewer, :] = s_pad[c, x, base : base + fewer, :] + change
            s_out[c, x, fewer:, :] = nothing

    def layer(kind, c, x):
        if kind == "s":
            return s_out[c, x, EDGE : EDGE + cy, :]
        old = v_out[c, x, EDGE : EDGE + cy, :]
        return old + DT * b[x] * force(s_out, c, x, EDGE, cy, weights)

    def edge(_, c, x, n):
        past = slice(EDGE + cy, EDGE + cy + n)
        return jnp.where(sec == 0, s_out[c, x, past, :], s_out[c, x, EDGE - n : EDGE, :])

    layers, edges = second_lists(cx)
    pay_a[-8:, :] = pay_b[-8:, :] = jnp.zeros((8, nz), F32)
    send_layers(odd, *layers, layer, pay_a, pay_b, 0)
    counts = [LAST_NEEDED] * len(edges[0])
    at = LAYERS * cy
    send(odd, sea[0, :sea_rows], sea[1, :sea_rows], pay_a, pay_b, at)
    send_thin(odd, edges, counts, edge, pay_a, pay_b, at + sea_rows)


def last_step(
    sea_rows,
    s,
    v,
    b,
    lam,
    mu,
    b_near,
    from_a,
    from_b,
    v_out,
    s_out,
    v_rows,
    b_rows,
    halo_s,
    halo_v,
    made,
    sems,
):
    odd, sec, _ = place()
    cx, cy, nz = b.shape
    weights = depth_weights(nz)
    rows = cy + 2 * LAST_NEEDED
    here = slice(SIDE - LAST_NEEDED, SIDE - LAST_NEEDED + rows)
    index_s, index_v = halo_stress(cx), halo_velocity(cx)
    layers, edges = second_lists(cx)
    own = received(odd, layers, [cy] * LAYERS, from_a, from_b, cx, 0)
    counts = [LAST_NEEDED] * len(edges[0])
    rest = received(odd, edges, counts, from_a, from_b, cx, LAYERS * cy + sea_rows)
    for key, k in index_s.items():
        put_layer(halo_s, k, own["s", *key](), rest["s", *key](), sec)
    for x in range(cx):
        part = slice(4 * cy + x * SIDE, 4 * cy + (x + 1) * SIDE)
        b_rows[...] = with_strip(b[x], b_near[part, :], sec)
        scale = DT * b_rows[here, :]
        for c in range(3):
            terms = halo_share(c, x, cx, lambda k, j: halo_s[index_s[k, j], here, :])
            new = v[c, x, here, :]
            v_rows[c, x, here, :] = new if terms is None else new + scale * terms
    copies = [pltpu.make_async_copy(v_rows.at[:, :, pl.ds(SIDE, cy), :], v_out, sems.at[cx])]
    copies[0].start()
    for (c, i), k in index_v.items():
        at = (i + 2 if i < 0 else i - cx + 2) * cy
        scale = DT * b_near[at : at + cy, :]
        halo_v[k] = own["v", c, i]() + scale * own_share(s, c, i, EDGE, cy)
    for x in range(cx):
        parts = strains(v_rows, lambda c, j: halo_v[index_v[c, j]], x, SIDE, cy, weights)
        for c, change in enumerate(stress_change(lam[x], mu[x], parts)):
            made[c, x] = s[c, x, EDGE : EDGE + cy, :] + change
        copies.append(pltpu.make_async_copy(made.at[:, x], s_out.at[:, x], sems.at[x]))
        copies[-1].start()
    return copies


def floor_line(left, right):
    rows = left.shape[0]
    row = lax.broadcasted_iota(jnp.int32, (rows, 2 * rows), 0)
    lane = lax.broadcasted_iota(jnp.int32, (rows, 2 * rows), 1)
    picked = jnp.where(lane == row, left[:, 0:1], 0.0)
    picked = jnp.where(lane == row + rows, right[:, 0:1], picked)
    return jnp.sum(picked, axis=0, keepdims=True)


def floor_parts(s, v, b, b_near, info, parts, v_part, b_rows):
    cx, cy, nz = b.shape
    weights = depth_weights(nz)
    _, sec, _ = place()
    own = slice(EDGE, EDGE + cy)
    first, rows = EDGE - LAST_NEEDED, cy + 2 * LAST_NEEDED
    here = slice(SIDE - LAST_NEEDED, SIDE - LAST_NEEDED + rows)
    for x in range(cx):
        part = slice(4 * cy + x * SIDE, 4 * cy + (x + 1) * SIDE)
        b_rows[...] = with_strip(b[x], b_near[part, :], sec)
        scale = DT * b_rows[here, :]
        for c in range(3):
            terms = force(s, c, x, first, rows, weights)
            v_part[c, x, here, :] = v[c, x, first : first + rows, :] + scale * terms
    layers = [v_part[2, x, SIDE : SIDE + cy, :] for x in range(cx)]
    lines = [floor_line(layers[x], layers[x + 1]) for x in range(0, cx, 2)]
    lines.append(floor_line(s[4, cx - 1, own, :], s[4, cx - 2, own, :]))
    lines.append(floor_line(s[4, 0, own, :], (-FAR * DT) * b[cx - 1]))
    lines.append(floor_line(DT * b[0], DT * b[1]))
    lines.append(info[...])
    row = lax.broadcasted_iota(jnp.int32, (SIDE, 2 * cy), 0)
    period = 3 * SIDE
    for k in range(0, period, SIDE):
        tiled = jnp.zeros((SIDE, 2 * cy), F32)
        for j in range(SIDE):
            tiled = jnp.where(row == j, lines[(k + j) % LINES], tiled)
        for at in range(k, parts.shape[0], period):
            parts[at : at + SIDE, :] = tiled


def column(line, first, count):
    wide = jnp.broadcast_to(line, (count, line.shape[1]))
    row = lax.broadcasted_iota(jnp.int32, wide.shape, 0)
    lane = lax.broadcasted_iota(jnp.int32, wide.shape, 1)
    return jnp.sum(jnp.where(lane == row + first, wide, 0.0), axis=1, keepdims=True)


def ocean_steps(
    start, from_a, from_b, near, state, depth, wet_ref, info, patches, ocean_out, ocean_ref, send_out, told_ref
):
    odd, sec, tile = place()
    count = lax.axis_size("tile")
    rows, own = depth.shape
    columns = own + 128
    at = start
    for k in range(columns // 128):
        lanes = slice(k * 128, (k + 1) * 128)
        for f, n in enumerate(DEEP if k < own // 128 else CORNER):
            here = ocean_field(state, depth, wet_ref, near, f, k)
            a, b = from_a[at : at + n, :], from_b[at : at + n, :]
            low, high = jnp.where(odd, a, b), jnp.where(odd, b, a)
            ocean_ref[f, 0:SIDE, lanes] = jnp.zeros((SIDE, 128), F32)
            ocean_ref[f, SIDE + rows :, lanes] = jnp.zeros((SIDE, 128), F32)
            ocean_ref[f, SIDE - n : SIDE, lanes] = low
            ocean_ref[f, SIDE : SIDE + rows, lanes] = here
            ocean_ref[f, SIDE + rows : SIDE + rows + n, lanes] = high
            at += n

    total = rows + 2 * SIDE
    lane = lax.broadcasted_iota(jnp.int32, (1, columns), 1)
    ahead = jnp.where((lane == own - 1) & (sec == 1), 0.0, 0.5).astype(F32)
    behind = jnp.where((lane == 0) & (sec == 0), 0.0, 0.5).astype(F32)
    line = lax.broadcasted_iota(jnp.int32, (total, 1), 0)
    inside = ((line >= SIDE) | (tile > 0)) & ((line < SIDE + rows) | (tile < count - 1))
    inside = inside.astype(F32)

    def across(f):
        return pltpu.roll(f, columns - 1, 1) * ahead - pltpu.roll(f, 1, 1) * behind

    def down(f):
        return 0.5 * (pltpu.roll(f, total - 1, 0) - pltpu.roll(f, 1, 0))

    eta, u, v_sea = ocean_ref[0], ocean_ref[1], ocean_ref[2]
    depth, wet = ocean_ref[3], ocean_ref[4]
    window = min(WINDOW, count)
    base = jnp.clip(tile - REACH - 1, 0, count - window)

    told_ref[0 : patches.shape[0], :] = patches[...]
    told_ref[patches.shape[0] :, :] = jnp.zeros((8, 128), F32)

    def told(half, k):
        return told_ref[pl.ds((half * count + k) * LINES, LINES), :]

    below = told(sec, jnp.maximum(tile - 1, 0))[5:6]
    above = told(sec, jnp.minimum(tile + 1, count - 1))[5:6]
    line = info[...]
    marks = [
        jnp.concatenate(
            [
                column(below, k * rows + rows - SIDE, SIDE),
                column(line, k * rows, rows),
                column(above, k * rows, SIDE),
            ],
            axis=0,
        )
        for k in range(2)
    ]
    owner = jnp.broadcast_to(marks[0] - base.astype(F32), (total, 128))
    share = marks[1]
    width = own // 4
    left = lax.broadcasted_iota(jnp.int32, (1, 128), 1) < width
    near = jnp.where(left, -NEAR, FAR).astype(F32)
    far = jnp.where(left, FAR, 0.0).astype(F32)
    uplift = []
    for half in (sec, 1 - sec):
        tiles = []
        for k in range(-1, window + 1):
            here = jnp.clip(base + k, 0, count - 1)
            there = (here == base + k).astype(F32)
            tiles.append(told(half, here) * there)
        levels = [jnp.zeros((total, 128), F32) for _ in range(2)]
        for k in range(window):
            below, this, above = tiles[k], tiles[k + 1], tiles[k + 2]
            last = pltpu.roll(below[2:3], width, 1)
            last = near * jnp.where(left, below[2:3], last) + far * last
            first = this[0:1] + this[4:5] * last
            second = this[1:2] + jnp.where(left, 0.0, this[3:4]) * pltpu.roll(above[3:4], width, 1)
            mine = owner == float(k)
            levels = [jnp.where(mine, q, level) for q, level in zip((first, second), levels)]
        uplift.append(levels)
    uplift = uplift[0] + [jnp.where(sec == 0, uplift[1][0], uplift[1][1])]
    uplift = jnp.concatenate(uplift, axis=1)
    lift = ODT * (share * wet * uplift)
    part = slice(SIDE, SIDE + rows)
    for step in range(2):
        u = wet * (u - ODT * down(eta))
        v_sea = wet * (v_sea - ODT * across(eta))
        if step == 1:
            ocean_out[1] = u[part, :own]
            ocean_out[2] = v_sea[part, :own]
            send_out(slice(1, 3))
        eta = inside * (eta - ODT * (down(depth * u) + across(depth * v_sea)) + lift)
    ocean_out[0] = eta[part, :own]
    send_out(slice(0, 1))


def finish(
    sea_rows,
    s,
    v,
    b,
    lam,
    mu,
    b_near,
    from_a,
    from_b,
    near,
    state,
    depth,
    wet,
    info,
    patches,
    v_out,
    s_out,
    ocean_out,
    v_rows,
    b_rows,
    halo_s,
    halo_v,
    made,
    ocean_ref,
    ocean_made,
    told_ref,
    sems,
    ocean_sems,
):
    cx, cy, _ = b.shape
    copies = last_step(
        sea_rows,
        s,
        v,
        b,
        lam,
        mu,
        b_near,
        from_a,
        from_b,
        v_out,
        s_out,
        v_rows,
        b_rows,
        halo_s,
        halo_v,
        made,
        sems,
    )

    def send_out(part):
        size = part.stop - part.start
        here = (pl.ds(part.start, size),)
        copies.append(
            pltpu.make_async_copy(
                ocean_made.at[here], ocean_out.at[here], ocean_sems.at[part.start]
            )
        )
        copies[-1].start()

    ocean_steps(
        LAYERS * cy,
        from_a,
        from_b,
        near,
        state,
        depth,
        wet,
        info,
        patches,
        ocean_made,
        ocean_ref,
        send_out,
        told_ref,
    )
    for copy in copies:
        copy.wait()


VMEM = pl.BlockSpec(memory_space=pltpu.VMEM)
ANY = pl.BlockSpec(memory_space=pl.ANY)


def call(body, name, outs, scratch, operands, weight=1, ins=VMEM, where=VMEM, grant=8):
    shapes = [jax.ShapeDtypeStruct(o, F32) for o in outs]
    moved = sum(o.size for o in operands) * 4 + sum(o.size for o in shapes) * 4
    return pl.pallas_call(
        body,
        name=name,
        out_shape=shapes,
        in_specs=ins if isinstance(ins, list) else [ins] * len(operands),
        out_specs=where if isinstance(where, list) else [where] * len(outs),
        scratch_shapes=scratch,
        compiler_params=pltpu.CompilerParams(vmem_limit_bytes=int(grant * 1024 * 1024)),
        cost_estimate=pl.CostEstimate(
            flops=moved * weight, bytes_accessed=moved * weight, transcendentals=0
        ),
    )(*operands)


def exchange(pay_a, pay_b, count):
    def swap(pay, first):
        pairs = []
        for i in range(first, count - 1, 2):
            pairs += [(i, i + 1), (i + 1, i)]
        return lax.ppermute(pay, "tile", pairs)

    from_a = swap(pay_a, 0)
    return from_a, swap(pay_b, 1)


def across(pay):
    return lax.ppermute(pay, "sec", [(0, 1), (1, 0)])


def shards(
    velocity,
    stresses,
    buoyancy,
    lame_first,
    shear_mod,
    ocean_state,
    depth_map,
    wet_mask,
    intersection_src,
    intersection_share,
):
    count = lax.axis_size("tile")
    sec = lax.axis_index("sec")
    _, cx, cy, nz = stresses.shape
    _, rows, columns = ocean_state.shape
    tall = cy + 2 * SIDE
    halo = pltpu.VMEM((LAYERS, tall, nz), F32)

    first = ((LAYERS + 2) // 2 + 1) * cy
    pay_a, pay_b, edges = call(
        opening,
        "opening",
        [(first, nz), (first, nz), (10, cx, SIDE, nz)],
        [pltpu.SemaphoreType.DMA((10 + 2 * (first // cy),))],
        [stresses, velocity, buoyancy],
        ins=ANY,
        grant=60,
    )
    strips = across(edges.reshape(10 * cx * SIDE, nz))
    early_a, early_b = exchange(pay_a, pay_b, count)
    early_list, late_list = first_lists(cx)
    per = columns // 128 * sum(DEEP) + sum(CORNER)
    late = len(late_list[0]) * cy + rounded(sum(thin_counts(early_list) + thin_counts(late_list)))
    pay_a, pay_b, stresses, velocity = call(
        first_round,
        "first_round",
        [(late, nz), (late, nz), (6, cx, tall + 2 * SIDE, nz), (3, cx, tall, nz)],
        [],
        [stresses, velocity, buoyancy, strips],
    )
    late_a, late_b = exchange(pay_a, pay_b, count)

    source, share, lame, shear, _ = lax.optimization_barrier(
        (intersection_src, intersection_share, lame_first, shear_mod, early_b)
    )
    ocean_state, depth_map, wet_mask, _ = lax.optimization_barrier(
        (ocean_state, depth_map, wet_mask, early_a)
    )
    (edges,) = call(edge_rows, "edge_rows", [(2 * cx * SIDE, nz)], [], [lame, shear])
    more_strips = across(edges)
    sea = [ocean_state, depth_map, wet_mask]
    (near,) = call(near_columns, "near_columns", [(len(DEEP) * rows, 128)], [], sea)
    near = across(near)
    (edges,) = call(ocean_edges, "ocean_edges", [(2, rounded(per) + 8, 128)], [], sea + [near])
    info = jnp.concatenate([source.astype(F32), share])[None]

    kept = cy + 2 * EDGE + 8
    second = (LAYERS * cy + rounded(per + 5 * LAST_NEEDED), nz)
    velocity, stresses, pay_a, pay_b, b_near = call(
        functools.partial(whole_step, per),
        "whole_step",
        [(3, cx, kept, nz), (6, cx, kept, nz), second, second]
        + [(4 * cy + cx * SIDE, nz)],
        [
            pltpu.VMEM((3, cx, tall + 2 * SIDE, nz), F32),
            halo,
            halo,
            pltpu.VMEM((4, tall, nz), F32),
            pltpu.VMEM((2, tall, nz), F32),
        ],
        [stresses, velocity, buoyancy, lame_first, shear_mod, strips, more_strips]
        + [early_a, early_b, late_a, late_b, edges],
    )
    from_a, from_b = exchange(pay_a, pay_b, count)
    parts, velocity = call(
        floor_parts,
        "floor_parts",
        [(2 * count * LINES, 2 * cy), (3, cx, tall, nz)],
        [pltpu.VMEM((tall, nz), F32)],
        [stresses, velocity, buoyancy, b_near, info],
    )
    parts = parts.reshape(2 * count * LINES // 2, 2, 2 * cy)
    patches = lax.all_to_all(parts, ("sec", "tile"), 0, 0, tiled=True).reshape(-1, 2 * cy)
    velocity, stresses, ocean_state = call(
        functools.partial(finish, per),
        "finish",
        [(3, cx, cy, nz), (6, cx, cy, nz), ocean_state.shape],
        [
            pltpu.VMEM((3, cx, tall, nz), F32),
            pltpu.VMEM((tall, nz), F32),
            halo,
            pltpu.VMEM((LAYERS, cy, nz), F32),
            pltpu.VMEM((6, cx, cy, nz), F32),
            pltpu.VMEM((len(DEEP), rows + 2 * SIDE, columns + 128), F32),
            pltpu.VMEM(ocean_state.shape, F32),
            pltpu.VMEM((2 * count * LINES + 8, 128), F32),
            pltpu.SemaphoreType.DMA((cx + 1,)),
            pltpu.SemaphoreType.DMA((2,)),
        ],
        [stresses, velocity, buoyancy, lame_first, shear_mod, b_near]
        + [from_a, from_b, near] + sea + [info, patches],
        where=ANY,
        grant=16,
    )
    return velocity, stresses, ocean_state


def solution(mesh):
    cube = P("tile", "sec", None)
    return jax.shard_map(
        shards,
        mesh=mesh,
        in_specs=(
            P(None, "tile", "sec", None),
            P(None, "tile", "sec", None),
            cube,
            cube,
            cube,
            P(None, "tile", "sec"),
            P("tile", "sec"),
            P("tile", "sec"),
            P("tile"),
            P("tile"),
        ),
        out_specs=(
            P(None, "tile", "sec", None),
            P(None, "tile", "sec", None),
            P(None, "tile", "sec"),
        ),
        check_vma=False,
    )
```

```python
import functools

import jax
import jax.numpy as jnp
from jax import lax
from jax.experimental import pallas as pl
from jax.experimental.pallas import tpu as pltpu
from jax.sharding import PartitionSpec as P

REACH = 2
NEAR = 9.0 / 8.0
FAR = 1.0 / 24.0
DT = 0.15
ODT = 0.3
F32 = jnp.float32
EDGE = 4
SIDE = 8
WINDOW = 8
DEEP = (4, 3, 2, 3, 3)
CORNER = (2, 1, 2, 2, 2)
LINES = 4
NEEDED = {"s": 5, "v": 3, "b": 3}
LAST_NEEDED = 2
LAYERS = 9
STRESS_X = ((0, True), (3, False), (4, False))


def depth_weights(width):
    lane = lax.broadcasted_iota(jnp.int32, (1, width), 1)

    def weight(value, first, last):
        return jnp.where((lane >= first) & (lane < last), value, 0.0).astype(F32)

    forward = (weight(NEAR, 0, width - 1), weight(-FAR, 0, width - 2), weight(FAR, 1, width))
    backward = (weight(-NEAR, 1, width), weight(-FAR, 0, width - 1), weight(FAR, 2, width))
    return forward, backward


def forward_z(f, weights):
    near, far, behind = weights
    n = f.shape[-1]
    return (
        pltpu.roll(f, n - 1, 1) * near
        - NEAR * f
        + pltpu.roll(f, n - 2, 1) * far
        + pltpu.roll(f, 1, 1) * behind
    )


def backward_z(f, weights):
    near, far, behind = weights
    n = f.shape[-1]
    return (
        NEAR * f
        + pltpu.roll(f, 1, 1) * near
        + pltpu.roll(f, n - 1, 1) * far
        + pltpu.roll(f, 2, 1) * behind
    )


def forward(at, i):
    return NEAR * (at(i + 1) - at(i)) - FAR * (at(i + 2) - at(i - 1))


def backward(at, i):
    return NEAR * (at(i) - at(i - 1)) - FAR * (at(i + 1) - at(i - 2))


def rounded(rows):
    return -(-rows // 8) * 8


def place():
    tile, sec = lax.axis_index("tile"), lax.axis_index("sec")
    return lax.rem(tile, 2) == 1, sec, tile


def along_x(ahead, i, get):
    if ahead:
        taps = ((i + 1, NEAR), (i, -NEAR), (i + 2, -FAR), (i - 1, FAR))
    else:
        taps = ((i, NEAR), (i - 1, -NEAR), (i + 1, -FAR), (i - 2, FAR))
    total = None
    for j, weight in taps:
        layer = get(j)
        if layer is not None:
            total = weight * layer if total is None else total + weight * layer
    return total


def up_layers(cx):
    stress = [(0, cx - 1), (3, cx - 2), (3, cx - 1), (4, cx - 2), (4, cx - 1)]
    return stress, [(0, cx - 2), (0, cx - 1), (1, cx - 1), (2, cx - 1)]


def down_layers(cx):
    return [(0, 0), (0, 1), (3, 0), (4, 0)], [(0, 0), (1, 0), (1, 1), (2, 0), (2, 1)]


def halo_stress(cx):
    low = [(c, x - cx) for c, x in up_layers(cx)[0]]
    return {key: k for k, key in enumerate(low + [(c, x + cx) for c, x in down_layers(cx)[0]])}


def halo_velocity(cx):
    low = [(c, x - cx) for c, x in up_layers(cx)[1]]
    return {key: k for k, key in enumerate(low + [(c, x + cx) for c, x in down_layers(cx)[1]])}


def strip(ref, k, x, cx):
    return ref[(k * cx + x) * SIDE : (k * cx + x + 1) * SIDE, :]


def with_strip(own, edge, sec):
    return jnp.concatenate(
        [jnp.where(sec == 1, edge, 0.0), own, jnp.where(sec == 0, edge, 0.0)], axis=0
    )


def yz_terms(s, comp, x, base, rows, weights):
    fw, bw = weights
    here = slice(base, base + rows)

    def beside(c):
        return lambda shift: s[c, x, base + shift : base + shift + rows, :]

    if comp == 0:
        return backward(beside(3), 0) + backward_z(s[4, x, here, :], bw)
    if comp == 1:
        return forward(beside(1), 0) + backward_z(s[5, x, here, :], bw)
    return backward(beside(5), 0) + forward_z(s[2, x, here, :], fw)


def force(s, comp, x, base, rows, weights, halo=None):
    source, ahead = STRESS_X[comp]
    cx = s.shape[1]

    def get(j):
        if 0 <= j < cx:
            return s[source, j, base : base + rows, :]
        return None if halo is None else halo(source, j)

    return along_x(ahead, x, get) + yz_terms(s, comp, x, base, rows, weights)


def halo_share(comp, x, cx, halo):
    source, ahead = STRESS_X[comp]
    return along_x(ahead, x, lambda j: None if 0 <= j < cx else halo(source, j))


def own_share(s, comp, i, base, rows):
    source, ahead = STRESS_X[comp]
    cx = s.shape[1]
    return along_x(
        ahead, i, lambda j: s[source, j, base : base + rows, :] if 0 <= j < cx else None
    )


def load_stress(s, strips, s_pad, sec):
    comps, cx, cy, nz = s.shape
    nothing = jnp.zeros((SIDE, nz), F32)
    for c in range(comps):
        for x in range(cx):
            s_pad[c, x, 0:SIDE, :] = nothing
            s_pad[c, x, SIDE : 3 * SIDE + cy, :] = with_strip(s[c, x], strip(strips, c, x, cx), sec)
            s_pad[c, x, 3 * SIDE + cy :, :] = nothing


def send(odd, upper, lower, pay_a, pay_b, at):
    part = slice(at, at + upper.shape[0])
    pay_a[part, :] = jnp.where(odd, lower, upper)
    pay_b[part, :] = jnp.where(odd, upper, lower)


def send_layers(odd, up, down, layer, pay_a, pay_b, at):
    for k, (upper, lower) in enumerate(zip(up, down)):
        rows = layer(*upper)
        send(odd, rows, layer(*lower), pay_a, pay_b, at)
        at += rows.shape[0]


def first_lists(cx):
    (up_s, up_v), (down_s, down_v) = up_layers(cx), down_layers(cx)
    up_s, down_s = [("s", *key) for key in up_s], [("s", *key) for key in down_s]
    up_v, down_v = [("v", *key) for key in up_v], [("v", *key) for key in down_v]
    early = up_s + [("b", 0, cx - 1)], down_s + [("b", 0, 0), ("b", 0, 1)]
    late = up_v + [("b", 0, cx - 2)], down_v
    return early, late


def second_lists(cx):
    (up_s, up_v), (down_s, down_v) = up_layers(cx), down_layers(cx)
    up_s, down_s = [("s", *key) for key in up_s], [("s", *key) for key in down_s]
    up = up_s + [("v", *key) for key in up_v]
    return (up, down_s + [("v", *key) for key in down_v]), (up_s, down_s + down_s[-1:])


def thin_counts(lists):
    return [max(NEEDED[upper[0]], NEEDED[lower[0]]) for upper, lower in zip(*lists)]


def send_thin(odd, lists, counts, edge, pay_a, pay_b, at):
    for upper, lower, n in zip(*lists, counts):

        send(odd, edge(*upper, n), edge(*lower, n), pay_a, pay_b, at)
        at += n


def received(odd, lists, counts, pay_a, pay_b, cx, at):
    found = {}
    for upper, lower, n in zip(*lists, counts):
        part = slice(at, at + n)
        at += n
        for kind, c, x, below in ((*upper, True), (*lower, False)):

            def get(part=part, below=below):
                a, b = pay_a[part, :], pay_b[part, :]
                return jnp.where(odd, a, b) if below else jnp.where(odd, b, a)

            found[kind, c, x - cx if below else x + cx] = get
    return found


def put_layer(ref, k, own, thin, sec):
    cy, nz = own.shape
    n = thin.shape[0]
    ref[k, 0:SIDE, :] = jnp.zeros((SIDE, nz), F32)
    ref[k, SIDE : SIDE + cy, :] = own
    ref[k, SIDE + cy :, :] = jnp.zeros((SIDE, nz), F32)
    ref[k, SIDE - n : SIDE, :] = jnp.where(sec == 1, thin, 0.0)
    ref[k, SIDE + cy : SIDE + cy + n, :] = jnp.where(sec == 0, thin, 0.0)


def strains(velocity, halo, x, base, rows, weights):
    fw, bw = weights
    cx = velocity.shape[1]

    def layers(c):
        def get(j):
            if 0 <= j < cx:
                return velocity[c, j, base : base + rows, :]
            return halo(c, j)

        return get

    def beside(c):
        return lambda shift: velocity[c, x, base + shift : base + shift + rows, :]

    vx, vy, vz = (velocity[c, x, base : base + rows, :] for c in range(3))
    return (
        along_x(False, x, layers(0)),
        backward(beside(1), 0),
        backward_z(vz, bw),
        forward(beside(0), 0) + along_x(True, x, layers(1)),
        forward_z(vx, fw) + along_x(True, x, layers(2)),
        forward_z(vy, fw) + forward(beside(2), 0),
    )


def stress_change(lam, mu, parts):
    exx, eyy, ezz, xy, xz, yz = parts
    shear = DT * mu
    volume = (DT * lam) * (exx + eyy + ezz)
    double = 2.0 * shear
    return (
        volume + double * exx,
        volume + double * eyy,
        volume + double * ezz,
        shear * xy,
        shear * xz,
        shear * yz,
    )


def edge_rows(*refs):
    *fields, out = refs
    _, sec, _ = place()
    at = 0
    for field in fields:
        flat = field if len(field.shape) == 4 else None
        for c in range(field.shape[0] if flat is not None else 1):
            layers = field.shape[-3]
            for x in range(layers):
                rows = field[c, x] if flat is not None else field[x]
                out[at : at + SIDE, :] = jnp.where(sec == 0, rows[-SIDE:], rows[:SIDE])
                at += SIDE


def opening(s, v, b, pay_a, pay_b, edges, sems):
    odd, sec, _ = place()
    cx, cy, _ = b.shape
    up, down = first_lists(cx)[0]
    begin = pl.multiple_of(jnp.where(sec == 0, cy - SIDE, 0), SIDE)
    rows = [s.at[c, :, pl.ds(begin, SIDE), :] for c in range(6)]
    rows += [v.at[c, :, pl.ds(begin, SIDE), :] for c in range(3)]
    rows.append(b.at[:, pl.ds(begin, SIDE), :])
    rows = [pltpu.make_async_copy(r, edges.at[k], sems.at[k]) for k, r in enumerate(rows)]

    def run(above, below):
        copies = []
        for pay, layers in ((above, up), (below, down)):
            for k, (kind, c, x) in enumerate(layers):
                source = s.at[c, x] if kind == "s" else b.at[x]
                sem = sems.at[len(rows) + len(copies)]
                copies.append(pltpu.make_async_copy(source, pay.at[pl.ds(k * cy, cy)], sem))
        for copy in copies + rows:
            copy.start()
        for copy in copies:
            copy.wait()

    @pl.when(odd)
    def _():
        run(pay_b, pay_a)

    @pl.when(jnp.logical_not(odd))
    def _():
        run(pay_a, pay_b)

    for copy in rows:
        copy.wait()


def near_columns(state, depth, wet, out):
    _, sec, _ = place()
    rows, own = depth.shape
    for k, field in enumerate((state.at[0], state.at[1], state.at[2], depth, wet)):
        near = jnp.where(sec == 0, field[:, own - 128 :], field[:, :128])
        out[k * rows : (k + 1) * rows, :] = near.astype(F32)


def ocean_field(state, depth, wet, near, f, k):
    rows, own = depth.shape
    if k == own // 128:
        return near[f * rows : (f + 1) * rows, :]
    field = state.at[f] if f < 3 else depth if f == 3 else wet
    return field[:, k * 128 : (k + 1) * 128].astype(F32)


def ocean_edges(state, depth, wet, near, edges):
    rows, own = depth.shape
    at = 0
    for k in range(own // 128 + 1):
        for f, n in enumerate(DEEP if k < own // 128 else CORNER):
            field = ocean_field(state, depth, wet, near, f, k)
            edges[0, at : at + n, :] = field[rows - n :]
            edges[1, at : at + n, :] = field[:n]
            at += n


def first_round(s, v, b, strips, pay_a, pay_b, s_pad, v_part):
    odd, sec, _ = place()
    _, cx, cy, nz = s.shape
    weights = depth_weights(nz)
    rows = cy + 2 * SIDE
    load_stress(s, strips, s_pad, sec)
    for x in range(cx):
        scale = DT * with_strip(b[x], strip(strips, 9, x, cx), sec)
        for c in range(3):
            old = with_strip(v[c, x], strip(strips, 6 + c, x, cx), sec)
            v_part[c, x] = old + scale * force(s_pad, c, x, SIDE, rows, weights)

    def layer(kind, c, x):
        return v_part[c, x, SIDE : SIDE + cy, :] if kind == "v" else b[x]

    def edge(kind, c, x, n):
        if kind == "v":
            past = slice(SIDE + cy, SIDE + cy + n)
            return jnp.where(sec == 0, v_part[c, x, past, :], v_part[c, x, SIDE - n : SIDE, :])
        whole = strip(strips, c if kind == "s" else 9, x, cx)
        return jnp.where(sec == 0, whole[:n], whole[SIDE - n :])

    early, late = first_lists(cx)
    pay_a[-8:, :] = pay_b[-8:, :] = jnp.zeros((8, nz), F32)
    send_layers(odd, *late, layer, pay_a, pay_b, 0)
    at = len(late[0]) * cy
    for lists in (early, late):
        counts = thin_counts(lists)
        send_thin(odd, lists, counts, edge, pay_a, pay_b, at)
        at += sum(counts)


def first_received(odd, cx, cy, early_a, early_b, late_a, late_b):
    early, late = first_lists(cx)
    own = received(odd, early, [cy] * len(early[0]), early_a, early_b, cx, 0)
    own.update(received(odd, late, [cy] * len(late[0]), late_a, late_b, cx, 0))
    at = len(late[0]) * cy
    rest = received(odd, early, thin_counts(early), late_a, late_b, cx, at)
    at += sum(thin_counts(early))
    rest.update(received(odd, late, thin_counts(late), late_a, late_b, cx, at))
    return own, rest


def whole_step(
    sea_rows,
    s_pad,
    v_part,
    b,
    lam,
    mu,
    strips,
    more_strips,
    early_a,
    early_b,
    late_a,
    late_b,
    sea,
    info,
    v_out,
    s_out,
    pay_a,
    pay_b,
    b_near,
    v_pad,
    halo_s,
    halo_v,
    halo_b,
    materials,
):
    odd, sec, _ = place()
    cx, cy, nz = b.shape
    weights = depth_weights(nz)
    rows = cy + 2 * SIDE
    index_s, index_v = halo_stress(cx), halo_velocity(cx)
    own, rest = first_received(odd, cx, cy, early_a, early_b, late_a, late_b)
    for key, k in index_s.items():
        put_layer(halo_s, k, own["s", *key](), rest["s", *key](), sec)
    for key, k in index_v.items():
        put_layer(halo_v, k, own["v", *key](), rest["v", *key](), sec)
    index_b = {i: k for k, i in enumerate((-2, -1, cx, cx + 1))}
    for i, k in index_b.items():
        put_layer(halo_b, k, own["b", 0, i](), rest["b", 0, i](), sec)
        b_near[k * cy : (k + 1) * cy, :] = own["b", 0, i]()
    for x in range(cx):
        part = slice(4 * cy + x * SIDE, 4 * cy + (x + 1) * SIDE)
        b_near[part, :] = strip(strips, 9, x, cx)
    nothing = jnp.zeros((SIDE, nz), F32)
    for x in range(cx):
        scale = DT * with_strip(b[x], strip(strips, 9, x, cx), sec)
        for c in range(3):
            new = v_part[c, x]
            terms = halo_share(c, x, cx, lambda k, j: halo_s[index_s[k, j]])
            if terms is not None:
                new = new + scale * terms
            v_pad[c, x, 0:SIDE, :] = nothing
            v_pad[c, x, SIDE : SIDE + rows, :] = new
            v_pad[c, x, SIDE + rows :, :] = nothing
            v_out[c, x, 0 : rows - 2 * EDGE, :] = v_pad[c, x, SIDE + EDGE : SIDE + rows - EDGE, :]
            v_out[c, x, rows - 2 * EDGE :, :] = nothing
    for (c, i), k in index_v.items():
        halo_v[k] = halo_v[k] + DT * halo_b[index_b[i]] * own_share(s_pad, c, i, SIDE, rows)
    kept = slice(EDGE, rows - EDGE)
    base, fewer = SIDE + EDGE, rows - 2 * EDGE
    halo = lambda c, j: halo_v[index_v[c, j], kept, :]
    for x in range(cx):
        parts = strains(v_pad, halo, x, base, fewer, weights)
        materials[0] = with_strip(lam[x], strip(more_strips, 0, x, cx), sec)
        materials[1] = with_strip(mu[x], strip(more_strips, 1, x, cx), sec)
        changes = stress_change(materials[0, kept, :], materials[1, kept, :], parts)
        for c, change in enumerate(changes):
            s_out[c, x, 0:fewer, :] = s_pad[c, x, base : base + fewer, :] + change
            s_out[c, x, fewer:, :] = nothing

    def layer(kind, c, x):
        if kind == "s":
            return s_out[c, x, EDGE : EDGE + cy, :]
        old = v_out[c, x, EDGE : EDGE + cy, :]
        return old + DT * b[x] * force(s_out, c, x, EDGE, cy, weights)

    def edge(_, c, x, n):
        past = slice(EDGE + cy, EDGE + cy + n)
        return jnp.where(sec == 0, s_out[c, x, past, :], s_out[c, x, EDGE - n : EDGE, :])

    layers, edges = second_lists(cx)
    pay_a[-8:, :] = pay_b[-8:, :] = jnp.zeros((8, nz), F32)
    send_layers(odd, *layers, layer, pay_a, pay_b, 0)
    counts = [LAST_NEEDED] * len(edges[0])
    at = LAYERS * cy
    send(odd, sea[0, :sea_rows], sea[1, :sea_rows], pay_a, pay_b, at)
    send(odd, info[...], info[...], pay_a, pay_b, at + sea_rows)
    send_thin(odd, edges, counts, edge, pay_a, pay_b, at + sea_rows + 1)


def last_step(
    sea_rows,
    s,
    v,
    b,
    lam,
    mu,
    b_near,
    from_a,
    from_b,
    v_out,
    s_out,
    v_rows,
    b_rows,
    halo_s,
    halo_v,
    made,
    sems,
):
    odd, sec, _ = place()
    cx, cy, nz = b.shape
    weights = depth_weights(nz)
    rows = cy + 2 * LAST_NEEDED
    here = slice(SIDE - LAST_NEEDED, SIDE - LAST_NEEDED + rows)
    index_s, index_v = halo_stress(cx), halo_velocity(cx)
    layers, edges = second_lists(cx)
    own = received(odd, layers, [cy] * LAYERS, from_a, from_b, cx, 0)
    counts = [LAST_NEEDED] * len(edges[0])
    rest = received(odd, edges, counts, from_a, from_b, cx, LAYERS * cy + sea_rows + 1)
    for key, k in index_s.items():
        put_layer(halo_s, k, own["s", *key](), rest["s", *key](), sec)
    for x in range(cx):
        part = slice(4 * cy + x * SIDE, 4 * cy + (x + 1) * SIDE)
        b_rows[...] = with_strip(b[x], b_near[part, :], sec)
        scale = DT * b_rows[here, :]
        for c in range(3):
            terms = halo_share(c, x, cx, lambda k, j: halo_s[index_s[k, j], here, :])
            new = v[c, x, here, :]
            v_rows[c, x, here, :] = new if terms is None else new + scale * terms
    copies = [pltpu.make_async_copy(v_rows.at[:, :, pl.ds(SIDE, cy), :], v_out, sems.at[cx])]
    copies[0].start()
    for (c, i), k in index_v.items():
        at = (i + 2 if i < 0 else i - cx + 2) * cy
        scale = DT * b_near[at : at + cy, :]
        halo_v[k] = own["v", c, i]() + scale * own_share(s, c, i, EDGE, cy)
    for x in range(cx):
        parts = strains(v_rows, lambda c, j: halo_v[index_v[c, j]], x, SIDE, cy, weights)
        for c, change in enumerate(stress_change(lam[x], mu[x], parts)):
            made[c, x] = s[c, x, EDGE : EDGE + cy, :] + change
        copies.append(pltpu.make_async_copy(made.at[:, x], s_out.at[:, x], sems.at[x]))
        copies[-1].start()
    return copies


def floor_line(left, right):
    rows = left.shape[0]
    row = lax.broadcasted_iota(jnp.int32, (rows, 2 * rows), 0)
    lane = lax.broadcasted_iota(jnp.int32, (rows, 2 * rows), 1)
    picked = jnp.where(lane == row, left[:, 0:1], 0.0)
    picked = jnp.where(lane == row + rows, right[:, 0:1], picked)
    return jnp.sum(picked, axis=0, keepdims=True)


def floor_parts(s, v, b, b_near, parts, v_part, b_rows):
    cx, cy, nz = b.shape
    weights = depth_weights(nz)
    _, sec, _ = place()
    own = slice(EDGE, EDGE + cy)
    first, rows = EDGE - LAST_NEEDED, cy + 2 * LAST_NEEDED
    here = slice(SIDE - LAST_NEEDED, SIDE - LAST_NEEDED + rows)
    for x in range(cx):
        part = slice(4 * cy + x * SIDE, 4 * cy + (x + 1) * SIDE)
        b_rows[...] = with_strip(b[x], b_near[part, :], sec)
        scale = DT * b_rows[here, :]
        for c in range(3):
            terms = force(s, c, x, first, rows, weights)
            v_part[c, x, here, :] = v[c, x, first : first + rows, :] + scale * terms
    layers = [v_part[2, x, SIDE : SIDE + cy, :] for x in range(cx)]
    lines = [floor_line(layers[x], layers[x + 1]) for x in range(0, cx, 2)]
    below, first_above, second_above = (
        DT * b_near[k * cy : (k + 1) * cy, :] for k in (1, 2, 3)
    )
    last, before, start = s[4, cx - 1, own, :], s[4, cx - 2, own, :], s[4, 0, own, :]
    reached = first_above * (FAR * before - NEAR * last)
    lines.append(floor_line(reached, second_above * (FAR * last)))
    lines.append(floor_line(jnp.zeros((cy, nz), F32), below * (-FAR * start)))
    row = lax.broadcasted_iota(jnp.int32, (SIDE, 2 * cy), 0)
    tiled = jnp.zeros((SIDE, 2 * cy), F32)
    for j in range(SIDE):
        tiled = jnp.where(row == j, lines[j % LINES], tiled)
    for at in range(0, parts.shape[0], SIDE):
        parts[at : at + SIDE, :] = tiled


def column(line, first, count):
    wide = jnp.broadcast_to(line, (count, line.shape[1]))
    row = lax.broadcasted_iota(jnp.int32, wide.shape, 0)
    lane = lax.broadcasted_iota(jnp.int32, wide.shape, 1)
    return jnp.sum(jnp.where(lane == row + first, wide, 0.0), axis=1, keepdims=True)


def ocean_steps(
    start, from_a, from_b, near, state, depth, wet_ref, info, patches, ocean_out, ocean_ref, send_out, told_ref
):
    odd, sec, tile = place()
    count = lax.axis_size("tile")
    rows, own = depth.shape
    columns = own + 128
    at = start
    for k in range(columns // 128):
        lanes = slice(k * 128, (k + 1) * 128)
        for f, n in enumerate(DEEP if k < own // 128 else CORNER):
            here = ocean_field(state, depth, wet_ref, near, f, k)
            a, b = from_a[at : at + n, :], from_b[at : at + n, :]
            low, high = jnp.where(odd, a, b), jnp.where(odd, b, a)
            ocean_ref[f, 0:SIDE, lanes] = jnp.zeros((SIDE, 128), F32)
            ocean_ref[f, SIDE + rows :, lanes] = jnp.zeros((SIDE, 128), F32)
            ocean_ref[f, SIDE - n : SIDE, lanes] = low
            ocean_ref[f, SIDE : SIDE + rows, lanes] = here
            ocean_ref[f, SIDE + rows : SIDE + rows + n, lanes] = high
            at += n

    total = rows + 2 * SIDE
    lane = lax.broadcasted_iota(jnp.int32, (1, columns), 1)
    ahead = jnp.where((lane == own - 1) & (sec == 1), 0.0, 0.5).astype(F32)
    behind = jnp.where((lane == 0) & (sec == 0), 0.0, 0.5).astype(F32)
    line = lax.broadcasted_iota(jnp.int32, (total, 1), 0)
    inside = ((line >= SIDE) | (tile > 0)) & ((line < SIDE + rows) | (tile < count - 1))
    inside = inside.astype(F32)

    def across(f):
        return pltpu.roll(f, columns - 1, 1) * ahead - pltpu.roll(f, 1, 1) * behind

    def down(f):
        return 0.5 * (pltpu.roll(f, total - 1, 0) - pltpu.roll(f, 1, 0))

    eta, u, v_sea = ocean_ref[0], ocean_ref[1], ocean_ref[2]
    depth, wet = ocean_ref[3], ocean_ref[4]
    window = min(WINDOW, count)
    base = jnp.clip(tile - REACH - 1, 0, count - window)

    told_ref[0 : patches.shape[0], :] = patches[...]
    told_ref[patches.shape[0] :, :] = jnp.zeros((8, 128), F32)

    def told(half, k):
        return told_ref[pl.ds((half * count + k) * LINES, LINES), :]

    a, b = from_a[at : at + 1, :], from_b[at : at + 1, :]
    below, above = jnp.where(odd, a, b), jnp.where(odd, b, a)
    line = info[...]
    marks = [
        jnp.concatenate(
            [
                column(below, k * rows + rows - SIDE, SIDE),
                column(line, k * rows, rows),
                column(above, k * rows, SIDE),
            ],
            axis=0,
        )
        for k in range(2)
    ]
    owner = jnp.broadcast_to(marks[0] - base.astype(F32), (total, 128))
    share = marks[1]
    uplift = []
    for half in (sec, 1 - sec):
        tiles = []
        for k in range(-1, window + 1):
            here = jnp.clip(base + k, 0, count - 1)
            there = (here == base + k).astype(F32)
            tiles.append(told(half, here) * there)
        levels = [jnp.zeros((total, 128), F32) for _ in range(2)]
        for k in range(window):
            below, this, above = tiles[k], tiles[k + 1], tiles[k + 2]
            first, second = this[0:1] + below[2:3], this[1:2] + above[3:4]
            mine = owner == float(k)
            levels = [jnp.where(mine, q, level) for q, level in zip((first, second), levels)]
        uplift.append(levels)
    uplift = uplift[0] + [jnp.where(sec == 0, uplift[1][0], uplift[1][1])]
    uplift = jnp.concatenate(uplift, axis=1)
    lift = ODT * (share * wet * uplift)
    part = slice(SIDE, SIDE + rows)
    for step in range(2):
        u = wet * (u - ODT * down(eta))
        v_sea = wet * (v_sea - ODT * across(eta))
        if step == 1:
            ocean_out[1] = u[part, :own]
            ocean_out[2] = v_sea[part, :own]
            send_out(slice(1, 3))
        eta = inside * (eta - ODT * (down(depth * u) + across(depth * v_sea)) + lift)
    ocean_out[0] = eta[part, :own]
    send_out(slice(0, 1))


def finish(
    sea_rows,
    s,
    v,
    b,
    lam,
    mu,
    b_near,
    from_a,
    from_b,
    near,
    state,
    depth,
    wet,
    info,
    patches,
    v_out,
    s_out,
    ocean_out,
    v_rows,
    b_rows,
    halo_s,
    halo_v,
    made,
    ocean_ref,
    ocean_made,
    told_ref,
    sems,
    ocean_sems,
):
    cx, cy, _ = b.shape
    copies = last_step(
        sea_rows,
        s,
        v,
        b,
        lam,
        mu,
        b_near,
        from_a,
        from_b,
        v_out,
        s_out,
        v_rows,
        b_rows,
        halo_s,
        halo_v,
        made,
        sems,
    )

    def send_out(part):
        size = part.stop - part.start
        here = (pl.ds(part.start, size),)
        copies.append(
            pltpu.make_async_copy(
                ocean_made.at[here], ocean_out.at[here], ocean_sems.at[part.start]
            )
        )
        copies[-1].start()

    ocean_steps(
        LAYERS * cy,
        from_a,
        from_b,
        near,
        state,
        depth,
        wet,
        info,
        patches,
        ocean_made,
        ocean_ref,
        send_out,
        told_ref,
    )
    for copy in copies:
        copy.wait()


VMEM = pl.BlockSpec(memory_space=pltpu.VMEM)
ANY = pl.BlockSpec(memory_space=pl.ANY)


def call(body, name, outs, scratch, operands, weight=1, ins=VMEM, where=VMEM, grant=8):
    shapes = [jax.ShapeDtypeStruct(o, F32) for o in outs]
    moved = sum(o.size for o in operands) * 4 + sum(o.size for o in shapes) * 4
    return pl.pallas_call(
        body,
        name=name,
        out_shape=shapes,
        in_specs=ins if isinstance(ins, list) else [ins] * len(operands),
        out_specs=where if isinstance(where, list) else [where] * len(outs),
        scratch_shapes=scratch,
        compiler_params=pltpu.CompilerParams(vmem_limit_bytes=int(grant * 1024 * 1024)),
        cost_estimate=pl.CostEstimate(
            flops=moved * weight, bytes_accessed=moved * weight, transcendentals=0
        ),
    )(*operands)


def exchange(pay_a, pay_b, count):
    def swap(pay, first):
        pairs = []
        for i in range(first, count - 1, 2):
            pairs += [(i, i + 1), (i + 1, i)]
        return lax.ppermute(pay, "tile", pairs)

    from_a = swap(pay_a, 0)
    return from_a, swap(pay_b, 1)


def across(pay):
    return lax.ppermute(pay, "sec", [(0, 1), (1, 0)])


def shards(
    velocity,
    stresses,
    buoyancy,
    lame_first,
    shear_mod,
    ocean_state,
    depth_map,
    wet_mask,
    intersection_src,
    intersection_share,
):
    count = lax.axis_size("tile")
    sec = lax.axis_index("sec")
    _, cx, cy, nz = stresses.shape
    _, rows, columns = ocean_state.shape
    tall = cy + 2 * SIDE
    halo = pltpu.VMEM((LAYERS, tall, nz), F32)

    first = ((LAYERS + 2) // 2 + 1) * cy
    pay_a, pay_b, edges = call(
        opening,
        "opening",
        [(first, nz), (first, nz), (10, cx, SIDE, nz)],
        [pltpu.SemaphoreType.DMA((10 + 2 * (first // cy),))],
        [stresses, velocity, buoyancy],
        ins=ANY,
        grant=60,
    )
    strips = across(edges.reshape(10 * cx * SIDE, nz))
    early_a, early_b = exchange(pay_a, pay_b, count)
    early_list, late_list = first_lists(cx)
    per = columns // 128 * sum(DEEP) + sum(CORNER)
    late = len(late_list[0]) * cy + rounded(sum(thin_counts(early_list) + thin_counts(late_list)))
    pay_a, pay_b, stresses, velocity = call(
        first_round,
        "first_round",
        [(late, nz), (late, nz), (6, cx, tall + 2 * SIDE, nz), (3, cx, tall, nz)],
        [],
        [stresses, velocity, buoyancy, strips],
    )
    late_a, late_b = exchange(pay_a, pay_b, count)

    source, share, lame, shear, _ = lax.optimization_barrier(
        (intersection_src, intersection_share, lame_first, shear_mod, early_b)
    )
    ocean_state, depth_map, wet_mask, _ = lax.optimization_barrier(
        (ocean_state, depth_map, wet_mask, early_a)
    )
    (edges,) = call(edge_rows, "edge_rows", [(2 * cx * SIDE, nz)], [], [lame, shear])
    more_strips = across(edges)
    sea = [ocean_state, depth_map, wet_mask]
    (near,) = call(near_columns, "near_columns", [(len(DEEP) * rows, 128)], [], sea)
    near = across(near)
    (edges,) = call(ocean_edges, "ocean_edges", [(2, rounded(per) + 8, 128)], [], sea + [near])
    info = jnp.concatenate([source.astype(F32), share])[None]

    kept = cy + 2 * EDGE + 8
    second = (LAYERS * cy + rounded(per + 1 + 5 * LAST_NEEDED), nz)
    velocity, stresses, pay_a, pay_b, b_near = call(
        functools.partial(whole_step, per),
        "whole_step",
        [(3, cx, kept, nz), (6, cx, kept, nz), second, second]
        + [(4 * cy + cx * SIDE, nz)],
        [
            pltpu.VMEM((3, cx, tall + 2 * SIDE, nz), F32),
            halo,
            halo,
            pltpu.VMEM((4, tall, nz), F32),
            pltpu.VMEM((2, tall, nz), F32),
        ],
        [stresses, velocity, buoyancy, lame_first, shear_mod, strips, more_strips]
        + [early_a, early_b, late_a, late_b, edges, info],
    )
    from_a, from_b = exchange(pay_a, pay_b, count)
    parts, velocity = call(
        floor_parts,
        "floor_parts",
        [(2 * count * LINES, 2 * cy), (3, cx, tall, nz)],
        [pltpu.VMEM((tall, nz), F32)],
        [stresses, velocity, buoyancy, b_near],
    )
    parts = parts.reshape(2 * count * LINES // 2, 2, 2 * cy)
    patches = lax.all_to_all(parts, ("sec", "tile"), 0, 0, tiled=True).reshape(-1, 2 * cy)
    velocity, stresses, ocean_state = call(
        functools.partial(finish, per),
        "finish",
        [(3, cx, cy, nz), (6, cx, cy, nz), ocean_state.shape],
        [
            pltpu.VMEM((3, cx, tall, nz), F32),
            pltpu.VMEM((tall, nz), F32),
            halo,
            pltpu.VMEM((LAYERS, cy, nz), F32),
            pltpu.VMEM((6, cx, cy, nz), F32),
            pltpu.VMEM((len(DEEP), rows + 2 * SIDE, columns + 128), F32),
            pltpu.VMEM(ocean_state.shape, F32),
            pltpu.VMEM((2 * count * LINES + 8, 128), F32),
            pltpu.SemaphoreType.DMA((cx + 1,)),
            pltpu.SemaphoreType.DMA((2,)),
        ],
        [stresses, velocity, buoyancy, lame_first, shear_mod, b_near]
        + [from_a, from_b, near] + sea + [info, patches],
        where=ANY,
        grant=16,
    )
    return velocity, stresses, ocean_state


def solution(mesh):
    cube = P("tile", "sec", None)
    return jax.shard_map(
        shards,
        mesh=mesh,
        in_specs=(
            P(None, "tile", "sec", None),
            P(None, "tile", "sec", None),
            cube,
            cube,
            cube,
            P(None, "tile", "sec"),
            P("tile", "sec"),
            P("tile", "sec"),
            P("tile"),
            P("tile"),
        ),
        out_specs=(
            P(None, "tile", "sec", None),
            P(None, "tile", "sec", None),
            P(None, "tile", "sec"),
        ),
        check_vma=False,
    )
```

```python
import functools

import jax
import jax.numpy as jnp
from jax import lax
from jax.experimental import pallas as pl
from jax.experimental.pallas import tpu as pltpu
from jax.sharding import PartitionSpec as P

REACH = 2
NEAR = 9.0 / 8.0
FAR = 1.0 / 24.0
DT = 0.15
ODT = 0.3
F32 = jnp.float32
EDGE = 4
SIDE = 8
WINDOW = 8
DEEP = (4, 3, 2, 3)
CORNER = (2, 1, 2, 2)
LINES = 4
NEEDED = {"s": 5, "v": 3, "b": 3}
LAST_NEEDED = 2
LAYERS = 9
STRESS_X = ((0, True), (3, False), (4, False))


def depth_weights(width):
    lane = lax.broadcasted_iota(jnp.int32, (1, width), 1)

    def weight(value, first, last):
        return jnp.where((lane >= first) & (lane < last), value, 0.0).astype(F32)

    forward = (weight(NEAR, 0, width - 1), weight(-FAR, 0, width - 2), weight(FAR, 1, width))
    backward = (weight(-NEAR, 1, width), weight(-FAR, 0, width - 1), weight(FAR, 2, width))
    return forward, backward


def forward_z(f, weights):
    near, far, behind = weights
    n = f.shape[-1]
    return (
        pltpu.roll(f, n - 1, 1) * near
        - NEAR * f
        + pltpu.roll(f, n - 2, 1) * far
        + pltpu.roll(f, 1, 1) * behind
    )


def backward_z(f, weights):
    near, far, behind = weights
    n = f.shape[-1]
    return (
        NEAR * f
        + pltpu.roll(f, 1, 1) * near
        + pltpu.roll(f, n - 1, 1) * far
        + pltpu.roll(f, 2, 1) * behind
    )


def forward(at, i):
    return NEAR * (at(i + 1) - at(i)) - FAR * (at(i + 2) - at(i - 1))


def backward(at, i):
    return NEAR * (at(i) - at(i - 1)) - FAR * (at(i + 1) - at(i - 2))


def rounded(rows):
    return -(-rows // 8) * 8


def place():
    tile, sec = lax.axis_index("tile"), lax.axis_index("sec")
    return lax.rem(tile, 2) == 1, sec, tile


def along_x(ahead, i, get):
    if ahead:
        taps = ((i + 1, NEAR), (i, -NEAR), (i + 2, -FAR), (i - 1, FAR))
    else:
        taps = ((i, NEAR), (i - 1, -NEAR), (i + 1, -FAR), (i - 2, FAR))
    total = None
    for j, weight in taps:
        layer = get(j)
        if layer is not None:
            total = weight * layer if total is None else total + weight * layer
    return total


def up_layers(cx):
    stress = [(0, cx - 1), (3, cx - 2), (3, cx - 1), (4, cx - 2), (4, cx - 1)]
    return stress, [(0, cx - 2), (0, cx - 1), (1, cx - 1), (2, cx - 1)]


def down_layers(cx):
    return [(0, 0), (0, 1), (3, 0), (4, 0)], [(0, 0), (1, 0), (1, 1), (2, 0), (2, 1)]


def halo_stress(cx):
    low = [(c, x - cx) for c, x in up_layers(cx)[0]]
    return {key: k for k, key in enumerate(low + [(c, x + cx) for c, x in down_layers(cx)[0]])}


def halo_velocity(cx):
    low = [(c, x - cx) for c, x in up_layers(cx)[1]]
    return {key: k for k, key in enumerate(low + [(c, x + cx) for c, x in down_layers(cx)[1]])}


def strip(ref, k, x, cx):
    return ref[(k * cx + x) * SIDE : (k * cx + x + 1) * SIDE, :]


def with_strip(own, edge, sec):
    return jnp.concatenate(
        [jnp.where(sec == 1, edge, 0.0), own, jnp.where(sec == 0, edge, 0.0)], axis=0
    )


def yz_terms(s, comp, x, base, rows, weights):
    fw, bw = weights
    here = slice(base, base + rows)

    def beside(c):
        return lambda shift: s[c, x, base + shift : base + shift + rows, :]

    if comp == 0:
        return backward(beside(3), 0) + backward_z(s[4, x, here, :], bw)
    if comp == 1:
        return forward(beside(1), 0) + backward_z(s[5, x, here, :], bw)
    return backward(beside(5), 0) + forward_z(s[2, x, here, :], fw)


def force(s, comp, x, base, rows, weights, halo=None):
    source, ahead = STRESS_X[comp]
    cx = s.shape[1]

    def get(j):
        if 0 <= j < cx:
            return s[source, j, base : base + rows, :]
        return None if halo is None else halo(source, j)

    return along_x(ahead, x, get) + yz_terms(s, comp, x, base, rows, weights)


def halo_share(comp, x, cx, halo):
    source, ahead = STRESS_X[comp]
    return along_x(ahead, x, lambda j: None if 0 <= j < cx else halo(source, j))


def own_share(s, comp, i, base, rows):
    source, ahead = STRESS_X[comp]
    cx = s.shape[1]
    return along_x(
        ahead, i, lambda j: s[source, j, base : base + rows, :] if 0 <= j < cx else None
    )


def load_stress(s, strips, s_pad, sec):
    comps, cx, cy, nz = s.shape
    nothing = jnp.zeros((SIDE, nz), F32)
    for c in range(comps):
        for x in range(cx):
            s_pad[c, x, 0:SIDE, :] = nothing
            s_pad[c, x, SIDE : 3 * SIDE + cy, :] = with_strip(s[c, x], strip(strips, c, x, cx), sec)
            s_pad[c, x, 3 * SIDE + cy :, :] = nothing


def send(odd, upper, lower, pay_a, pay_b, at):
    part = slice(at, at + upper.shape[0])
    pay_a[part, :] = jnp.where(odd, lower, upper)
    pay_b[part, :] = jnp.where(odd, upper, lower)


def send_layers(odd, up, down, layer, pay_a, pay_b, at):
    for k, (upper, lower) in enumerate(zip(up, down)):
        rows = layer(*upper)
        send(odd, rows, layer(*lower), pay_a, pay_b, at)
        at += rows.shape[0]


def first_lists(cx):
    (up_s, up_v), (down_s, down_v) = up_layers(cx), down_layers(cx)
    up_s, down_s = [("s", *key) for key in up_s], [("s", *key) for key in down_s]
    up_v, down_v = [("v", *key) for key in up_v], [("v", *key) for key in down_v]
    early = up_s + [("b", 0, cx - 1)], down_s + [("b", 0, 0), ("b", 0, 1)]
    late = up_v + [("b", 0, cx - 2)], down_v
    return early, late


def second_lists(cx):
    (up_s, up_v), (down_s, down_v) = up_layers(cx), down_layers(cx)
    up_s, down_s = [("s", *key) for key in up_s], [("s", *key) for key in down_s]
    up = up_s + [("v", *key) for key in up_v]
    return (up, down_s + [("v", *key) for key in down_v]), (up_s, down_s + down_s[-1:])


def thin_counts(lists):
    return [max(NEEDED[upper[0]], NEEDED[lower[0]]) for upper, lower in zip(*lists)]


def send_thin(odd, lists, counts, edge, pay_a, pay_b, at):
    for upper, lower, n in zip(*lists, counts):

        send(odd, edge(*upper, n), edge(*lower, n), pay_a, pay_b, at)
        at += n


def received(odd, lists, counts, pay_a, pay_b, cx, at):
    found = {}
    for upper, lower, n in zip(*lists, counts):
        part = slice(at, at + n)
        at += n
        for kind, c, x, below in ((*upper, True), (*lower, False)):

            def get(part=part, below=below):
                a, b = pay_a[part, :], pay_b[part, :]
                return jnp.where(odd, a, b) if below else jnp.where(odd, b, a)

            found[kind, c, x - cx if below else x + cx] = get
    return found


def put_layer(ref, k, own, thin, sec):
    cy, nz = own.shape
    n = thin.shape[0]
    ref[k, 0:SIDE, :] = jnp.zeros((SIDE, nz), F32)
    ref[k, SIDE : SIDE + cy, :] = own
    ref[k, SIDE + cy :, :] = jnp.zeros((SIDE, nz), F32)
    ref[k, SIDE - n : SIDE, :] = jnp.where(sec == 1, thin, 0.0)
    ref[k, SIDE + cy : SIDE + cy + n, :] = jnp.where(sec == 0, thin, 0.0)


def strains(velocity, halo, x, base, rows, weights):
    fw, bw = weights
    cx = velocity.shape[1]

    def layers(c):
        def get(j):
            if 0 <= j < cx:
                return velocity[c, j, base : base + rows, :]
            return halo(c, j)

        return get

    def beside(c):
        return lambda shift: velocity[c, x, base + shift : base + shift + rows, :]

    vx, vy, vz = (velocity[c, x, base : base + rows, :] for c in range(3))
    return (
        along_x(False, x, layers(0)),
        backward(beside(1), 0),
        backward_z(vz, bw),
        forward(beside(0), 0) + along_x(True, x, layers(1)),
        forward_z(vx, fw) + along_x(True, x, layers(2)),
        forward_z(vy, fw) + forward(beside(2), 0),
    )


def stress_change(lam, mu, parts):
    exx, eyy, ezz, xy, xz, yz = parts
    shear = DT * mu
    volume = (DT * lam) * (exx + eyy + ezz)
    double = 2.0 * shear
    return (
        volume + double * exx,
        volume + double * eyy,
        volume + double * ezz,
        shear * xy,
        shear * xz,
        shear * yz,
    )


def edge_rows(*refs):
    *fields, out = refs
    _, sec, _ = place()
    at = 0
    for field in fields:
        flat = field if len(field.shape) == 4 else None
        for c in range(field.shape[0] if flat is not None else 1):
            layers = field.shape[-3]
            for x in range(layers):
                rows = field[c, x] if flat is not None else field[x]
                out[at : at + SIDE, :] = jnp.where(sec == 0, rows[-SIDE:], rows[:SIDE])
                at += SIDE


def opening(s, v, b, pay_a, pay_b, edges, sems):
    odd, sec, _ = place()
    cx, cy, _ = b.shape
    up, down = first_lists(cx)[0]
    begin = pl.multiple_of(jnp.where(sec == 0, cy - SIDE, 0), SIDE)
    rows = [s.at[c, :, pl.ds(begin, SIDE), :] for c in range(6)]
    rows += [v.at[c, :, pl.ds(begin, SIDE), :] for c in range(3)]
    rows.append(b.at[:, pl.ds(begin, SIDE), :])
    rows = [pltpu.make_async_copy(r, edges.at[k], sems.at[k]) for k, r in enumerate(rows)]

    def run(above, below):
        copies = []
        for pay, layers in ((above, up), (below, down)):
            for k, (kind, c, x) in enumerate(layers):
                source = s.at[c, x] if kind == "s" else b.at[x]
                sem = sems.at[len(rows) + len(copies)]
                copies.append(pltpu.make_async_copy(source, pay.at[pl.ds(k * cy, cy)], sem))
        for copy in copies + rows:
            copy.start()
        for copy in copies:
            copy.wait()

    @pl.when(odd)
    def _():
        run(pay_b, pay_a)

    @pl.when(jnp.logical_not(odd))
    def _():
        run(pay_a, pay_b)

    for copy in rows:
        copy.wait()


def near_columns(state, depth, wet, out):
    _, sec, _ = place()
    rows, own = depth.shape

    def beside(field):
        return jnp.where(sec == 0, field[:, own - 128 :], field[:, :128]).astype(F32)

    for k in range(3):
        out[k * rows : (k + 1) * rows, :] = beside(state.at[k])
    out[3 * rows :, :] = beside(depth) * beside(wet)


def ocean_field(state, depth, wet, near, f, k):
    rows, own = depth.shape
    if k == own // 128:
        return near[f * rows : (f + 1) * rows, :]
    lanes = slice(k * 128, (k + 1) * 128)
    return state[f, :, lanes] if f < 3 else depth[:, lanes] * wet[:, lanes].astype(F32)


def ocean_edges(state, depth, wet, near, edges):
    rows, own = depth.shape
    at = 0
    for k in range(own // 128 + 1):
        for f, n in enumerate(DEEP if k < own // 128 else CORNER):
            field = ocean_field(state, depth, wet, near, f, k)
            edges[0, at : at + n, :] = field[rows - n :]
            edges[1, at : at + n, :] = field[:n]
            at += n


def first_round(s, v, b, strips, pay_a, pay_b, s_pad, v_part):
    odd, sec, _ = place()
    _, cx, cy, nz = s.shape
    weights = depth_weights(nz)
    rows = cy + 2 * SIDE
    load_stress(s, strips, s_pad, sec)
    for x in range(cx):
        scale = DT * with_strip(b[x], strip(strips, 9, x, cx), sec)
        for c in range(3):
            old = with_strip(v[c, x], strip(strips, 6 + c, x, cx), sec)
            v_part[c, x] = old + scale * force(s_pad, c, x, SIDE, rows, weights)

    def layer(kind, c, x):
        return v_part[c, x, SIDE : SIDE + cy, :] if kind == "v" else b[x]

    def edge(kind, c, x, n):
        if kind == "v":
            past = slice(SIDE + cy, SIDE + cy + n)
            return jnp.where(sec == 0, v_part[c, x, past, :], v_part[c, x, SIDE - n : SIDE, :])
        whole = strip(strips, c if kind == "s" else 9, x, cx)
        return jnp.where(sec == 0, whole[:n], whole[SIDE - n :])

    early, late = first_lists(cx)
    pay_a[-8:, :] = pay_b[-8:, :] = jnp.zeros((8, nz), F32)
    send_layers(odd, *late, layer, pay_a, pay_b, 0)
    at = len(late[0]) * cy
    for lists in (early, late):
        counts = thin_counts(lists)
        send_thin(odd, lists, counts, edge, pay_a, pay_b, at)
        at += sum(counts)


def first_received(odd, cx, cy, early_a, early_b, late_a, late_b):
    early, late = first_lists(cx)
    own = received(odd, early, [cy] * len(early[0]), early_a, early_b, cx, 0)
    own.update(received(odd, late, [cy] * len(late[0]), late_a, late_b, cx, 0))
    at = len(late[0]) * cy
    rest = received(odd, early, thin_counts(early), late_a, late_b, cx, at)
    at += sum(thin_counts(early))
    rest.update(received(odd, late, thin_counts(late), late_a, late_b, cx, at))
    return own, rest


def whole_step(
    sea_rows,
    s_pad,
    v_part,
    b,
    lam,
    mu,
    strips,
    more_strips,
    early_a,
    early_b,
    late_a,
    late_b,
    sea,
    info,
    v_out,
    s_out,
    pay_a,
    pay_b,
    b_near,
    v_pad,
    halo_s,
    halo_v,
    halo_b,
    materials,
):
    odd, sec, _ = place()
    cx, cy, nz = b.shape
    weights = depth_weights(nz)
    rows = cy + 2 * SIDE
    index_s, index_v = halo_stress(cx), halo_velocity(cx)
    own, rest = first_received(odd, cx, cy, early_a, early_b, late_a, late_b)
    for key, k in index_s.items():
        put_layer(halo_s, k, own["s", *key](), rest["s", *key](), sec)
    for key, k in index_v.items():
        put_layer(halo_v, k, own["v", *key](), rest["v", *key](), sec)
    index_b = {i: k for k, i in enumerate((-2, -1, cx, cx + 1))}
    for i, k in index_b.items():
        put_layer(halo_b, k, own["b", 0, i](), rest["b", 0, i](), sec)
        b_near[k * cy : (k + 1) * cy, :] = own["b", 0, i]()
    for x in range(cx):
        part = slice(4 * cy + x * SIDE, 4 * cy + (x + 1) * SIDE)
        b_near[part, :] = strip(strips, 9, x, cx)
    nothing = jnp.zeros((SIDE, nz), F32)
    for x in range(cx):
        scale = DT * with_strip(b[x], strip(strips, 9, x, cx), sec)
        for c in range(3):
            new = v_part[c, x]
            terms = halo_share(c, x, cx, lambda k, j: halo_s[index_s[k, j]])
            if terms is not None:
                new = new + scale * terms
            v_pad[c, x, 0:SIDE, :] = nothing
            v_pad[c, x, SIDE : SIDE + rows, :] = new
            v_pad[c, x, SIDE + rows :, :] = nothing
            v_out[c, x, 0 : rows - 2 * EDGE, :] = v_pad[c, x, SIDE + EDGE : SIDE + rows - EDGE, :]
            v_out[c, x, rows - 2 * EDGE :, :] = nothing
    for (c, i), k in index_v.items():
        halo_v[k] = halo_v[k] + DT * halo_b[index_b[i]] * own_share(s_pad, c, i, SIDE, rows)
    kept = slice(EDGE, rows - EDGE)
    base, fewer = SIDE + EDGE, rows - 2 * EDGE
    halo = lambda c, j: halo_v[index_v[c, j], kept, :]
    for x in range(cx):
        parts = strains(v_pad, halo, x, base, fewer, weights)
        materials[0] = with_strip(lam[x], strip(more_strips, 0, x, cx), sec)
        materials[1] = with_strip(mu[x], strip(more_strips, 1, x, cx), sec)
        changes = stress_change(materials[0, kept, :], materials[1, kept, :], parts)
        for c, change in enumerate(changes):
            s_out[c, x, 0:fewer, :] = s_pad[c, x, base : base + fewer, :] + change
            s_out[c, x, fewer:, :] = nothing

    def layer(kind, c, x):
        if kind == "s":
            return s_out[c, x, EDGE : EDGE + cy, :]
        old = v_out[c, x, EDGE : EDGE + cy, :]
        return old + DT * b[x] * force(s_out, c, x, EDGE, cy, weights)

    def edge(_, c, x, n):
        past = slice(EDGE + cy, EDGE + cy + n)
        return jnp.where(sec == 0, s_out[c, x, past, :], s_out[c, x, EDGE - n : EDGE, :])

    layers, edges = second_lists(cx)
    pay_a[-8:, :] = pay_b[-8:, :] = jnp.zeros((8, nz), F32)
    send_layers(odd, *layers, layer, pay_a, pay_b, 0)
    counts = [LAST_NEEDED] * len(edges[0])
    at = LAYERS * cy
    send(odd, sea[0, :sea_rows], sea[1, :sea_rows], pay_a, pay_b, at)
    send(odd, info[...], info[...], pay_a, pay_b, at + sea_rows)
    send_thin(odd, edges, counts, edge, pay_a, pay_b, at + sea_rows + 1)


def last_step(
    sea_rows,
    s,
    v,
    b,
    lam,
    mu,
    b_near,
    from_a,
    from_b,
    v_out,
    s_out,
    v_rows,
    b_rows,
    halo_s,
    halo_v,
    made,
    sems,
):
    odd, sec, _ = place()
    cx, cy, nz = b.shape
    weights = depth_weights(nz)
    rows = cy + 2 * LAST_NEEDED
    here = slice(SIDE - LAST_NEEDED, SIDE - LAST_NEEDED + rows)
    index_s, index_v = halo_stress(cx), halo_velocity(cx)
    layers, edges = second_lists(cx)
    own = received(odd, layers, [cy] * LAYERS, from_a, from_b, cx, 0)
    counts = [LAST_NEEDED] * len(edges[0])
    rest = received(odd, edges, counts, from_a, from_b, cx, LAYERS * cy + sea_rows + 1)
    for key, k in index_s.items():
        put_layer(halo_s, k, own["s", *key](), rest["s", *key](), sec)
    for x in range(cx):
        part = slice(4 * cy + x * SIDE, 4 * cy + (x + 1) * SIDE)
        b_rows[...] = with_strip(b[x], b_near[part, :], sec)
        scale = DT * b_rows[here, :]
        for c in range(3):
            terms = halo_share(c, x, cx, lambda k, j: halo_s[index_s[k, j], here, :])
            new = v[c, x, here, :]
            v_rows[c, x, here, :] = new if terms is None else new + scale * terms
    copies = [pltpu.make_async_copy(v_rows.at[:, :, pl.ds(SIDE, cy), :], v_out, sems.at[cx])]
    copies[0].start()
    for (c, i), k in index_v.items():
        at = (i + 2 if i < 0 else i - cx + 2) * cy
        scale = DT * b_near[at : at + cy, :]
        halo_v[k] = own["v", c, i]() + scale * own_share(s, c, i, EDGE, cy)
    for x in range(cx):
        parts = strains(v_rows, lambda c, j: halo_v[index_v[c, j]], x, SIDE, cy, weights)
        for c, change in enumerate(stress_change(lam[x], mu[x], parts)):
            made[c, x] = s[c, x, EDGE : EDGE + cy, :] + change
        copies.append(pltpu.make_async_copy(made.at[:, x], s_out.at[:, x], sems.at[x]))
        copies[-1].start()
    return copies


def floor_line(left, right):
    rows = left.shape[0]
    row = lax.broadcasted_iota(jnp.int32, (rows, 2 * rows), 0)
    lane = lax.broadcasted_iota(jnp.int32, (rows, 2 * rows), 1)
    picked = jnp.where(lane == row, left[:, 0:1], 0.0)
    picked = jnp.where(lane == row + rows, right[:, 0:1], picked)
    return jnp.sum(picked, axis=0, keepdims=True)


def floor_parts(s, v, b, b_near, parts, v_part, b_rows):
    cx, cy, nz = b.shape
    weights = depth_weights(nz)
    _, sec, _ = place()
    own = slice(EDGE, EDGE + cy)
    first, rows = EDGE - LAST_NEEDED, cy + 2 * LAST_NEEDED
    here = slice(SIDE - LAST_NEEDED, SIDE - LAST_NEEDED + rows)
    for x in range(cx):
        part = slice(4 * cy + x * SIDE, 4 * cy + (x + 1) * SIDE)
        b_rows[...] = with_strip(b[x], b_near[part, :], sec)
        scale = DT * b_rows[here, :]
        for c in range(3):
            terms = force(s, c, x, first, rows, weights)
            v_part[c, x, here, :] = v[c, x, first : first + rows, :] + scale * terms
    layers = [v_part[2, x, SIDE : SIDE + cy, :] for x in range(cx)]
    lines = [floor_line(layers[x], layers[x + 1]) for x in range(0, cx, 2)]
    below, first_above, second_above = (
        DT * b_near[k * cy : (k + 1) * cy, :] for k in (1, 2, 3)
    )
    last, before, start = s[4, cx - 1, own, :], s[4, cx - 2, own, :], s[4, 0, own, :]
    reached = first_above * (FAR * before - NEAR * last)
    lines.append(floor_line(reached, second_above * (FAR * last)))
    lines.append(floor_line(jnp.zeros((cy, nz), F32), below * (-FAR * start)))
    row = lax.broadcasted_iota(jnp.int32, (SIDE, 2 * cy), 0)
    tiled = jnp.zeros((SIDE, 2 * cy), F32)
    for j in range(SIDE):
        tiled = jnp.where(row == j, lines[j % LINES], tiled)
    for at in range(0, parts.shape[0], SIDE):
        parts[at : at + SIDE, :] = tiled


def column(line, first, count):
    wide = jnp.broadcast_to(line, (count, line.shape[1]))
    row = lax.broadcasted_iota(jnp.int32, wide.shape, 0)
    lane = lax.broadcasted_iota(jnp.int32, wide.shape, 1)
    return jnp.sum(jnp.where(lane == row + first, wide, 0.0), axis=1, keepdims=True)


def ocean_steps(
    start, from_a, from_b, near, state, depth, wet_ref, info, patches, ocean_out, ocean_ref, send_out, told_ref
):
    odd, sec, tile = place()
    count = lax.axis_size("tile")
    rows, own = depth.shape
    columns = own + 128
    at = start
    for k in range(columns // 128):
        lanes = slice(k * 128, (k + 1) * 128)
        for f, n in enumerate(DEEP if k < own // 128 else CORNER):
            here = ocean_field(state, depth, wet_ref, near, f, k)
            a, b = from_a[at : at + n, :], from_b[at : at + n, :]
            low, high = jnp.where(odd, a, b), jnp.where(odd, b, a)
            ocean_ref[f, 0:SIDE, lanes] = jnp.zeros((SIDE, 128), F32)
            ocean_ref[f, SIDE + rows :, lanes] = jnp.zeros((SIDE, 128), F32)
            ocean_ref[f, SIDE - n : SIDE, lanes] = low
            ocean_ref[f, SIDE : SIDE + rows, lanes] = here
            ocean_ref[f, SIDE + rows : SIDE + rows + n, lanes] = high
            at += n

    total = rows + 2 * SIDE
    lane = lax.broadcasted_iota(jnp.int32, (1, columns), 1)
    ahead = jnp.where((lane == own - 1) & (sec == 1), 0.0, 0.5).astype(F32)
    behind = jnp.where((lane == 0) & (sec == 0), 0.0, 0.5).astype(F32)
    line = lax.broadcasted_iota(jnp.int32, (total, 1), 0)
    inside = ((line >= SIDE) | (tile > 0)) & ((line < SIDE + rows) | (tile < count - 1))
    inside = inside.astype(F32)

    def across(f):
        return pltpu.roll(f, columns - 1, 1) * ahead - pltpu.roll(f, 1, 1) * behind

    def down(f):
        return 0.5 * (pltpu.roll(f, total - 1, 0) - pltpu.roll(f, 1, 0))

    eta, u, v_sea = ocean_ref[0], ocean_ref[1], ocean_ref[2]
    depth = ocean_ref[3]
    wet = (depth > 0.0).astype(F32)
    window = min(WINDOW, count)
    base = jnp.clip(tile - REACH - 1, 0, count - window)

    told_ref[0 : patches.shape[0], :] = patches[...]
    told_ref[patches.shape[0] :, :] = jnp.zeros((8, 128), F32)

    def told(half, k):
        return told_ref[pl.ds((half * count + k) * LINES, LINES), :]

    a, b = from_a[at : at + 1, :], from_b[at : at + 1, :]
    below, above = jnp.where(odd, a, b), jnp.where(odd, b, a)
    line = info[...]
    marks = [
        jnp.concatenate(
            [
                column(below, k * rows + rows - SIDE, SIDE),
                column(line, k * rows, rows),
                column(above, k * rows, SIDE),
            ],
            axis=0,
        )
        for k in range(2)
    ]
    owner = jnp.broadcast_to(marks[0] - base.astype(F32), (total, 128))
    share = marks[1]
    uplift = []
    for half in (sec, 1 - sec):
        tiles = []
        for k in range(-1, window + 1):
            here = jnp.clip(base + k, 0, count - 1)
            there = (here == base + k).astype(F32)
            tiles.append(told(half, here) * there)
        levels = [jnp.zeros((total, 128), F32) for _ in range(2)]
        for k in range(window):
            below, this, above = tiles[k], tiles[k + 1], tiles[k + 2]
            first, second = this[0:1] + below[2:3], this[1:2] + above[3:4]
            mine = owner == float(k)
            levels = [jnp.where(mine, q, level) for q, level in zip((first, second), levels)]
        uplift.append(levels)
    uplift = uplift[0] + [jnp.where(sec == 0, uplift[1][0], uplift[1][1])]
    uplift = jnp.concatenate(uplift, axis=1)
    lift = ODT * (share * wet * uplift)
    part = slice(SIDE, SIDE + rows)
    for step in range(2):
        u = wet * (u - ODT * down(eta))
        v_sea = wet * (v_sea - ODT * across(eta))
        if step == 1:
            ocean_out[1] = u[part, :own]
            ocean_out[2] = v_sea[part, :own]
            send_out(slice(1, 3))
        eta = inside * (eta - ODT * (down(depth * u) + across(depth * v_sea)) + lift)
    ocean_out[0] = eta[part, :own]
    send_out(slice(0, 1))


def finish(
    sea_rows,
    s,
    v,
    b,
    lam,
    mu,
    b_near,
    from_a,
    from_b,
    near,
    state,
    depth,
    wet,
    info,
    patches,
    v_out,
    s_out,
    ocean_out,
    v_rows,
    b_rows,
    halo_s,
    halo_v,
    made,
    ocean_ref,
    ocean_made,
    told_ref,
    sems,
    ocean_sems,
):
    cx, cy, _ = b.shape
    copies = last_step(
        sea_rows,
        s,
        v,
        b,
        lam,
        mu,
        b_near,
        from_a,
        from_b,
        v_out,
        s_out,
        v_rows,
        b_rows,
        halo_s,
        halo_v,
        made,
        sems,
    )

    def send_out(part):
        size = part.stop - part.start
        here = (pl.ds(part.start, size),)
        copies.append(
            pltpu.make_async_copy(
                ocean_made.at[here], ocean_out.at[here], ocean_sems.at[part.start]
            )
        )
        copies[-1].start()

    ocean_steps(
        LAYERS * cy,
        from_a,
        from_b,
        near,
        state,
        depth,
        wet,
        info,
        patches,
        ocean_made,
        ocean_ref,
        send_out,
        told_ref,
    )
    for copy in copies:
        copy.wait()


VMEM = pl.BlockSpec(memory_space=pltpu.VMEM)
ANY = pl.BlockSpec(memory_space=pl.ANY)


def call(body, name, outs, scratch, operands, weight=1, ins=VMEM, where=VMEM, grant=8):
    shapes = [jax.ShapeDtypeStruct(o, F32) for o in outs]
    moved = sum(o.size for o in operands) * 4 + sum(o.size for o in shapes) * 4
    return pl.pallas_call(
        body,
        name=name,
        out_shape=shapes,
        in_specs=ins if isinstance(ins, list) else [ins] * len(operands),
        out_specs=where if isinstance(where, list) else [where] * len(outs),
        scratch_shapes=scratch,
        compiler_params=pltpu.CompilerParams(vmem_limit_bytes=int(grant * 1024 * 1024)),
        cost_estimate=pl.CostEstimate(
            flops=moved * weight, bytes_accessed=moved * weight, transcendentals=0
        ),
    )(*operands)


def exchange(pay_a, pay_b, count):
    def swap(pay, first):
        pairs = []
        for i in range(first, count - 1, 2):
            pairs += [(i, i + 1), (i + 1, i)]
        return lax.ppermute(pay, "tile", pairs)

    from_a = swap(pay_a, 0)
    return from_a, swap(pay_b, 1)


def across(pay):
    return lax.ppermute(pay, "sec", [(0, 1), (1, 0)])


def shards(
    velocity,
    stresses,
    buoyancy,
    lame_first,
    shear_mod,
    ocean_state,
    depth_map,
    wet_mask,
    intersection_src,
    intersection_share,
):
    count = lax.axis_size("tile")
    sec = lax.axis_index("sec")
    _, cx, cy, nz = stresses.shape
    _, rows, columns = ocean_state.shape
    tall = cy + 2 * SIDE
    halo = pltpu.VMEM((LAYERS, tall, nz), F32)

    first = ((LAYERS + 2) // 2 + 1) * cy
    pay_a, pay_b, edges = call(
        opening,
        "opening",
        [(first, nz), (first, nz), (10, cx, SIDE, nz)],
        [pltpu.SemaphoreType.DMA((10 + 2 * (first // cy),))],
        [stresses, velocity, buoyancy],
        ins=ANY,
        grant=60,
    )
    strips = across(edges.reshape(10 * cx * SIDE, nz))
    early_a, early_b = exchange(pay_a, pay_b, count)
    early_list, late_list = first_lists(cx)
    per = columns // 128 * sum(DEEP) + sum(CORNER)
    late = len(late_list[0]) * cy + rounded(sum(thin_counts(early_list) + thin_counts(late_list)))
    pay_a, pay_b, stresses, velocity = call(
        first_round,
        "first_round",
        [(late, nz), (late, nz), (6, cx, tall + 2 * SIDE, nz), (3, cx, tall, nz)],
        [],
        [stresses, velocity, buoyancy, strips],
    )
    late_a, late_b = exchange(pay_a, pay_b, count)

    source, share, lame, shear, _ = lax.optimization_barrier(
        (intersection_src, intersection_share, lame_first, shear_mod, early_b)
    )
    ocean_state, depth_map, wet_mask, _ = lax.optimization_barrier(
        (ocean_state, depth_map, wet_mask, early_a)
    )
    (edges,) = call(edge_rows, "edge_rows", [(2 * cx * SIDE, nz)], [], [lame, shear])
    more_strips = across(edges)
    sea = [ocean_state, depth_map, wet_mask]
    (near,) = call(near_columns, "near_columns", [(len(DEEP) * rows, 128)], [], sea)
    near = across(near)
    (edges,) = call(ocean_edges, "ocean_edges", [(2, rounded(per) + 8, 128)], [], sea + [near])
    info = jnp.concatenate([source.astype(F32), share])[None]

    kept = cy + 2 * EDGE + 8
    second = (LAYERS * cy + rounded(per + 1 + 5 * LAST_NEEDED), nz)
    velocity, stresses, pay_a, pay_b, b_near = call(
        functools.partial(whole_step, per),
        "whole_step",
        [(3, cx, kept, nz), (6, cx, kept, nz), second, second]
        + [(4 * cy + cx * SIDE, nz)],
        [
            pltpu.VMEM((3, cx, tall + 2 * SIDE, nz), F32),
            halo,
            halo,
            pltpu.VMEM((4, tall, nz), F32),
            pltpu.VMEM((2, tall, nz), F32),
        ],
        [stresses, velocity, buoyancy, lame_first, shear_mod, strips, more_strips]
        + [early_a, early_b, late_a, late_b, edges, info],
    )
    from_a, from_b = exchange(pay_a, pay_b, count)
    parts, velocity = call(
        floor_parts,
        "floor_parts",
        [(2 * count * LINES, 2 * cy), (3, cx, tall, nz)],
        [pltpu.VMEM((tall, nz), F32)],
        [stresses, velocity, buoyancy, b_near],
    )
    parts = parts.reshape(2 * count * LINES // 2, 2, 2 * cy)
    patches = lax.all_to_all(parts, ("sec", "tile"), 0, 0, tiled=True).reshape(-1, 2 * cy)
    velocity, stresses, ocean_state = call(
        functools.partial(finish, per),
        "finish",
        [(3, cx, cy, nz), (6, cx, cy, nz), ocean_state.shape],
        [
            pltpu.VMEM((3, cx, tall, nz), F32),
            pltpu.VMEM((tall, nz), F32),
            halo,
            pltpu.VMEM((LAYERS, cy, nz), F32),
            pltpu.VMEM((6, cx, cy, nz), F32),
            pltpu.VMEM((len(DEEP), rows + 2 * SIDE, columns + 128), F32),
            pltpu.VMEM(ocean_state.shape, F32),
            pltpu.VMEM((2 * count * LINES + 8, 128), F32),
            pltpu.SemaphoreType.DMA((cx + 1,)),
            pltpu.SemaphoreType.DMA((2,)),
        ],
        [stresses, velocity, buoyancy, lame_first, shear_mod, b_near]
        + [from_a, from_b, near] + sea + [info, patches],
        where=ANY,
        grant=16,
    )
    return velocity, stresses, ocean_state


def solution(mesh):
    cube = P("tile", "sec", None)
    return jax.shard_map(
        shards,
        mesh=mesh,
        in_specs=(
            P(None, "tile", "sec", None),
            P(None, "tile", "sec", None),
            cube,
            cube,
            cube,
            P(None, "tile", "sec"),
            P("tile", "sec"),
            P("tile", "sec"),
            P("tile"),
            P("tile"),
        ),
        out_specs=(
            P(None, "tile", "sec", None),
            P(None, "tile", "sec", None),
            P(None, "tile", "sec"),
        ),
        check_vma=False,
    )
```
